32 devices in a mesh: batch: 8 (over y, x, core), seq: 4 (over z).
Axes of the slice: x: 2, y: 2, z: 4, core: 2. Of those that a mesh axis runs over, the one named last changes fastest.
Arguments:
- inputs: bfloat16 [32, 2048, 768], P('batch', 'seq'), may hold values from -6 to 6
- cotangent: bfloat16 [32, 2048, 768], P('batch', 'seq'), may hold values from -12 to 12
- set_kind: int32 [32], P('batch'), may hold values from 0 to 1, as said below
- row_offset: int32 [32, 4], P('batch'), may hold values from 0 to 1536, as said below
- query_w: bfloat16 [768, 768], replicated, may hold values from -0.21875 to 0.21875
- key_w: bfloat16 [768, 768], replicated, may hold values from -0.21875 to 0.21875
- value_w: bfloat16 [768, 768], replicated, may hold values from -0.21875 to 0.21875
- output_w: bfloat16 [768, 768], replicated, may hold values from -0.875 to 0.875
- up_w: bfloat16 [768, 3072], replicated, may hold values from -0.21875 to 0.21875
- down_w: bfloat16 [3072, 768], replicated, may hold values from -0.109375 to 0.109375
- compress: bfloat16 [2048, 256], replicated, may hold values from -0.1875 to 0.1875
- first_gain: float32 [768], replicated, may hold values from 0.1 to 1.9
- first_bias: float32 [768], replicated, may hold values from -3 to 3
- second_gain: float32 [768], replicated, may hold values from 0.1 to 1.9
- second_bias: float32 [768], replicated, may hold values from -3 to 3
Outputs:
- layer_out: bfloat16 [32, 2048, 768], P('batch', 'seq')
- input_grad: float32 [32, 2048, 768], P('batch', 'seq')
- query_grad: float32 [768, 768], P('batch', 'seq')
- key_grad: float32 [768, 768], P('batch', 'seq')
- value_grad: float32 [768, 768], P('batch', 'seq')
- output_grad: float32 [768, 768], P('batch', 'seq')
- up_grad: float32 [768, 3072], P('batch', 'seq')
- down_grad: float32 [3072, 768], P('batch', 'seq')
- compress_grad: float32 [2048, 256], replicated
- first_gain_grad: float32 [768], replicated
- first_bias_grad: float32 [768], replicated
- second_gain_grad: float32 [768], replicated
- second_bias_grad: float32 [768], replicated
The draws below stay inside these ranges and needn't reach their ends.
Inputs may be any that keep to these rules, and one draw needn't show every extreme that they name: `set_kind`: the 4 consecutive sets of each batch index include at least one set that is a single sequence. `row_offset`: entries of a set that is a single sequence are not read.
All inputs are finite; a program needn't handle non-finite values.
Results may differ from the reference program's by a relative error of at most 0.028.
Values may be sent and summed in bfloat16 or wider, within the bound.
A program may use at most 256 MiB of HBM per device.

```python
import math
import jax
import jax.numpy as jnp
from jax import lax

D = 768
H = 12
DH = 64
FF = 3072
COMP = 256
LONG = 2048
SETS = 4
SHORT = 512
GROUPS = 32
N_SEQ = 4


def draw_cotangent(key, part):
    key = jax.random.fold_in(key, 11)
    key_one, key_two = jax.random.split(key)
    along_rows = jnp.arange(LONG, dtype=jnp.float32) / max(LONG - 1, 1)
    along_sets = jnp.arange(GROUPS, dtype=jnp.float32) / max(GROUPS - 1, 1)
    base_draw = jax.random.truncated_normal(key_one, -4.0, 4.0, (GROUPS, LONG, D), jnp.float32)
    growth = math.log(3.0)
    ramp = jnp.exp(growth * (along_sets[:, None] - 0.5) + growth * (along_rows[None, :] - 0.5))
    rough = jnp.exp(jax.random.uniform(key_two, (GROUPS, LONG), jnp.float32, -0.35, 0.35))
    return jnp.clip(base_draw * (ramp * rough)[:, :, None], -12.0, 12.0).astype(jnp.bfloat16)


def draw_set_kind(key, part):
    key = jax.random.fold_in(key, 5)
    key_one, key_two = jax.random.split(key)
    kind_draw = jax.random.randint(key_one, (GROUPS // SETS, SETS), 0, 2)
    forced = jax.random.randint(key_two, (GROUPS // SETS, 1), 0, SETS)
    places = jnp.arange(SETS)[None, :]
    kind_draw = jnp.where(places == forced, 1, kind_draw)
    group_zero = jnp.arange(GROUPS // SETS)[:, None] == 0
    neighbour = (forced + 1) % SETS
    kind_draw = jnp.where(group_zero & (places == neighbour), 0, kind_draw)
    return kind_draw.reshape(GROUPS).astype(jnp.int32)


def draw_row_offset(key, part):
    key = jax.random.fold_in(key, 7)
    offsets = jax.random.randint(key, (GROUPS, 4), 0, LONG - SHORT + 1)
    corner = jnp.arange(GROUPS * 4).reshape(GROUPS, 4)
    offsets = jnp.where(corner == 0, LONG - SHORT, offsets)
    offsets = jnp.where(corner == 1, 0, offsets)
    return offsets.astype(jnp.int32)


def shard_levels(stream_key, dims, cuts, smallest, largest):
    level = 1.0
    for axis_at, blocks in cuts:
        heights = jax.random.uniform(jax.random.fold_in(jax.random.fold_in(stream_key, 6), axis_at), (blocks,), jnp.float32, smallest / len(cuts), largest / len(cuts))
        level = level * jnp.repeat(jnp.exp(heights), dims[axis_at] // blocks).reshape((-1,) + (1,) * (len(dims) - 1 - axis_at))
    return level


def normal_values(stream_key, dims, scale, most, shards=(), kind=jnp.bfloat16):
    level = shard_levels(stream_key, dims, shards, -0.22, 0.18) if shards else 1.0
    entries = jax.random.normal(stream_key, dims, jnp.float32) * scale * level
    return jnp.minimum(jnp.maximum(entries, -most), most).astype(kind)


def setup_inputs(seed: int = 0) -> dict:
    splits = jax.random.split(jax.random.key(seed), 16)
    inputs = normal_values(splits[0], (GROUPS, LONG, D), 1.0, 6.0, ((0, 8), (1, 4)))
    cotangent = draw_cotangent(jax.random.fold_in(splits[15], 71), 0)
    set_kind = draw_set_kind(jax.random.fold_in(splits[15], 71), 0)
    row_offset = draw_row_offset(jax.random.fold_in(splits[15], 71), 0)
    query_w = normal_values(splits[4], (D, D), D ** -0.5, 0.21875)
    key_w = normal_values(splits[5], (D, D), D ** -0.5, 0.21875)
    value_w = normal_values(splits[6], (D, D), D ** -0.5, 0.21875)
    output_w = normal_values(splits[7], (D, D), (D // 16) ** -0.5, 0.875)
    up_w = normal_values(splits[8], (D, FF), D ** -0.5, 0.21875)
    down_w = normal_values(splits[9], (FF, D), FF ** -0.5, 0.109375)
    compress = normal_values(splits[10], (LONG, COMP), (LONG // 2) ** -0.5, 0.1875)
    first_gain = jnp.clip(1.0 + 0.18 * jax.random.normal(splits[11], (D,), jnp.float32), 0.1, 1.9)
    first_bias = normal_values(splits[12], (D,), 0.5, 3.0, (), jnp.float32)
    second_gain = jnp.clip(1.0 + 0.18 * jax.random.normal(splits[13], (D,), jnp.float32), 0.1, 1.9)
    second_bias = normal_values(splits[14], (D,), 0.5, 3.0, (), jnp.float32)
    return {"inputs": inputs, "cotangent": cotangent, "set_kind": set_kind, "row_offset": row_offset, "query_w": query_w, "key_w": key_w, "value_w": value_w, "output_w": output_w, "up_w": up_w, "down_w": down_w, "compress": compress, "first_gain": first_gain, "first_bias": first_bias, "second_gain": second_gain, "second_bias": second_bias}


highest = lax.Precision.HIGHEST

@jax.custom_vjp
def low(v):
    return lax.optimization_barrier(v.astype(jnp.bfloat16)).astype(jnp.float32)

@jax.custom_vjp
def low_back(v):
    return v

def low_keep(v):
    return (low(v), None)

def low_pass(kept, grad):
    return (grad,)

def back_keep(v):
    return (v, None)

def back_low(kept, grad):
    return (low(grad),)
low.defvjp(low_keep, low_pass)
low_back.defvjp(back_keep, back_low)

def both_ways(values_in):
    return low_back(low(values_in))

def matmul(left_in, right_in):
    return jnp.dot(left_in, right_in, precision=highest)

def layer_norm(values_in, gain_in, bias_in):
    average = lax.optimization_barrier(jnp.mean(values_in, axis=-1, keepdims=True))
    centered = values_in - average
    variance = lax.optimization_barrier(jnp.mean(centered * centered, axis=-1, keepdims=True))
    return centered * lax.rsqrt(variance + 1e-05) * gain_in + bias_in

def set_forward(params, block_in, kind_one, offsets_one):
    query_w, key_w, value_w, output_w, up_w, down_w, compress, first_gain, first_bias, second_gain, second_bias = params
    queries = both_ways(matmul(block_in, query_w))
    keys = both_ways(matmul(block_in, key_w))
    values = both_ways(matmul(block_in, value_w))
    positions = jnp.arange(LONG, dtype=jnp.int32)
    member = (positions // SHORT).astype(jnp.int32)
    short_rows = offsets_one[member] + positions % SHORT
    table_row = jnp.where(kind_one > 0, positions, short_rows).astype(jnp.int32)
    table = compress[table_row]
    packed = jnp.concatenate([keys, values], axis=1)
    table_blocks = table.reshape(N_SEQ, LONG // N_SEQ, COMP)
    packed_blocks = packed.reshape(N_SEQ, LONG // N_SEQ, 2 * D)
    partial_value = low(jnp.einsum('nrk,nrd->nkd', table_blocks, packed_blocks, precision=highest))
    block_member = jnp.arange(N_SEQ, dtype=jnp.int32) * (LONG // N_SEQ) // SHORT
    selector = (block_member[:, None] == jnp.arange(4, dtype=jnp.int32)[None, :]).astype(partial_value.dtype)
    short_sums = both_ways(jnp.einsum('nm,nkd->mkd', selector, partial_value, precision=highest))
    long_sum = both_ways(lax.optimization_barrier(jnp.sum(partial_value, axis=0)))
    summary = jnp.where(kind_one > 0, long_sum[None], short_sums)
    keys_c = summary[:, :, :D].reshape(4, COMP, H, DH)
    values_c = summary[:, :, D:].reshape(4, COMP, H, DH)
    query_blocks = queries.reshape(4, SHORT, H, DH)
    scores = low_back(jnp.einsum('mshd,mkhd->mhsk', query_blocks, keys_c, precision=highest) * DH ** (-0.5))
    weights = low(jax.nn.softmax(scores, axis=-1))
    mixed = both_ways(jnp.einsum('mhsk,mkhd->mshd', weights, values_c, precision=highest).reshape(LONG, D))
    attended = low_back(matmul(mixed, output_w))
    hidden = layer_norm(block_in + attended, first_gain, first_bias)
    upward = low_back(matmul(low(hidden), up_w))
    activated = low(jax.nn.gelu(upward, approximate=False))
    downward = low_back(matmul(activated, down_w))
    return layer_norm(hidden + downward, second_gain, second_bias)

def reference(inputs, cotangent, set_kind, row_offset, query_w, key_w, value_w, output_w, up_w, down_w, compress, first_gain, first_bias, second_gain, second_bias):
    params = tuple((weight.astype(jnp.float32) for weight in (query_w, key_w, value_w, output_w, up_w, down_w, compress, first_gain, first_bias, second_gain, second_bias)))

    def one_set(totals, items):
        block_in, block_cot, kind_one, offsets_one = items

        def forward(param_set, values_in):
            return set_forward(param_set, values_in, kind_one, offsets_one)
        outputs, pullback = jax.vjp(forward, params, block_in.astype(jnp.float32))
        grads, grad_in = pullback(block_cot.astype(jnp.float32))
        totals = jax.tree.map(jnp.add, totals, grads)
        return (totals, (outputs.astype(jnp.bfloat16), grad_in))
    zeros_init = jax.tree.map(jnp.zeros_like, params)
    totals, (layer_out, input_grad) = lax.scan(one_set, zeros_init, (inputs, cotangent, set_kind, row_offset))
    return (layer_out, input_grad, totals[0], totals[1], totals[2], totals[3], totals[4], totals[5], totals[6], totals[7], totals[8], totals[9], totals[10])
```

```python
import functools

import jax
import jax.numpy as jnp
from jax import lax
from jax.experimental import pallas as pl
from jax.experimental.pallas import tpu as pltpu
from jax.sharding import PartitionSpec as P

DH = 64
LANES = 128
TILE = 8
SCALE = DH ** (-0.5)
EPS = 1e-05
MESH = pl.DeviceIdType.MESH
VMEM_LIMIT = 63 * 1024 * 1024
bf16 = jnp.bfloat16
f32 = jnp.float32


def dot(left, right):
    return lax.dot_general(left, right, (((1,), (0,)), ((), ())), preferred_element_type=f32)


def dot_nt(left, right):
    return lax.dot_general(left, right, (((1,), (1,)), ((), ())), preferred_element_type=f32)


def dot_tn(left, right):
    return lax.dot_general(left, right, (((0,), (0,)), ((), ())), preferred_element_type=f32)


def params(**more):
    return pltpu.CompilerParams(vmem_limit_bytes=VMEM_LIMIT, **more)


def whole(shape):
    return pl.BlockSpec(shape, lambda *_: (0,) * len(shape), pipeline_mode=pl.Buffered(1))


def per_set(shape):
    return pl.BlockSpec((1,) + tuple(shape), lambda s, *_: (s,) + (0,) * len(shape))


def aligned(start):
    begin = start // TILE * TILE
    return pl.multiple_of(begin, TILE), start - begin


def place():
    batch = lax.axis_index("batch")
    return batch // 4, batch // 2 % 2, batch % 2, lax.axis_index("seq")


def device(y, x, core, z):
    return ((y * 2 + x) * 2 + core, z)


def greet(others):
    barrier = pltpu.get_barrier_semaphore()
    for other in others:
        pl.semaphore_signal(barrier, inc=1, device_id=other, device_id_type=MESH)
    pl.semaphore_wait(barrier, len(others))


def remote(src, dst, send_sem, recv_sem, target):
    return pltpu.make_async_remote_copy(src, dst, send_sem, recv_sem, device_id=target, device_id_type=MESH)


class LineSum:
    lag = 2

    def __init__(self, line, own, from_left, from_right, to_right, to_left, sems):
        y, x, core, self.z = place()
        self.line = line
        self.own = own
        right, left = device(y, x, core, (self.z + 1) % line), device(y, x, core, (self.z + line - 1) % line)
        self.ways = (
            (from_left, to_right, right, self.z > 0, self.z < line - 1, sems[0], sems[1]),
            (from_right, to_left, left, self.z < line - 1, self.z > 0, sems[2], sems[3]),
        )

    def prepare(self):
        for arrived, _, _, has_before, _, _, _ in self.ways:

            @pl.when(jnp.logical_not(has_before))
            def _():
                arrived[...] = jnp.zeros_like(arrived)

    def copy(self, way, at):
        arrived, leaving, target, _, _, send, recv = way
        return remote(leaving.at[at], arrived.at[at], send.at[at], recv.at[at], target)

    def forward(self, way, at):
        arrived, leaving, _, has_before, has_after, _, _ = way

        @pl.when(has_before)
        def _():
            self.copy(way, at).wait_recv()

        leaving[at] = arrived[at] + self.own[at]

        @pl.when(has_after)
        def _():
            self.copy(way, at).start()

    def slots(self):
        return self.own.shape[0] + self.lag * (self.line - 1)

    def serve(self, slot):
        for way, hops in zip(self.ways, (self.z, self.line - 1 - self.z)):
            at = slot - self.lag * hops

            @pl.when(jnp.logical_and(at >= 0, at < self.own.shape[0]))
            def _():
                self.forward(way, at)

    def total(self, at, joined):
        left, right = self.ways[0][0][at].astype(f32), self.ways[1][0][at].astype(f32)
        return (self.own[at].astype(f32) + jnp.where(joined, left + right, 0.0)).astype(bf16)

    def finish(self, at):
        for way in self.ways:

            @pl.when(way[4])
            def _():
                self.copy(way, at).wait_send()


def line_sum_kernel(line, own_ref, long_ref, out_ref, from_left, from_right, to_right, to_left, *sems):
    y, x, core, z = place()
    barrier = pltpu.get_barrier_semaphore()
    for there, other in ((z > 0, z - 1), (z < line - 1, z + 1)):

        @pl.when(there)
        def _():
            pl.semaphore_signal(barrier, inc=1, device_id=device(y, x, core, other), device_id_type=MESH)

    both = jnp.logical_and(z > 0, z < line - 1).astype(jnp.int32)
    pl.semaphore_wait(barrier, 1 + both)
    sums = LineSum(line, own_ref, from_left, from_right, to_right, to_left, sems)
    sums.prepare()
    count = own_ref.shape[0]

    def slot(at, carry):
        sums.serve(at)
        return carry

    lax.fori_loop(0, sums.slots(), slot, 0)
    for at in range(count):
        out_ref[at] = sums.total(at, long_ref[at * long_ref.shape[0] // count] > 0)
        sums.finish(at)


def line_sum(part, set_kind, identity):
    sets, rows, width = part.shape
    pieces = 4
    split = part.reshape(sets * pieces, rows // pieces, width)
    line = lax.axis_size("seq")
    vmem = pl.BlockSpec(memory_space=pltpu.VMEM)
    out = pl.pallas_call(
        functools.partial(line_sum_kernel, line),
        in_specs=[vmem, pl.BlockSpec(memory_space=pltpu.SMEM)],
        out_specs=vmem,
        out_shape=jax.ShapeDtypeStruct(split.shape, bf16),
        scratch_shapes=[pltpu.VMEM(split.shape, bf16)] * 4 + [pltpu.SemaphoreType.DMA((sets * pieces,))] * 4,
        compiler_params=params(collective_id=identity, has_side_effects=True),
        name="line_sum",
    )(split, set_kind)
    return out.reshape(part.shape)


class Scatter:
    def __init__(self, x_first, part, from_core, from_first, from_second, send, recv):
        y, x, core, z = place()
        self.part, self.recvs = part, (from_core, from_first, from_second)
        along_x, along_y = device(y, 1 - x, core, z), device(1 - y, x, core, z)
        self.core, self.x, self.y, self.x_first = core, x, y, x_first
        if x_first:
            sources = (part.at[:, :, 1 - core], from_core.at[:, 1 - x], from_first.at[1 - y])
            targets = (device(y, x, 1 - core, z), along_x, along_y)
        else:
            sources = (part.at[:, :, 1 - core], from_core.at[1 - y], from_first.at[1 - x])
            targets = (device(y, x, 1 - core, z), along_y, along_x)
        self.copies = [
            remote(sources[i], self.recvs[i], send.at[i], recv.at[i], targets[i]) for i in range(3)
        ]

    def start(self):
        self.copies[0].start()

    def first(self):
        self.copies[0].wait_recv()
        self.recvs[0][...] = self.recvs[0][...] + self.part[:, :, self.core]
        self.copies[1].start()

    def second(self):
        self.copies[1].wait_recv()
        kept = self.recvs[0][:, self.x] if self.x_first else self.recvs[0][self.y]
        self.recvs[1][...] = self.recvs[1][...] + kept
        self.copies[2].start()

    def done(self):
        self.copies[2].wait_recv()
        kept = self.recvs[1][self.y] if self.x_first else self.recvs[1][self.x]
        return self.recvs[2][...].astype(f32) + kept.astype(f32)

    def finish(self):
        for copy in self.copies:
            copy.wait_send()


class LineScatter:
    def __init__(self, line, blocks, arrived, send, recv):
        y, x, core, self.z = place()
        self.blocks, self.arrived, self.line = blocks, arrived, line
        self.copies = []
        for d in range(1, line):
            to = (self.z + d) % line
            self.copies.append(
                remote(blocks.at[to], arrived.at[d - 1], send.at[d - 1], recv.at[d - 1], device(y, x, core, to))
            )

    def start(self):
        for copy in self.copies:
            copy.start()

    def done(self):
        total = self.blocks[self.z].astype(f32)
        for d, copy in enumerate(self.copies):
            copy.wait_recv()
            total = total + self.arrived[d].astype(f32)
        return total

    def finish(self):
        for copy in self.copies:
            copy.wait_send()


def line_scatter_blocks(blocks, rows, line):
    step = rows.shape[1] // line
    for z in range(line):
        mine = rows[:, z * step : (z + 1) * step]
        if step % LANES:
            top = rows.shape[0] // 2
            mine = jnp.concatenate([mine[:top], mine[top:]], axis=1)
        blocks[z] = mine.astype(bf16)


def scatter_kernel(line, query, key, value, output, up, down, query_out, key_out, value_out, output_out, up_out, down_out, *scratch):
    y, x, core, z = place()
    greet(
        [device(y, x, 1 - core, z), device(y, 1 - x, core, z), device(1 - y, x, core, z)]
        + [device(y, x, core, (z + d) % line) for d in range(1, line)]
    )
    scratch = list(scratch)
    take = lambda n: [scratch.pop(0) for _ in range(n)]
    jobs = []
    for i, (part, out) in enumerate(
        ((up, up_out), (down, down_out), (output, output_out), (query, query_out), (key, key_out), (value, value_out))
    ):
        job = Scatter(i % 2 == 0, part, *take(3), *take(2))
        jobs.append((job, LineScatter(line, *take(4)), out))
    for job, _, _ in jobs:
        job.start()
    for job, _, _ in jobs:
        job.first()
    for job, _, _ in jobs:
        job.second()
    for job, across, _ in jobs:
        line_scatter_blocks(across.blocks, job.done(), line)
        across.start()
    for job, across, out in jobs:
        total = across.done()
        if total.shape != out.shape:
            top, step = total.shape[0], total.shape[1] // 2
            out[:top, :] = total[:, :step]
            out[top:, :] = total[:, step:]
        else:
            out[...] = total
        job.finish()
        across.finish()


def scatter(query, key, value, output, up, down):
    line = lax.axis_size("seq")
    grads = (query, key, value, output, up, down)
    blocked = [v.reshape(2, 2, 2, v.shape[0] // 8, v.shape[1]) for v in grads]
    vmem = pl.BlockSpec(memory_space=pltpu.VMEM)
    scratch = []
    for v in (up, down, output, query, key, value):
        rows, width = v.shape[0] // 8, v.shape[1]
        step = width // line
        block = (rows, step) if step % LANES == 0 else (rows // 2, step * 2)
        scratch += [
            pltpu.VMEM((2, 2, rows, width), bf16),
            pltpu.VMEM((2, rows, width), bf16),
            pltpu.VMEM((rows, width), bf16),
            pltpu.SemaphoreType.DMA((3,)),
            pltpu.SemaphoreType.DMA((3,)),
            pltpu.VMEM((line,) + block, bf16),
            pltpu.VMEM((line - 1,) + block, bf16),
            pltpu.SemaphoreType.DMA((line - 1,)),
            pltpu.SemaphoreType.DMA((line - 1,)),
        ]
    return pl.pallas_call(
        functools.partial(scatter_kernel, line),
        in_specs=[vmem] * 6,
        out_specs=[vmem] * 6,
        out_shape=[jax.ShapeDtypeStruct((v.shape[0] // 8, v.shape[1] // line), f32) for v in grads],
        scratch_shapes=scratch,
        compiler_params=params(collective_id=2, has_side_effects=True),
        name="scatter",
    )(*blocked)


def total_kernel(line, table_ref, norms_ref, table_out, norms_out, mine, from_core, from_plane, from_line, gathered,
                 core_norms, plane_norms, line_norms, *sems):
    y, x, core, z = place()
    plane = y * 2 + x
    sems = list(sems)
    take = lambda: (sems.pop(0), sems.pop(0))
    other = device(y, x, 1 - core, z)
    places = [((y + dy) % 2, (x + dx) % 2) for dy, dx in ((0, 1), (1, 0), (1, 1))]
    planes = [(py * 2 + px, device(py, px, core, z)) for py, px in places]
    lines = [((z + d) % line, device(y, x, core, (z + d) % line)) for d in range(1, line)]
    greet([other] + [to for _, to in planes] + [to for _, to in lines])

    def run(copies):
        for copy in copies:
            copy.start()
        for copy in copies:
            copy.wait()

    rows = mine.shape[-2]
    mine[...] = table_ref[...].astype(bf16)
    core_norms[0] = norms_ref[...]
    s, r = take()
    run([
        remote(mine.at[1 - core], from_core, s.at[0], r.at[0], other),
        remote(core_norms.at[0], core_norms.at[1], s.at[1], r.at[1], other),
    ])
    from_core[...] = from_core[...] + mine[core]
    plane_norms[plane] = core_norms[0] + core_norms[1]
    s, r = take()
    run([remote(from_core.at[p], from_plane.at[i], s.at[i], r.at[i], to) for i, (p, to) in enumerate(planes)]
        + [remote(plane_norms.at[plane], plane_norms.at[plane], s.at[3 + i], r.at[3 + i], to) for i, (_, to) in enumerate(planes)])
    total = from_core[plane].astype(f32)
    for i in range(3):
        total = total + from_plane[i].astype(f32)
    mine[0, 0] = total.astype(bf16)
    line_norms[z] = plane_norms[0] + plane_norms[1] + plane_norms[2] + plane_norms[3]
    s, r = take()
    run([remote(mine.at[0, 0, p], from_line.at[i], s.at[i], r.at[i], to) for i, (p, to) in enumerate(lines)]
        + [remote(line_norms.at[z], line_norms.at[z], s.at[line - 1 + i], r.at[line - 1 + i], to) for i, (_, to) in enumerate(lines)])
    total = mine[0, 0, z].astype(f32)
    for i in range(line - 1):
        total = total + from_line[i].astype(f32)
    gathered[core, plane, z] = total.astype(bf16)
    all_norms = line_norms[0]
    for i in range(1, line):
        all_norms = all_norms + line_norms[i]
    norms_out[...] = all_norms
    s, r = take()
    block = gathered.at[core, plane, z]
    run([remote(block, block, s.at[i], r.at[i], to) for i, (_, to) in enumerate(lines)])
    s, r = take()
    block = gathered.at[core, plane]
    run([remote(block, block, s.at[i], r.at[i], to) for i, (_, to) in enumerate(planes)])
    s, r = take()
    block = gathered.at[core]
    run([remote(block, block, s.at[0], r.at[0], other)])
    table_out[...] = gathered[...].astype(f32)


def total_sum(table, norms):
    line = lax.axis_size("seq")
    longest, comp = table.shape
    rows = longest // (8 * line)
    shape = (2, 4, line, rows, comp)
    vmem = pl.BlockSpec(memory_space=pltpu.VMEM)
    counts = (2, 6, 2 * (line - 1), line - 1, 3, 1)
    out, sums = pl.pallas_call(
        functools.partial(total_kernel, line),
        in_specs=[vmem] * 2,
        out_specs=[vmem] * 2,
        out_shape=[jax.ShapeDtypeStruct(shape, f32), jax.ShapeDtypeStruct(norms.shape, f32)],
        scratch_shapes=[
            pltpu.VMEM(shape, bf16),
            pltpu.VMEM(shape[1:], bf16),
            pltpu.VMEM((3,) + shape[2:], bf16),
            pltpu.VMEM((line - 1,) + shape[3:], bf16),
            pltpu.VMEM(shape, bf16),
            pltpu.VMEM((2,) + norms.shape, f32),
            pltpu.VMEM((4,) + norms.shape, f32),
            pltpu.VMEM((line,) + norms.shape, f32),
        ]
        + [pltpu.SemaphoreType.DMA((n,)) for n in counts for _ in range(2)],
        compiler_params=params(collective_id=3, has_side_effects=True),
        name="total_sum",
    )(table.reshape(shape), norms)
    return out.reshape(longest, comp), sums


def front_kernel(start_ref, compress_ref, x_ref, wq_ref, table_ref, c_ref, q_ref, wide):
    step = pl.program_id(0)

    longest = compress_ref.shape[0]

    @pl.when(step == 0)
    def _():
        wide[:longest, :] = compress_ref[...].astype(f32)
        wide[longest:, :] = jnp.zeros((TILE, wide.shape[1]), f32)

    rows = x_ref.shape[1]
    begin, shift = aligned(start_ref[step])
    window = wide[pl.ds(begin, rows + TILE), :]
    table = pltpu.roll(window, lax.rem(rows + TILE - shift, rows + TILE), 0)[:rows].astype(bf16)
    table_ref[0] = table
    x = x_ref[0]
    c_ref[0] = dot_tn(table, x).astype(bf16)
    q_ref[0] = (dot(x, wq_ref[...]) * SCALE).astype(bf16)


def front(starts, compress, x, wq):
    sets, rows, width = x.shape
    longest, comp = compress.shape
    grid_spec = pltpu.PrefetchScalarGridSpec(
        num_scalar_prefetch=1,
        grid=(sets,),
        in_specs=[whole(compress.shape), per_set((rows, width)), whole(wq.shape)],
        out_specs=[per_set((rows, comp)), per_set((comp, width)), per_set((rows, width))],
        scratch_shapes=[pltpu.VMEM((longest + TILE, comp), f32)],
    )
    return pl.pallas_call(
        front_kernel,
        grid_spec=grid_spec,
        out_shape=[
            jax.ShapeDtypeStruct((sets, rows, comp), bf16),
            jax.ShapeDtypeStruct((sets, comp, width), bf16),
            jax.ShapeDtypeStruct((sets, rows, width), bf16),
        ],
        compiler_params=params(),
        name="front",
    )(starts, compress, x, wq)


def head_blocks(pair, first_half):
    zero = jnp.zeros_like(pair)
    return jnp.concatenate([jnp.where(first_half, pair, zero), jnp.where(first_half, zero, pair)], axis=0)


def norm_forward(v):
    average = jnp.mean(v, axis=-1, keepdims=True)
    centered = v - average
    variance = jnp.mean(centered * centered, axis=-1, keepdims=True)
    inverse = lax.rsqrt(variance + EPS)
    return centered * inverse, inverse


def norm_backward(dz, z, inverse):
    return (dz - jnp.mean(dz, axis=-1, keepdims=True) - z * jnp.mean(dz * z, axis=-1, keepdims=True)) * inverse


def middle_kernel(
    c_ref, x_ref, q_ref, cot_ref, wk_ref, wv_ref, wo_ref, up_ref, down_ref, norms_ref,
    kc_ref, vc_ref, e_ref, mixed_ref, hidden_ref, act_ref, out_ref, gdown_ref, gup_ref,
    gfirst_ref, gatt_ref, go_ref, sums_ref,
    dgelu, z_first, rinv_ref,
):
    step = pl.program_id(0)
    rows, width = x_ref.shape[1:]
    comp = c_ref.shape[1]
    units = up_ref.shape[1]
    chunk = 768
    c = c_ref[0]
    kc_ref[0] = dot(c, wk_ref[...]).astype(bf16)
    vc_ref[0] = dot(c, wv_ref[...]).astype(bf16)
    half = lax.broadcasted_iota(jnp.int32, (comp, LANES), 1) < DH
    ones = head_blocks(jnp.ones((comp, LANES), bf16), half)
    for pair in range(width // LANES):
        lanes = pl.ds(pair * LANES, LANES)
        keys = head_blocks(kc_ref[0, :, lanes], half)
        values = jnp.concatenate([head_blocks(vc_ref[0, :, lanes], half), ones], axis=1)
        scores = dot_nt(q_ref[0, :, lanes], keys)
        parts = []
        for head in range(2):
            mine = scores[:, head * comp : (head + 1) * comp]
            top = jnp.max(mine, axis=-1, keepdims=True)
            parts.append(jnp.exp(mine - top).astype(bf16))
        e = jnp.concatenate(parts, axis=1)
        e_ref[0, :, pl.ds(pair * 2 * comp, 2 * comp)] = e
        sums = dot(e, values)
        rinv = 1.0 / sums[:, LANES:]
        rinv_ref[:, lanes] = rinv
        mixed_ref[0, :, lanes] = (sums[:, :LANES] * rinv).astype(bf16)
    gain1, bias1, gain2, bias2 = (norms_ref[i : i + 1, :] for i in range(4))
    z1, inv1 = norm_forward(x_ref[0].astype(f32) + dot(mixed_ref[0], wo_ref[...]))
    z_first[...] = z1
    hidden = z1 * gain1 + bias1
    hidden_low = hidden.astype(bf16)
    hidden_ref[0] = hidden_low
    gfirst_ref[0] = hidden
    for at in range(0, units, chunk):
        span = pl.ds(at, chunk)
        upward = dot(hidden_low, up_ref[:, span])
        cdf = 0.5 + 0.5 * lax.erf(upward * (0.5**0.5))
        density = jnp.exp(upward * upward * -0.5) * 0.3989422804014327
        act_ref[0, :, span] = (upward * cdf).astype(bf16)
        dgelu[:, span] = (cdf + upward * density).astype(bf16)
    z2, inv2 = norm_forward(gfirst_ref[0] + dot(act_ref[0], down_ref[...]))
    out_ref[0] = (z2 * gain2 + bias2).astype(bf16)
    dy = cot_ref[0].astype(f32)
    gsecond = norm_backward(dy * gain2, z2, inv2)
    gain2_part = jnp.sum(dy * z2, axis=0, keepdims=True)
    bias2_part = jnp.sum(dy, axis=0, keepdims=True)
    gdown = gsecond.astype(bf16)
    gdown_ref[0] = gdown
    gfirst_ref[0] = gsecond
    for at in range(0, units, chunk):
        span = pl.ds(at, chunk)
        gact = dot_nt(gdown, down_ref[span, :])
        gup_ref[0, :, span] = (gact * dgelu[:, span].astype(f32)).astype(bf16)
    ghidden = gfirst_ref[0] + dot_nt(gup_ref[0], up_ref[...])
    z1 = z_first[...]
    gfirst = norm_backward(ghidden * gain1, z1, inv1)
    gain1_part = jnp.sum(ghidden * z1, axis=0, keepdims=True)
    bias1_part = jnp.sum(ghidden, axis=0, keepdims=True)
    gfirst_ref[0] = gfirst
    gatt = gfirst.astype(bf16)
    gatt_ref[0] = gatt
    go_ref[0] = (dot_nt(gatt, wo_ref[...]) * rinv_ref[...]).astype(bf16)

    @pl.when(step == 0)
    def _():
        sums_ref[...] = jnp.zeros_like(sums_ref)

    for i, part in enumerate((gain1_part, bias1_part, gain2_part, bias2_part)):
        sums_ref[i : i + 1, :] += part


def middle(c, x, q, cot, wk, wv, wo, up, down, norms):
    sets, rows, width = x.shape
    comp = c.shape[1]
    units = up.shape[1]
    pairs = width // LANES
    outs = [
        ((comp, width), bf16),
        ((comp, width), bf16),
        ((rows, pairs * 2 * comp), bf16),
        ((rows, width), bf16),
        ((rows, width), bf16),
        ((rows, units), bf16),
        ((rows, width), bf16),
        ((rows, width), bf16),
        ((rows, units), bf16),
        ((rows, width), f32),
        ((rows, width), bf16),
        ((rows, width), bf16),
    ]
    return pl.pallas_call(
        middle_kernel,
        grid=(sets,),
        in_specs=[per_set((comp, width))] + [per_set((rows, width))] * 3
        + [whole(w.shape) for w in (wk, wv, wo, up, down, norms)],
        out_specs=[per_set(shape) for shape, _ in outs] + [whole((8, width))],
        out_shape=[jax.ShapeDtypeStruct((sets,) + shape, kind) for shape, kind in outs]
        + [jax.ShapeDtypeStruct((8, width), f32)],
        scratch_shapes=[
            pltpu.VMEM((rows, units), bf16),
            pltpu.VMEM((rows, width), f32),
            pltpu.VMEM((rows, width), f32),
        ],
        compiler_params=params(),
        name="middle",
    )(c, x, q, cot, wk, wv, wo, up, down, norms)


def attention_back_kernel(
    e_ref, go_ref, mixed_ref, q_ref, kc_ref, vc_ref, gfirst_ref, wq_ref, wk_ref, wv_ref,
    gq_ref, gk_ref, gv_ref, g_ref, gin_ref,
    gkt, gvt,
):
    width = q_ref.shape[2]
    comp = kc_ref.shape[1]
    half = lax.broadcasted_iota(jnp.int32, (comp, LANES), 1) < DH
    minus = head_blocks(jnp.full((comp, LANES), -1.0, bf16), half)
    for pair in range(width // LANES):
        lanes = pl.ds(pair * LANES, LANES)
        e = e_ref[0, :, pl.ds(pair * 2 * comp, 2 * comp)]
        keys = head_blocks(kc_ref[0, :, lanes], half)
        values = jnp.concatenate([head_blocks(vc_ref[0, :, lanes], half), minus], axis=1)
        go = go_ref[0, :, lanes]
        delta = (go.astype(f32) * mixed_ref[0, :, lanes].astype(f32)).astype(bf16)
        gp = dot_nt(jnp.concatenate([go, delta], axis=1), values)
        gs = (gp * e.astype(f32)).astype(bf16)
        gq_ref[0, :, lanes] = (dot(gs, keys) * SCALE).astype(bf16)
        for into, left, right in ((gkt, q_ref[0, :, lanes], gs), (gvt, go, e)):
            both = dot_tn(left, right)
            at = pair * LANES
            into[at : at + DH, :] = both[:DH, :comp].astype(bf16)
            into[at + DH : at + LANES, :] = both[DH:, comp:].astype(bf16)
    g_ref[0] = (dot(wk_ref[...], gkt[...]) + dot(wv_ref[...], gvt[...])).astype(bf16)
    gk_ref[0] = gkt[...].T
    gv_ref[0] = gvt[...].T
    gin_ref[0] = gfirst_ref[0] + dot_nt(gq_ref[0], wq_ref[...])


def attention_back(e, go, mixed, q, kc, vc, gfirst, wq, wk, wv):
    sets, rows, width = q.shape
    comp = kc.shape[1]
    outs = [
        ((rows, width), bf16),
        ((comp, width), bf16),
        ((comp, width), bf16),
        ((width, comp), bf16),
        ((rows, width), f32),
    ]
    tokens = per_set((rows, width))
    short = per_set((comp, width))
    return pl.pallas_call(
        attention_back_kernel,
        grid=(sets,),
        in_specs=[per_set(e.shape[1:])] + [tokens] * 3 + [short] * 2 + [tokens]
        + [whole(w.shape) for w in (wq, wk, wv)],
        out_specs=[per_set(shape) for shape, _ in outs],
        out_shape=[jax.ShapeDtypeStruct((sets,) + shape, kind) for shape, kind in outs],
        scratch_shapes=[pltpu.VMEM((width, comp), bf16)] * 2,
        compiler_params=params(),
        name="attention_back",
    )(e, go, mixed, q, kc, vc, gfirst, wq, wk, wv)


def feed_grads_kernel(hidden_ref, gup_ref, act_ref, gdown_ref, up_out, down_out):
    up_out[...] = dot_tn(hidden_ref[...], gup_ref[...]).astype(bf16)
    down_out[...] = dot_tn(act_ref[...], gdown_ref[...]).astype(bf16)


def feed_grads(hidden, gup, act, gdown):
    tokens, width = hidden.shape
    units = gup.shape[1]
    chunk = 512
    return pl.pallas_call(
        feed_grads_kernel,
        grid=(units // chunk,),
        in_specs=[
            whole((tokens, width)),
            pl.BlockSpec((tokens, chunk), lambda i: (0, i)),
            pl.BlockSpec((tokens, chunk), lambda i: (0, i)),
            whole((tokens, width)),
        ],
        out_specs=[
            pl.BlockSpec((width, chunk), lambda i: (0, i)),
            pl.BlockSpec((chunk, width), lambda i: (i, 0)),
        ],
        out_shape=[jax.ShapeDtypeStruct((width, units), bf16), jax.ShapeDtypeStruct((units, width), bf16)],
        compiler_params=params(),
        name="feed_grads",
    )(hidden, gup, act, gdown)


def square_grad_kernel(left_ref, right_ref, out_ref):
    out_ref[...] = dot_tn(left_ref[...], right_ref[...]).astype(bf16)


def square_grad(left, right):
    count, width = left.shape
    return pl.pallas_call(
        square_grad_kernel,
        grid=(1,),
        in_specs=[whole((count, width)), whole((count, width))],
        out_specs=whole((width, width)),
        out_shape=jax.ShapeDtypeStruct((width, width), bf16),
        compiler_params=params(),
        name="square_grad",
    )(left, right)


def last_kernel(start_ref, table_ref, x_ref, g_ref, gin_ref, out_ref, compress_ref, total):
    step = pl.program_id(0)

    @pl.when(step == 0)
    def _():
        total[...] = jnp.zeros_like(total)

    rows = x_ref.shape[1]
    g = g_ref[0]
    out_ref[0] = gin_ref[0] + dot_nt(table_ref[0], g)
    terms = dot(x_ref[0], g)
    begin, shift = aligned(start_ref[step])
    padded = jnp.concatenate([terms, jnp.zeros((TILE, terms.shape[1]), f32)], axis=0)
    total[pl.ds(begin, rows + TILE), :] += pltpu.roll(padded, shift, 0)

    @pl.when(step == pl.num_programs(0) - 1)
    def _():
        compress_ref[...] = total[: compress_ref.shape[0], :]


def last(starts, table, x, g, gin, longest):
    sets, rows, width = x.shape
    comp = table.shape[2]
    tokens = per_set((rows, width))
    grid_spec = pltpu.PrefetchScalarGridSpec(
        num_scalar_prefetch=1,
        grid=(sets,),
        in_specs=[per_set((rows, comp)), tokens, per_set((width, comp)), tokens],
        out_specs=[tokens, whole((longest, comp))],
        scratch_shapes=[pltpu.VMEM((longest + TILE, comp), f32)],
    )
    return pl.pallas_call(
        last_kernel,
        grid_spec=grid_spec,
        out_shape=[
            jax.ShapeDtypeStruct((sets, rows, width), f32),
            jax.ShapeDtypeStruct((longest, comp), f32),
        ],
        compiler_params=params(),
        name="last",
    )(starts, table, x, g, gin)


def sequence_sum(part, is_long, row_count, shortest):
    seq_count = lax.axis_size("seq")
    total = lax.psum(part, "seq")
    span = shortest // row_count
    if span > 1:
        groups = [list(range(i, i + span)) for i in range(0, seq_count, span)]
        part = lax.psum(part, "seq", axis_index_groups=groups)
    return jnp.where(is_long[:, None, None], total, part)


def table_start(set_kind, row_offset, block_index, row_count, shortest):
    position = block_index * row_count
    member = position // shortest
    chosen = jnp.sum(jnp.where(jnp.arange(4)[None, :] == member, row_offset, 0), axis=1)
    return jnp.where(set_kind > 0, position, chosen + position % shortest)


def local(
    inputs, cotangent, set_kind, row_offset, query_w, key_w, value_w, output_w, up_w, down_w, compress,
    first_gain, first_bias, second_gain, second_bias,
):
    sets, rows, width = inputs.shape
    longest, comp = compress.shape
    shortest = longest // 4
    ranked = lax.axis_index("seq")
    tokens = sets * rows
    is_long = set_kind > 0
    starts = table_start(set_kind, row_offset, ranked, rows, shortest).astype(jnp.int32)
    norms = jnp.concatenate(
        [jnp.stack([first_gain, first_bias, second_gain, second_bias]), jnp.zeros((4, width), f32)], axis=0
    )
    table, part, queries = front(starts, compress, inputs, query_w)
    linked = lax.axis_size("batch") == 8 and lax.axis_size("seq") == 4 and rows == shortest
    if linked:
        summed = line_sum(part, set_kind, 0)
    else:
        summed = sequence_sum(part, is_long, rows, shortest)
    (kc, vc, e, mixed, hidden, act, layer_out, gdown, gup, gfirst, gatt, go, norm_sums) = middle(
        summed, inputs, queries, cotangent, key_w, value_w, output_w, up_w, down_w, norms
    )
    flat = lambda v: v.reshape(-1, v.shape[-1])
    up_part, down_part = feed_grads(flat(hidden), flat(gup), flat(act), flat(gdown))
    output_part = square_grad(flat(mixed), flat(gatt))
    gq, gk, gv, g_part, gin = attention_back(
        e, go, mixed, queries, kc, vc, gfirst, query_w, key_w, value_w
    )
    if linked:
        g = line_sum(g_part, set_kind, 1)
    else:
        g = sequence_sum(g_part, is_long, rows, shortest)
    query_part = square_grad(flat(inputs), flat(gq))
    key_part = square_grad(flat(summed), flat(gk))
    value_part = square_grad(flat(summed), flat(gv))
    input_grad, compress_part = last(starts, table, inputs, g, gin, longest)

    def scattered(v):
        v = lax.psum_scatter(v, "seq", scatter_dimension=1, tiled=True)
        return lax.psum_scatter(v, "batch", scatter_dimension=0, tiled=True).astype(f32)

    parts = (query_part, key_part, value_part, output_part, up_part, down_part)
    if linked:
        weights = tuple(scatter(*parts))
        compress_grad, norm_grads = total_sum(compress_part, norm_sums)
    else:
        weights = tuple(scattered(v) for v in parts)
        compress_grad, norm_grads = lax.psum((compress_part, norm_sums), ("batch", "seq"))
    return (layer_out, input_grad) + weights + (compress_grad,) + tuple(norm_grads[i] for i in range(4))


def solution(mesh):
    tokens = P("batch", "seq", None)
    in_specs = (tokens, tokens, P("batch"), P("batch", None)) + (P(),) * 11
    out_specs = (tokens, tokens) + (P("batch", "seq"),) * 6 + (P(),) * 5
    return jax.shard_map(local, mesh=mesh, in_specs=in_specs, out_specs=out_specs, check_vma=False)
```

```python
import functools

import jax
import jax.numpy as jnp
from jax import lax
from jax.experimental import pallas as pl
from jax.experimental.pallas import tpu as pltpu
from jax.sharding import PartitionSpec as P

DH = 64
LANES = 128
TILE = 8
SCALE = DH ** (-0.5)
EPS = 1e-05
MESH = pl.DeviceIdType.MESH
VMEM_LIMIT = 63 * 1024 * 1024
bf16 = jnp.bfloat16
f32 = jnp.float32


def dot(left, right):
    return lax.dot_general(left, right, (((1,), (0,)), ((), ())), preferred_element_type=f32)


def dot_nt(left, right):
    return lax.dot_general(left, right, (((1,), (1,)), ((), ())), preferred_element_type=f32)


def dot_tn(left, right):
    return lax.dot_general(left, right, (((0,), (0,)), ((), ())), preferred_element_type=f32)


def params(**more):
    return pltpu.CompilerParams(vmem_limit_bytes=VMEM_LIMIT, **more)


def whole(shape):
    return pl.BlockSpec(shape, lambda *_: (0,) * len(shape), pipeline_mode=pl.Buffered(1))


def per_set(shape):
    return pl.BlockSpec((1,) + tuple(shape), lambda s, *_: (s,) + (0,) * len(shape))


def aligned(start):
    begin = start // TILE * TILE
    return pl.multiple_of(begin, TILE), start - begin


def place():
    batch = lax.axis_index("batch")
    return batch // 4, batch // 2 % 2, batch % 2, lax.axis_index("seq")


def device(y, x, core, z):
    return ((y * 2 + x) * 2 + core, z)


def greet(others):
    barrier = pltpu.get_barrier_semaphore()
    for other in others:
        pl.semaphore_signal(barrier, inc=1, device_id=other, device_id_type=MESH)
    pl.semaphore_wait(barrier, len(others))


def remote(src, dst, send_sem, recv_sem, target):
    return pltpu.make_async_remote_copy(src, dst, send_sem, recv_sem, device_id=target, device_id_type=MESH)


class LineSum:
    def __init__(self, line, lag, own, from_left, from_right, sems):
        y, x, core, self.z = place()
        self.line, self.lag, self.own = line, lag, own
        self.right = device(y, x, core, (self.z + 1) % line)
        self.left = device(y, x, core, (self.z + line - 1) % line)
        inner, outer = self.z > 0, self.z < line - 1
        self.ways = (
            (from_left, self.right, inner, outer, sems[0], sems[1]),
            (from_right, self.left, outer, inner, sems[2], sems[3]),
        )

    def greet(self):
        barrier = pltpu.get_barrier_semaphore()
        for way in self.ways:

            @pl.when(way[3])
            def _():
                pl.semaphore_signal(barrier, inc=1, device_id=way[1], device_id_type=MESH)

        both = jnp.logical_and(self.z > 0, self.z < self.line - 1).astype(jnp.int32)
        pl.semaphore_wait(barrier, 1 + both)

    def prepare(self):
        for way in self.ways:

            @pl.when(jnp.logical_not(way[2]))
            def _():
                way[0][...] = jnp.zeros_like(way[0])

    def copy(self, way, at):
        held, target, _, _, send, recv = way
        return remote(held.at[at], held.at[at], send.at[at], recv.at[at], target)

    def forward(self, way, at):
        @pl.when(way[2])
        def _():
            self.copy(way, at).wait_recv()

        way[0][at] = way[0][at] + self.own[at]

        @pl.when(way[3])
        def _():
            self.copy(way, at).start()

    def slots(self):
        return self.own.shape[0] + self.lag * (self.line - 1)

    def serve(self, slot):
        for way, hops in zip(self.ways, (self.z, self.line - 1 - self.z)):
            at = slot - self.lag * hops

            @pl.when(jnp.logical_and(at >= 0, at < self.own.shape[0]))
            def _():
                self.forward(way, at)

    def serve_many(self, begin, count):
        def slot(at, carry):
            self.serve(at)
            return carry

        lax.fori_loop(begin, begin + count, slot, 0)

    def total(self, at, joined):
        own = self.own[at].astype(f32)
        both = self.ways[0][0][at].astype(f32) + self.ways[1][0][at].astype(f32)
        return jnp.where(joined, both - own, own).astype(bf16)

    def finish(self):
        for way in self.ways:

            @pl.when(way[3])
            def _():
                def wait(at, carry):
                    self.copy(way, at).wait_send()
                    return carry

                lax.fori_loop(0, self.own.shape[0], wait, 0)


class Scatter:
    def __init__(self, x_first, part, from_core, from_first, from_second, send, recv):
        y, x, core, z = place()
        self.part, self.recvs = part, (from_core, from_first, from_second)
        along_x, along_y = device(y, 1 - x, core, z), device(1 - y, x, core, z)
        self.core, self.x, self.y, self.x_first = core, x, y, x_first
        if x_first:
            sources = (part.at[:, :, 1 - core], from_core.at[:, 1 - x], from_first.at[1 - y])
            targets = (device(y, x, 1 - core, z), along_x, along_y)
        else:
            sources = (part.at[:, :, 1 - core], from_core.at[1 - y], from_first.at[1 - x])
            targets = (device(y, x, 1 - core, z), along_y, along_x)
        self.copies = [
            remote(sources[i], self.recvs[i], send.at[i], recv.at[i], targets[i]) for i in range(3)
        ]

    def start(self):
        self.copies[0].start()

    def first(self):
        self.copies[0].wait()
        self.recvs[0][...] = self.recvs[0][...] + self.part[:, :, self.core]
        self.copies[1].start()

    def second(self):
        self.copies[1].wait_recv()
        kept = self.recvs[0][:, self.x] if self.x_first else self.recvs[0][self.y]
        self.recvs[1][...] = self.recvs[1][...] + kept
        self.copies[2].start()

    def done(self):
        self.copies[2].wait_recv()
        kept = self.recvs[1][self.y] if self.x_first else self.recvs[1][self.x]
        return self.recvs[2][...].astype(f32) + kept.astype(f32)

    def finish(self):
        for copy in self.copies[1:]:
            copy.wait_send()


class LineScatter:
    def __init__(self, line, blocks, arrived, send, recv):
        y, x, core, self.z = place()
        self.blocks, self.arrived, self.line = blocks, arrived, line
        self.copies = []
        for d in range(1, line):
            to = (self.z + d) % line
            self.copies.append(
                remote(blocks.at[to], arrived.at[d - 1], send.at[d - 1], recv.at[d - 1], device(y, x, core, to))
            )

    def start(self):
        for copy in self.copies:
            copy.start()

    def done(self):
        total = self.blocks[self.z].astype(f32)
        for d, copy in enumerate(self.copies):
            copy.wait_recv()
            total = total + self.arrived[d].astype(f32)
        return total

    def finish(self):
        for copy in self.copies:
            copy.wait_send()


def line_scatter_blocks(blocks, rows, line):
    step = rows.shape[1] // line
    for z in range(line):
        mine = rows[:, z * step : (z + 1) * step]
        if step % LANES:
            top = rows.shape[0] // 2
            mine = jnp.concatenate([mine[:top], mine[top:]], axis=1)
        blocks[z] = mine.astype(bf16)


def unfold(total, out):
    if total.shape[1] == out.shape[1]:
        out[...] = total
    else:
        top, step = total.shape[0], out.shape[1]
        out[:top, :] = total[:, :step]
        out[top:, :] = total[:, step:]


def block_shape(rows, width, line):
    step = width // line
    return (rows, step) if step % LANES == 0 else (rows // 2, step * 2)


def scatter_scratch(rows, width):
    shapes = [(2, 2, rows, width), (2, rows, width), (rows, width)]
    return [pltpu.VMEM(shape, bf16) for shape in shapes] + [pltpu.SemaphoreType.DMA((3,))] * 2


def line_scratch(rows, width, line):
    block = block_shape(rows, width, line)
    return [pltpu.VMEM((n,) + block, bf16) for n in (line, line - 1)] + [pltpu.SemaphoreType.DMA((line - 1,))] * 2


class Neighbours:
    def __init__(self, line):
        y, x, core, z = place()
        self.core = device(y, x, 1 - core, z)
        places = [((y + dy) % 2, (x + dx) % 2) for dy, dx in ((0, 1), (1, 0), (1, 1))]
        self.plane = [(py * 2 + px, device(py, px, core, z)) for py, px in places]
        self.line = [((z + d) % line, device(y, x, core, (z + d) % line)) for d in range(1, line)]

    def everyone(self):
        return [self.core] + [to for _, to in self.plane] + [to for _, to in self.line]


class Total:
    counts = lambda line: (2, 6, 2 * (line - 1), line - 1, 3, 1)

    def __init__(self, line, near, table, norms, table_out, norms_out, mine, from_core, from_plane, from_line, gathered,
                 core_norms, plane_norms, line_norms, *sems):
        y, x, core, z = place()
        plane = y * 2 + x
        pairs = [(sems[2 * i], sems[2 * i + 1]) for i in range(6)]
        self.running = []

        def start(stage, moves):
            send, recv = pairs[stage]
            self.running = [remote(src, dst, send.at[i], recv.at[i], to) for i, (src, dst, to) in enumerate(moves)]
            for copy in self.running:
                copy.start()

        def to_core():
            mine[...] = table[...].astype(bf16)
            core_norms[0] = norms[...]
            start(0, [(mine.at[1 - core], from_core, near.core), (core_norms.at[0], core_norms.at[1], near.core)])

        def to_plane():
            from_core[...] = from_core[...] + mine[core]
            plane_norms[plane] = core_norms[0] + core_norms[1]
            kept = plane_norms.at[plane]
            start(1, [(from_core.at[p], from_plane.at[i], to) for i, (p, to) in enumerate(near.plane)]
                  + [(kept, kept, to) for _, to in near.plane])

        def to_line():
            total = from_core[plane].astype(f32)
            for i in range(3):
                total = total + from_plane[i].astype(f32)
            mine[0, 0] = total.astype(bf16)
            line_norms[z] = plane_norms[0] + plane_norms[1] + plane_norms[2] + plane_norms[3]
            kept = line_norms.at[z]
            start(2, [(mine.at[0, 0, p], from_line.at[i], to) for i, (p, to) in enumerate(near.line)]
                  + [(kept, kept, to) for _, to in near.line])

        def back_line():
            total = mine[0, 0, z].astype(f32)
            for i in range(line - 1):
                total = total + from_line[i].astype(f32)
            gathered[core, plane, z] = total.astype(bf16)
            all_norms = line_norms[0]
            for i in range(1, line):
                all_norms = all_norms + line_norms[i]
            norms_out[...] = all_norms
            block = gathered.at[core, plane, z]
            start(3, [(block, block, to) for _, to in near.line])

        def back_plane():
            block = gathered.at[core, plane]
            start(4, [(block, block, to) for _, to in near.plane])

        def back_core():
            block = gathered.at[core]
            start(5, [(block, block, near.core)])

        def close():
            table_out[...] = gathered[...].astype(f32)

        self.stages = [to_core, to_plane, to_line, back_line, back_plane, back_core, close]

    def advance(self):
        for copy in self.running:
            copy.wait()
        self.running = []
        self.stages.pop(0)()

    @staticmethod
    def scratch(line, shape, norms):
        vmem = pltpu.VMEM
        return [
            vmem(shape, bf16), vmem(shape[1:], bf16), vmem((3,) + shape[2:], bf16), vmem((line - 1,) + shape[3:], bf16),
            vmem(shape, bf16), vmem((2,) + norms, f32), vmem((4,) + norms, f32), vmem((line,) + norms, f32),
        ] + [pltpu.SemaphoreType.DMA((n,)) for n in Total.counts(line) for _ in range(2)]


def closing_kernel(line, table_ref, norms_ref, x_any, gq_any, c_any, gk_any, gv_any, up_ref, down_ref,
                   table_out, norms_out, up_out, down_out, query_out, key_out, value_out,
                   x, gq, c, gk, gv, load_sems, *scratch):
    scratch = list(scratch)
    take = lambda n: [scratch.pop(0) for _ in range(n)]
    pairs = ((x_any, x), (gq_any, gq), (c_any, c), (gk_any, gk), (gv_any, gv))
    loads = [pltpu.make_async_copy(src, dst, load_sems.at[i]) for i, (src, dst) in enumerate(pairs)]
    for load in loads:
        load.start()
    near = Neighbours(line)
    greet(near.everyone())
    total = Total(line, near, table_ref, norms_ref, table_out, norms_out, *take(8 + 12))
    total.advance()
    across = []
    for rows, out in ((up_ref, up_out), (down_ref, down_out)):
        job = LineScatter(line, *take(4))
        line_scatter_blocks(job.blocks, rows[...], line)
        job.start()
        across.append((job, out))
    jobs = []
    for i, (left, right) in enumerate(((x, gq), (c, gk), (c, gv))):
        part = take(1)[0]
        jobs.append((Scatter(i % 2 == 0, part, *take(5)), LineScatter(line, *take(4)), (query_out, key_out, value_out)[i]))
        for load in ((loads[0], loads[1]), (loads[2], loads[3]), (loads[4],))[i]:
            load.wait()
        part[...] = dot_tn(left[...], right[...]).astype(bf16).reshape(part.shape)
        jobs[i][0].start()
        if i == 0:
            total.advance()
        if i > 0:
            jobs[i - 1][0].first()
    total.advance()
    jobs[2][0].first()
    total.advance()
    jobs[0][0].second()
    total.advance()
    jobs[1][0].second()
    jobs[2][0].second()
    for job, line_job, _ in jobs:
        line_scatter_blocks(line_job.blocks, job.done(), line)
        line_job.start()
    total.advance()
    for job, out in across:
        unfold(job.done(), out)
    total.advance()
    for _, line_job, out in jobs:
        unfold(line_job.done(), out)
    for job, _ in across:
        job.finish()
    for job, line_job, _ in jobs:
        job.finish()
        line_job.finish()


def closing(table, norms, x, gq, c, gk, gv, up_rows, down_rows):
    line = lax.axis_size("seq")
    longest, comp = table.shape
    width = x.shape[1]
    shape = (2, 4, line, longest // (8 * line), comp)
    rows = width // 8
    vmem, anywhere = pl.BlockSpec(memory_space=pltpu.VMEM), pl.BlockSpec(memory_space=pl.ANY)
    out = lambda *dims: jax.ShapeDtypeStruct(dims, f32)
    scratch = [pltpu.VMEM(v.shape, bf16) for v in (x, gq, c, gk, gv)] + [pltpu.SemaphoreType.DMA((5,))]
    scratch += Total.scratch(line, shape, norms.shape)
    for v in (up_rows, down_rows):
        scratch += line_scratch(v.shape[0], v.shape[1], line)
    for _ in range(3):
        scratch += [pltpu.VMEM((2, 2, 2, rows, width), bf16)] + scatter_scratch(rows, width) + line_scratch(rows, width, line)
    table_out, *rest = pl.pallas_call(
        functools.partial(closing_kernel, line),
        in_specs=[vmem] * 2 + [anywhere] * 5 + [vmem] * 2,
        out_specs=[vmem] * 7,
        out_shape=[out(*shape), out(*norms.shape), out(up_rows.shape[0], up_rows.shape[1] // line),
                   out(down_rows.shape[0], down_rows.shape[1] // line)] + [out(rows, width // line)] * 3,
        scratch_shapes=scratch,
        compiler_params=params(collective_id=3, has_side_effects=True),
        name="closing",
    )(table.reshape(shape), norms, x, gq, c, gk, gv, up_rows, down_rows)
    return [table_out.reshape(longest, comp)] + rest


def front_kernel(start_ref, compress_ref, x_ref, wq_ref, table_ref, c_ref, q_ref, wide):
    step = pl.program_id(0)

    longest = compress_ref.shape[0]

    @pl.when(step == 0)
    def _():
        wide[:longest, :] = compress_ref[...].astype(f32)
        wide[longest:, :] = jnp.zeros((TILE, wide.shape[1]), f32)

    rows = x_ref.shape[1]
    begin, shift = aligned(start_ref[step])
    window = wide[pl.ds(begin, rows + TILE), :]
    table = pltpu.roll(window, lax.rem(rows + TILE - shift, rows + TILE), 0)[:rows].astype(bf16)
    table_ref[0] = table
    x = x_ref[0]
    c_ref[0] = dot_tn(table, x).astype(bf16)
    q_ref[0] = (dot(x, wq_ref[...]) * SCALE).astype(bf16)


def front(starts, compress, x, wq):
    sets, rows, width = x.shape
    longest, comp = compress.shape
    grid_spec = pltpu.PrefetchScalarGridSpec(
        num_scalar_prefetch=1,
        grid=(sets,),
        in_specs=[whole(compress.shape), per_set((rows, width)), whole(wq.shape)],
        out_specs=[per_set((rows, comp)), per_set((comp, width)), per_set((rows, width))],
        scratch_shapes=[pltpu.VMEM((longest + TILE, comp), f32)],
    )
    return pl.pallas_call(
        front_kernel,
        grid_spec=grid_spec,
        out_shape=[
            jax.ShapeDtypeStruct((sets, rows, comp), bf16),
            jax.ShapeDtypeStruct((sets, comp, width), bf16),
            jax.ShapeDtypeStruct((sets, rows, width), bf16),
        ],
        compiler_params=params(),
        name="front",
    )(starts, compress, x, wq)


def head_blocks(pair, first_half):
    zero = jnp.zeros_like(pair)
    return jnp.concatenate([jnp.where(first_half, pair, zero), jnp.where(first_half, zero, pair)], axis=0)


def norm_forward(v):
    average = jnp.mean(v, axis=-1, keepdims=True)
    centered = v - average
    variance = jnp.mean(centered * centered, axis=-1, keepdims=True)
    inverse = lax.rsqrt(variance + EPS)
    return centered * inverse, inverse


def norm_backward(dz, z, inverse):
    return (dz - jnp.mean(dz, axis=-1, keepdims=True) - z * jnp.mean(dz * z, axis=-1, keepdims=True)) * inverse


PIECES = 4
LAG = 2


def layer_kernel(
    line, starts_ref, long_ref, compress_ref, c_ref, x_any, cot_ref, norms_ref, wq_any, wk_any, wv_any, wo_any, up_any, down_any,
    kc_ref, vc_ref, csum_ref, mixed_ref, hidden_ref, out_ref, gdown_ref, gfirst_ref, go_ref, table_any, q_any,
    e_any, act_any, gup_any, output_grad_ref, sums_ref,
    xs, qs, wq, wk, wv, wo, up, down, e_buf, act, gup, z_first, rinv_ref, output_grad, weight_sems, x_sems, out_sems,
    *linked,
):
    step = pl.program_id(0)
    last = pl.num_programs(0) - 1
    sets, rows, width = xs.shape
    comp = kc_ref.shape[1]
    units = up.shape[1]
    chunk = 768
    loads = [
        pltpu.make_async_copy(src, dst, weight_sems.at[i])
        for i, (src, dst) in enumerate(
            ((wq_any, wq), (wk_any, wk), (wv_any, wv), (wo_any, wo), (up_any, up), (down_any, down))
        )
    ]
    x_loads = [pltpu.make_async_copy(x_any.at[s], xs.at[s], x_sems.at[s]) for s in range(sets)]
    q_store = pltpu.make_async_copy(qs, q_any, out_sems.at[3])
    e_store = pltpu.make_async_copy(e_buf, e_any.at[step], out_sems.at[0])
    act_store = pltpu.make_async_copy(act, act_any.at[step], out_sems.at[1])
    gup_store = pltpu.make_async_copy(gup, gup_any.at[step], out_sems.at[2])

    if line:
        tables, own, from_left, from_right, table_sems, *sems = linked
        sums = LineSum(line, LAG, own, from_left, from_right, sems)
        ahead = PIECES + LAG * (line - 1)
        t_stores = [pltpu.make_async_copy(tables.at[s], table_any.at[s], table_sems.at[s]) for s in range(sets)]

    def first_use(load):
        @pl.when(step == 0)
        def _():
            load.wait()

    @pl.when(step == 0)
    def _():
        for load in x_loads[:1] + loads[:1] + x_loads[1:] + loads[1:]:
            load.start()
        sums_ref[...] = jnp.zeros_like(sums_ref)
        output_grad[...] = jnp.zeros_like(output_grad)
        if line:
            longest = compress_ref.shape[0]
            sums.greet()
            sums.prepare()
            grid = (rows, rows)
            ahead_by = lax.broadcasted_iota(jnp.int32, grid, 1) - lax.broadcasted_iota(jnp.int32, grid, 0)
        slot = 0
        for s in range(sets):
            x_loads[s].wait()
            if line:
                table = jnp.zeros((rows, comp), f32)
                for at in range(0, longest, rows):
                    chosen = jnp.where(ahead_by == starts_ref[s] - at, 1.0, 0.0).astype(bf16)
                    table = table + dot(chosen, compress_ref[at : at + rows, :])
                table = table.astype(bf16)
                tables[s] = table
                t_stores[s].start()
                own[s * PIECES : (s + 1) * PIECES] = (
                    dot_tn(table, xs[s]).astype(bf16).reshape(PIECES, comp // PIECES, width)
                )
                sums.serve(slot)
                slot += 1
        loads[0].wait()
        for s in range(sets):
            qs[s] = (dot(xs[s], wq[...]) * SCALE).astype(bf16)
            if line:
                sums.serve(slot)
                slot += 1
        q_store.start()
        if line:
            sums.serve_many(slot, ahead - slot)

    def serve(part):
        if line:
            count = PIECES // 4

            @pl.when(step < last)
            def _():
                sums.serve_many(ahead + step * PIECES + part * count, count)

    if line:
        joined = long_ref[step] > 0
        for piece in range(PIECES):
            size = comp // PIECES
            csum_ref[0, piece * size : (piece + 1) * size, :] = sums.total(step * PIECES + piece, joined)
    else:
        csum_ref[0] = c_ref[0]
    first_use(loads[1])
    first_use(loads[2])
    c = csum_ref[0]
    kc_ref[0] = dot(c, wk[...]).astype(bf16)
    vc_ref[0] = dot(c, wv[...]).astype(bf16)
    half = lax.broadcasted_iota(jnp.int32, (comp, LANES), 1) < DH
    ones = head_blocks(jnp.ones((comp, LANES), bf16), half)

    @pl.when(step > 0)
    def _():
        e_store.wait()

    for pair in range(width // LANES):
        lanes = pl.ds(pair * LANES, LANES)
        keys = head_blocks(kc_ref[0, :, lanes], half)
        values = jnp.concatenate([head_blocks(vc_ref[0, :, lanes], half), ones], axis=1)
        scores = dot_nt(qs[step, :, lanes], keys)
        parts = []
        for head in range(2):
            mine = scores[:, head * comp : (head + 1) * comp]
            top = jnp.max(mine, axis=-1, keepdims=True)
            parts.append(jnp.exp(mine - top).astype(bf16))
        e = jnp.concatenate(parts, axis=1)
        e_buf[:, pl.ds(pair * 2 * comp, 2 * comp)] = e
        total = dot(e, values)
        rinv = 1.0 / total[:, LANES:]
        rinv_ref[:, lanes] = rinv
        mixed_ref[0, :, lanes] = (total[:, :LANES] * rinv).astype(bf16)
    e_store.start()
    first_use(loads[3])
    serve(0)
    gain1, bias1, gain2, bias2 = (norms_ref[i : i + 1, :] for i in range(4))
    z1, inv1 = norm_forward(xs[step].astype(f32) + dot(mixed_ref[0], wo[...]))
    z_first[...] = z1
    hidden = z1 * gain1 + bias1
    hidden_low = hidden.astype(bf16)
    hidden_ref[0] = hidden_low
    gfirst_ref[0] = hidden
    first_use(loads[4])
    first_use(loads[5])

    @pl.when(step > 0)
    def _():
        act_store.wait()
        gup_store.wait()

    for at in range(0, units, chunk):
        span = pl.ds(at, chunk)
        upward = dot(hidden_low, up[:, span])
        cdf = 0.5 + 0.5 * lax.erf(upward * (0.5**0.5))
        density = jnp.exp(upward * upward * -0.5) * 0.3989422804014327
        act[:, span] = (upward * cdf).astype(bf16)
        gup[:, span] = (cdf + upward * density).astype(bf16)
    act_store.start()
    serve(1)
    z2, inv2 = norm_forward(gfirst_ref[0] + dot(act[...], down[...]))
    out_ref[0] = (z2 * gain2 + bias2).astype(bf16)
    dy = cot_ref[0].astype(f32)
    gsecond = norm_backward(dy * gain2, z2, inv2)
    gain2_part = jnp.sum(dy * z2, axis=0, keepdims=True)
    bias2_part = jnp.sum(dy, axis=0, keepdims=True)
    gdown = gsecond.astype(bf16)
    gdown_ref[0] = gdown
    gfirst_ref[0] = gsecond
    for at in range(0, units, chunk):
        span = pl.ds(at, chunk)
        gact = dot_nt(gdown, down[span, :])
        gup[:, span] = (gact * gup[:, span].astype(f32)).astype(bf16)
    gup_store.start()
    serve(2)
    ghidden = gfirst_ref[0] + dot_nt(gup[...], up[...])
    z1 = z_first[...]
    gfirst = norm_backward(ghidden * gain1, z1, inv1)
    gain1_part = jnp.sum(ghidden * z1, axis=0, keepdims=True)
    bias1_part = jnp.sum(ghidden, axis=0, keepdims=True)
    gfirst_ref[0] = gfirst
    gatt = gfirst.astype(bf16)
    go_ref[0] = (dot_nt(gatt, wo[...]) * rinv_ref[...]).astype(bf16)
    output_grad[...] += dot_tn(mixed_ref[0], gatt)
    for i, part in enumerate((gain1_part, bias1_part, gain2_part, bias2_part)):
        sums_ref[i : i + 1, :] += part
    serve(3)

    @pl.when(step == last)
    def _():
        output_grad_ref[...] = output_grad[...].astype(bf16)
        e_store.wait()
        act_store.wait()
        gup_store.wait()
        q_store.wait()
        if line:
            for store in t_stores:
                store.wait()
            sums.finish()


def layer(starts, set_kind, compress, c, x, cot, weights, norms, line):
    sets, rows, width = x.shape
    longest, comp = compress.shape
    wq, wk, wv, wo, up, down = weights
    units = up.shape[1]
    tokens = per_set((rows, width))
    short = per_set((comp, width))
    anywhere = pl.BlockSpec(memory_space=pl.ANY)
    smem = pl.BlockSpec(memory_space=pltpu.SMEM)
    shape = lambda *dims, kind=bf16: jax.ShapeDtypeStruct(dims, kind)
    dma = lambda n: pltpu.SemaphoreType.DMA((n,))
    linked = []
    if line:
        count = sets * PIECES
        linked = [pltpu.VMEM((sets, rows, comp), bf16)]
        linked += [pltpu.VMEM((count, comp // PIECES, width), bf16)] * 3 + [dma(sets)] + [dma(count)] * 4
    more = dict(collective_id=0, has_side_effects=True) if line else {}
    return pl.pallas_call(
        functools.partial(layer_kernel, line),
        grid=(sets,),
        in_specs=[smem, smem, whole(compress.shape), whole((1, 8, LANES)) if line else short, anywhere, tokens, whole(norms.shape)]
        + [anywhere] * 6,
        out_specs=[short] * 3 + [tokens] * 6 + [anywhere] * 5 + [whole((width, width)), whole((8, width))],
        out_shape=[shape(sets, comp, width)] * 3
        + [shape(sets, rows, width)] * 4
        + [shape(sets, rows, width, kind=f32), shape(sets, rows, width)]
        + [shape(sets, rows, comp), shape(sets, rows, width)]
        + [shape(sets, rows, width // DH * comp)]
        + [shape(sets, rows, units)] * 2
        + [shape(width, width), shape(8, width, kind=f32)],
        scratch_shapes=[pltpu.VMEM(x.shape, bf16)] * 2
        + [pltpu.VMEM(w.shape, bf16) for w in weights]
        + [pltpu.VMEM((rows, width // DH * comp), bf16)]
        + [pltpu.VMEM((rows, units), bf16)] * 2
        + [pltpu.VMEM((rows, width), f32)] * 2
        + [pltpu.VMEM((width, width), f32), dma(6), dma(sets), dma(4)]
        + linked,
        compiler_params=params(**more),
        name="layer",
    )(starts, set_kind, compress, c, x, cot, norms, *weights)


def pair_back(pair, e_ref, go_ref, mixed_ref, q_ref, kc_ref, vc_ref, gq_ref, gkt, gvt, half, minus):
    comp = kc_ref.shape[0]
    lanes = pl.ds(pair * LANES, LANES)
    e = e_ref[:, pl.ds(pair * 2 * comp, 2 * comp)]
    keys = head_blocks(kc_ref[:, lanes], half)
    values = jnp.concatenate([head_blocks(vc_ref[:, lanes], half), minus], axis=1)
    go = go_ref[:, lanes]
    delta = (go.astype(f32) * mixed_ref[:, lanes].astype(f32)).astype(bf16)
    gp = dot_nt(jnp.concatenate([go, delta], axis=1), values)
    gs = (gp * e.astype(f32)).astype(bf16)
    gq_ref[:, lanes] = (dot(gs, keys) * SCALE).astype(bf16)
    for into, left, right in ((gkt, q_ref[:, lanes], gs), (gvt, go, e)):
        both = dot_tn(left, right)
        at = pair * LANES
        into[at : at + DH, :] = both[:DH, :comp].astype(bf16)
        into[at + DH : at + LANES, :] = both[DH:, comp:].astype(bf16)


CHUNKS = 3


def back_kernel(
    line, long_ref, hidden_any, gup_any, act_any, gdown_any, output_any, e_any, go_any, mixed_any, q_any, kc_any, vc_any, gfirst_any,
    wq_any, wk_any, wv_any,
    gq_any, gk_any, gv_any, g_any, gin_any, up_out, down_out, output_out, up_rows, down_rows,
    hidden, gdown, feed, wq, wk, wv, e, go, mixed, q, kc, vc, gin, gq, gkt, gvt, gk, gv, own, from_left, from_right,
    up_part, down_part, output_part, load_sems, feed_sems, set_sems, gin_sems, out_sems, *scratch,
):
    scratch = list(scratch)
    take = lambda n: [scratch.pop(0) for _ in range(n)]
    sets, rows, width = q_any.shape
    comp = kc_any.shape[1]
    units = gup_any.shape[1]
    sums = LineSum(line, LAG, own, from_left, from_right, take(4))

    def copies(pairs, sems):
        return [pltpu.make_async_copy(src, dst, sems.at[i]) for i, (src, dst) in enumerate(pairs)]

    def feed_loads(chunk, which):
        if which == 0:
            wide, count, source = units // line, line, gup_any
        else:
            wide, count, source = units // 8, 8, act_any
        step = wide // CHUNKS
        return copies(
            [(source.at[:, pl.ds(i * wide + chunk * step, step)], feed.at[which, :, pl.ds(i * step, step)]) for i in range(count)],
            feed_sems.at[which],
        )

    def set_loads(s):
        at = s % 2
        return copies(
            [(e_any.at[s], e.at[at]), (go_any.at[s], go.at[at]), (mixed_any.at[s], mixed.at[at]), (q_any.at[s], q.at[at]),
             (kc_any.at[s], kc.at[at]), (vc_any.at[s], vc.at[at])],
            set_sems.at[at],
        )

    def gin_load(s):
        return pltpu.make_async_copy(gfirst_any.at[s], gin, gin_sems.at[0])

    def set_stores(s):
        return copies([(gin, gin_any.at[s]), (gq, gq_any.at[s]), (gk, gk_any.at[s]), (gv, gv_any.at[s])], out_sems)

    def begin(some):
        for copy in some:
            copy.start()

    def end(some):
        for copy in some:
            copy.wait()

    weights = copies(((output_any, output_part), (hidden_any, hidden), (gdown_any, gdown), (wq_any, wq), (wk_any, wk), (wv_any, wv)), load_sems)
    begin(weights[:2])
    begin(feed_loads(0, 0))
    begin(weights[2:3])
    begin(feed_loads(0, 1))
    begin(set_loads(0))
    begin(weights[3:])
    begin(set_loads(1))
    gin_load(0).start()
    near = Neighbours(line)
    greet(near.everyone())
    sums.prepare()

    jobs = {"o": (Scatter(True, output_part, *take(5)), LineScatter(line, *take(4)), output_out)}
    for chunk in range(CHUNKS):
        for which, part in ((0, up_part), (1, down_part)):
            job = Scatter(which == 0, part.at[chunk % 2], *take(5))
            if chunk < CHUNKS - 1:
                if which == 0:
                    out = up_out.at[:, pl.ds(chunk * up_out.shape[1] // 2, up_out.shape[1] // 2)]
                else:
                    out = down_out.at[pl.ds(chunk * down_out.shape[0] // 2, down_out.shape[0] // 2), :]
                jobs[which, chunk] = (job, LineScatter(line, *take(4)), out)
            else:
                jobs[which, chunk] = (job, None, (up_rows, down_rows)[which])

    def across(name):
        job, line_job, _ = jobs[name]
        line_scatter_blocks(line_job.blocks, job.done(), line)
        line_job.start()

    def feed_grad(chunk, which):
        end(feed_loads(chunk, which))
        if chunk == 0:
            weights[1 + which].wait()
        if which == 0:
            grad = dot_tn(hidden[...], feed[0])
        else:
            grad = dot_tn(feed[1], gdown[...])
        part = (up_part, down_part)[which]
        part[chunk % 2] = grad.astype(bf16).reshape(part.shape[1:])
        if chunk + 1 < CHUNKS:
            begin(feed_loads(chunk + 1, which))
        jobs[which, chunk][0].start()

    half = lax.broadcasted_iota(jnp.int32, (comp, LANES), 1) < DH
    minus = head_blocks(jnp.full((comp, LANES), -1.0, bf16), half)

    def heads(s):
        at = s % 2
        end(set_loads(s))
        if s > 0:
            end(set_stores(s - 1))
            gin_load(s).start()
        for pair in range(width // LANES):
            pair_back(pair, e.at[at], go.at[at], mixed.at[at], q.at[at], kc.at[at], vc.at[at], gq, gkt, gvt, half, minus)
        if s + 2 < sets:
            begin(set_loads(s + 2))

    def joins(s):
        if s == 0:
            end(weights[3:])
        g = dot(wk[...], gkt[...]) + dot(wv[...], gvt[...])
        own[s * PIECES : (s + 1) * PIECES] = g.astype(bf16).reshape(PIECES, width // PIECES, comp)
        gk[...] = gkt[...].T
        gv[...] = gvt[...].T
        gin_load(s).wait()
        gin[...] = gin[...] + dot_nt(gq[...], wq[...])
        begin(set_stores(s))

    slots = iter(range(sums.slots()))

    def serve(count):
        first = next(slots)
        for _ in range(count - 1):
            next(slots)
        sums.serve_many(first, count)

    weights[0].wait()
    jobs["o"][0].start()
    feed_grad(0, 0)
    jobs["o"][0].first()
    feed_grad(0, 1)
    jobs[0, 0][0].first()
    heads(0)
    jobs[1, 0][0].first()
    joins(0)
    serve(2)
    jobs["o"][0].second()
    feed_grad(1, 0)
    jobs[0, 0][0].second()
    serve(2)
    heads(1)
    jobs[1, 0][0].second()
    jobs[0, 1][0].first()
    joins(1)
    across("o")
    serve(2)
    feed_grad(1, 1)
    across((0, 0))
    serve(2)
    heads(2)
    jobs[1, 1][0].first()
    across((1, 0))
    joins(2)
    jobs[0, 1][0].second()
    serve(2)
    feed_grad(2, 0)
    serve(2)
    heads(3)
    jobs[0, 2][0].first()
    jobs[1, 1][0].second()
    joins(3)
    serve(2)
    feed_grad(2, 1)
    across((0, 1))
    serve(2)
    jobs[1, 2][0].first()
    serve(1)
    across((1, 1))
    serve(1)
    jobs[0, 2][0].second()
    serve(2)
    jobs[1, 2][0].second()
    serve(2)
    for s in range(sets):
        for piece in range(s * PIECES, (s + 1) * PIECES):
            own[piece] = sums.total(piece, long_ref[s] > 0)
    g_store = pltpu.make_async_copy(own, g_any, gin_sems.at[1])
    g_store.start()
    for name in jobs:
        job, line_job, out = jobs[name]
        if line_job is None:
            out[...] = job.done().astype(bf16)
        else:
            unfold(line_job.done(), out)
    for name in jobs:
        job, line_job, _ = jobs[name]
        job.finish()
        if line_job is not None:
            line_job.finish()
    end(set_stores(sets - 1))
    g_store.wait()
    sums.finish()


def back(set_kind, hidden, gup, act, gdown, output_part, e, go, mixed, q, kc, vc, gfirst, wq, wk, wv):
    line = lax.axis_size("seq")
    sets, rows, width = q.shape
    comp = kc.shape[1]
    tokens, units = gup.shape
    eighth = width // 8
    wide, tall = units // CHUNKS, units // 8 // CHUNKS
    count = sets * PIECES
    dma = lambda *n: pltpu.SemaphoreType.DMA(n)
    vmem, anywhere = pl.BlockSpec(memory_space=pltpu.VMEM), pl.BlockSpec(memory_space=pl.ANY)
    shape = lambda *dims, kind=bf16: jax.ShapeDtypeStruct(dims, kind)
    buffer = lambda *dims, kind=bf16: pltpu.VMEM(dims, kind)
    done = CHUNKS - 1
    scratch = [buffer(tokens, width)] * 2 + [buffer(2, tokens, wide)] + [buffer(width, width)] * 3
    scratch += [buffer(2, rows, e.shape[2])] + [buffer(2, rows, width)] * 3 + [buffer(2, comp, width)] * 2
    scratch += [buffer(rows, width, kind=f32), buffer(rows, width)] + [buffer(width, comp)] * 2 + [buffer(comp, width)] * 2
    scratch += [buffer(count, width // PIECES, comp)] * 3
    scratch += [buffer(2, 2, 2, 2, eighth, wide), buffer(2, 2, 2, 2, tall, width), buffer(2, 2, 2, eighth, width)]
    scratch += [dma(6), dma(2, 8), dma(2, 6), dma(2), dma(4)] + [dma(count)] * 4
    scratch += scatter_scratch(eighth, width) + line_scratch(eighth, width, line)
    for chunk in range(CHUNKS):
        for size in ((eighth, wide), (tall, width)):
            scratch += scatter_scratch(*size)
            if chunk < done:
                scratch += line_scratch(*size, line)
    return pl.pallas_call(
        functools.partial(back_kernel, line),
        in_specs=[pl.BlockSpec(memory_space=pltpu.SMEM)] + [anywhere] * 15,
        out_specs=[anywhere] * 5 + [vmem] * 5,
        out_shape=[
            shape(sets, rows, width), shape(sets, comp, width), shape(sets, comp, width),
            shape(count, width // PIECES, comp), shape(sets, rows, width, kind=f32),
            shape(eighth, wide // line * done, kind=f32), shape(tall * done, width // line, kind=f32),
            shape(eighth, width // line, kind=f32), shape(eighth, wide), shape(tall, width),
        ],
        scratch_shapes=scratch,
        compiler_params=params(collective_id=1, has_side_effects=True),
        name="back",
    )(set_kind, hidden, gup, act, gdown, output_part.reshape(2, 2, 2, eighth, width), e, go, mixed, q, kc, vc, gfirst, wq, wk, wv)


def attention_back_kernel(
    e_ref, go_ref, mixed_ref, q_ref, kc_ref, vc_ref, gfirst_ref, wq_ref, wk_ref, wv_ref,
    gq_ref, gk_ref, gv_ref, g_ref, gin_ref,
    gkt, gvt,
):
    width = q_ref.shape[2]
    comp = kc_ref.shape[1]
    half = lax.broadcasted_iota(jnp.int32, (comp, LANES), 1) < DH
    minus = head_blocks(jnp.full((comp, LANES), -1.0, bf16), half)
    refs = [ref.at[0] for ref in (e_ref, go_ref, mixed_ref, q_ref, kc_ref, vc_ref, gq_ref)]
    for pair in range(width // LANES):
        pair_back(pair, *refs, gkt, gvt, half, minus)
    g_ref[0] = (dot(wk_ref[...], gkt[...]) + dot(wv_ref[...], gvt[...])).astype(bf16)
    gk_ref[0] = gkt[...].T
    gv_ref[0] = gvt[...].T
    gin_ref[0] = gfirst_ref[0] + dot_nt(gq_ref[0], wq_ref[...])


def attention_back(e, go, mixed, q, kc, vc, gfirst, wq, wk, wv):
    sets, rows, width = q.shape
    comp = kc.shape[1]
    outs = [
        ((rows, width), bf16),
        ((comp, width), bf16),
        ((comp, width), bf16),
        ((width, comp), bf16),
        ((rows, width), f32),
    ]
    tokens = per_set((rows, width))
    short = per_set((comp, width))
    return pl.pallas_call(
        attention_back_kernel,
        grid=(sets,),
        in_specs=[per_set(e.shape[1:])] + [tokens] * 3 + [short] * 2 + [tokens]
        + [whole(w.shape) for w in (wq, wk, wv)],
        out_specs=[per_set(shape) for shape, _ in outs],
        out_shape=[jax.ShapeDtypeStruct((sets,) + shape, kind) for shape, kind in outs],
        scratch_shapes=[pltpu.VMEM((width, comp), bf16)] * 2,
        compiler_params=params(),
        name="attention_back",
    )(e, go, mixed, q, kc, vc, gfirst, wq, wk, wv)


def feed_grads_kernel(hidden_ref, gup_ref, act_ref, gdown_ref, up_out, down_out):
    up_out[...] = dot_tn(hidden_ref[...], gup_ref[...]).astype(bf16)
    down_out[...] = dot_tn(act_ref[...], gdown_ref[...]).astype(bf16)


def feed_grads(hidden, gup, act, gdown):
    tokens, width = hidden.shape
    units = gup.shape[1]
    chunk = 512
    return pl.pallas_call(
        feed_grads_kernel,
        grid=(units // chunk,),
        in_specs=[
            whole((tokens, width)),
            pl.BlockSpec((tokens, chunk), lambda i: (0, i)),
            pl.BlockSpec((tokens, chunk), lambda i: (0, i)),
            whole((tokens, width)),
        ],
        out_specs=[
            pl.BlockSpec((width, chunk), lambda i: (0, i)),
            pl.BlockSpec((chunk, width), lambda i: (i, 0)),
        ],
        out_shape=[jax.ShapeDtypeStruct((width, units), bf16), jax.ShapeDtypeStruct((units, width), bf16)],
        compiler_params=params(),
        name="feed_grads",
    )(hidden, gup, act, gdown)


def square_grad_kernel(left_ref, right_ref, out_ref):
    out_ref[...] = dot_tn(left_ref[...], right_ref[...]).astype(bf16)


def square_grad(left, right):
    count, width = left.shape
    return pl.pallas_call(
        square_grad_kernel,
        grid=(1,),
        in_specs=[whole((count, width)), whole((count, width))],
        out_specs=whole((width, width)),
        out_shape=jax.ShapeDtypeStruct((width, width), bf16),
        compiler_params=params(),
        name="square_grad",
    )(left, right)


def last_kernel(start_ref, table_ref, x_ref, g_ref, gin_ref, out_ref, compress_ref, total):
    step = pl.program_id(0)

    @pl.when(step == 0)
    def _():
        total[...] = jnp.zeros_like(total)

    rows = x_ref.shape[1]
    g = g_ref[0]
    out_ref[0] = gin_ref[0] + dot_nt(table_ref[0], g)
    terms = dot(x_ref[0], g)
    begin, shift = aligned(start_ref[step])
    padded = jnp.concatenate([terms, jnp.zeros((TILE, terms.shape[1]), f32)], axis=0)
    total[pl.ds(begin, rows + TILE), :] += pltpu.roll(padded, shift, 0)

    @pl.when(step == pl.num_programs(0) - 1)
    def _():
        compress_ref[...] = total[: compress_ref.shape[0], :]


def last(starts, table, x, g, gin, longest):
    sets, rows, width = x.shape
    comp = table.shape[2]
    tokens = per_set((rows, width))
    grid_spec = pltpu.PrefetchScalarGridSpec(
        num_scalar_prefetch=1,
        grid=(sets,),
        in_specs=[per_set((rows, comp)), tokens, per_set((width, comp)), tokens],
        out_specs=[tokens, whole((longest, comp))],
        scratch_shapes=[pltpu.VMEM((longest + TILE, comp), f32)],
    )
    return pl.pallas_call(
        last_kernel,
        grid_spec=grid_spec,
        out_shape=[
            jax.ShapeDtypeStruct((sets, rows, width), f32),
            jax.ShapeDtypeStruct((longest, comp), f32),
        ],
        compiler_params=params(),
        name="last",
    )(starts, table, x, g, gin)


def sequence_sum(part, is_long, row_count, shortest):
    seq_count = lax.axis_size("seq")
    total = lax.psum(part, "seq")
    span = shortest // row_count
    if span > 1:
        groups = [list(range(i, i + span)) for i in range(0, seq_count, span)]
        part = lax.psum(part, "seq", axis_index_groups=groups)
    return jnp.where(is_long[:, None, None], total, part)


def table_start(set_kind, row_offset, block_index, row_count, shortest):
    position = block_index * row_count
    member = position // shortest
    chosen = jnp.sum(jnp.where(jnp.arange(4)[None, :] == member, row_offset, 0), axis=1)
    return jnp.where(set_kind > 0, position, chosen + position % shortest)


def local(
    inputs, cotangent, set_kind, row_offset, query_w, key_w, value_w, output_w, up_w, down_w, compress,
    first_gain, first_bias, second_gain, second_bias,
):
    sets, rows, width = inputs.shape
    longest, comp = compress.shape
    shortest = longest // 4
    ranked = lax.axis_index("seq")
    tokens = sets * rows
    is_long = set_kind > 0
    starts = table_start(set_kind, row_offset, ranked, rows, shortest).astype(jnp.int32)
    norms = jnp.concatenate(
        [jnp.stack([first_gain, first_bias, second_gain, second_bias]), jnp.zeros((4, width), f32)], axis=0
    )
    linked = lax.axis_size("batch") == 8 and lax.axis_size("seq") == 4 and rows == shortest
    weights = (query_w, key_w, value_w, output_w, up_w, down_w)
    if linked:
        summed, line = jnp.zeros((1, 8, LANES), bf16), lax.axis_size("seq")
    else:
        table, part, _ = front(starts, compress, inputs, query_w)
        summed, line = sequence_sum(part, is_long, rows, shortest), 0
    (kc, vc, summed, mixed, hidden, layer_out, gdown, gfirst, go, new_table, queries, e, act, gup, output_part, norm_sums) = layer(
        starts, set_kind, compress, summed, inputs, cotangent, weights, norms, line
    )
    if linked:
        table = new_table
    flat = lambda v: v.reshape(-1, v.shape[-1])
    if linked:
        gq, gk, gv, g, gin, up_first, down_first, output_grad, up_rows, down_rows = back(
            set_kind, flat(hidden), flat(gup), flat(act), flat(gdown), output_part, e, go, mixed, queries, kc, vc, gfirst,
            query_w, key_w, value_w,
        )
        input_grad, compress_part = last(starts, table, inputs, g.reshape(sets, width, comp), gin, longest)
        compress_grad, norm_grads, up_last, down_last, query_grad, key_grad, value_grad = closing(
            compress_part, norm_sums, flat(inputs), flat(gq), flat(summed), flat(gk), flat(gv), up_rows, down_rows
        )
        up_grad = jnp.concatenate([up_first, up_last], axis=1)
        down_grad = jnp.concatenate([down_first, down_last], axis=0)
        weights = (query_grad, key_grad, value_grad, output_grad, up_grad, down_grad)
    else:
        up_part, down_part = feed_grads(flat(hidden), flat(gup), flat(act), flat(gdown))
        gq, gk, gv, g_part, gin = attention_back(
            e, go, mixed, queries, kc, vc, gfirst, query_w, key_w, value_w
        )
        g = sequence_sum(g_part, is_long, rows, shortest)
        query_part = square_grad(flat(inputs), flat(gq))
        key_part = square_grad(flat(summed), flat(gk))
        value_part = square_grad(flat(summed), flat(gv))
        input_grad, compress_part = last(starts, table, inputs, g, gin, longest)

        def scattered(v):
            v = lax.psum_scatter(v, "seq", scatter_dimension=1, tiled=True)
            return lax.psum_scatter(v, "batch", scatter_dimension=0, tiled=True).astype(f32)

        parts = (query_part, key_part, value_part, output_part, up_part, down_part)
        weights = tuple(scattered(v) for v in parts)
        compress_grad, norm_grads = lax.psum((compress_part, norm_sums), ("batch", "seq"))
    return (layer_out, input_grad) + weights + (compress_grad,) + tuple(norm_grads[i] for i in range(4))


def solution(mesh):
    tokens = P("batch", "seq", None)
    in_specs = (tokens, tokens, P("batch"), P("batch", None)) + (P(),) * 11
    out_specs = (tokens, tokens) + (P("batch", "seq"),) * 6 + (P(),) * 5
    return jax.shard_map(local, mesh=mesh, in_specs=in_specs, out_specs=out_specs, check_vma=False)
```

```python
import functools

import jax
import jax.numpy as jnp
from jax import lax
from jax.experimental import pallas as pl
from jax.experimental.pallas import tpu as pltpu
from jax.sharding import PartitionSpec as P

DH = 64
LANES = 128
TILE = 8
SCALE = DH ** (-0.5)
EPS = 1e-05
MESH = pl.DeviceIdType.MESH
VMEM_LIMIT = 63 * 1024 * 1024
bf16 = jnp.bfloat16
f32 = jnp.float32


def dot(left, right):
    return lax.dot_general(left, right, (((1,), (0,)), ((), ())), preferred_element_type=f32)


def dot_nt(left, right):
    return lax.dot_general(left, right, (((1,), (1,)), ((), ())), preferred_element_type=f32)


def dot_tn(left, right):
    return lax.dot_general(left, right, (((0,), (0,)), ((), ())), preferred_element_type=f32)


def params(**more):
    return pltpu.CompilerParams(vmem_limit_bytes=VMEM_LIMIT, **more)


def whole(shape):
    return pl.BlockSpec(shape, lambda *_: (0,) * len(shape), pipeline_mode=pl.Buffered(1))


def per_set(shape):
    return pl.BlockSpec((1,) + tuple(shape), lambda s, *_: (s,) + (0,) * len(shape))


def own_start(kinds, offsets, at, row_count, shortest):
    position = lax.axis_index("seq") * row_count
    return jnp.where(kinds[at] > 0, position, offsets[at, position // shortest] + position % shortest)


def aligned(start):
    begin = start // TILE * TILE
    return pl.multiple_of(begin, TILE), start - begin


def place():
    batch = lax.axis_index("batch")
    return batch // 4, batch // 2 % 2, batch % 2, lax.axis_index("seq")


def device(y, x, core, z):
    return ((y * 2 + x) * 2 + core, z)


def greet(others):
    barrier = pltpu.get_barrier_semaphore()
    for other in others:
        pl.semaphore_signal(barrier, inc=1, device_id=other, device_id_type=MESH)
    pl.semaphore_wait(barrier, len(others))


def remote(src, dst, send_sem, recv_sem, target):
    return pltpu.make_async_remote_copy(src, dst, send_sem, recv_sem, device_id=target, device_id_type=MESH)


class LineSum:
    def __init__(self, line, lag, own, from_left, from_right, sems):
        y, x, core, self.z = place()
        self.line, self.lag, self.own = line, lag, own
        self.right = device(y, x, core, (self.z + 1) % line)
        self.left = device(y, x, core, (self.z + line - 1) % line)
        inner, outer = self.z > 0, self.z < line - 1
        self.ways = (
            (from_left, self.right, inner, outer, sems[0], sems[1]),
            (from_right, self.left, outer, inner, sems[2], sems[3]),
        )

    def greet(self):
        barrier = pltpu.get_barrier_semaphore()
        for way in self.ways:

            @pl.when(way[3])
            def _():
                pl.semaphore_signal(barrier, inc=1, device_id=way[1], device_id_type=MESH)

        both = jnp.logical_and(self.z > 0, self.z < self.line - 1).astype(jnp.int32)
        pl.semaphore_wait(barrier, 1 + both)

    def prepare(self):
        for way in self.ways:

            @pl.when(jnp.logical_not(way[2]))
            def _():
                way[0][...] = jnp.zeros_like(way[0])

    def copy(self, way, at):
        held, target, _, _, send, recv = way
        return remote(held.at[at], held.at[at], send.at[at], recv.at[at], target)

    def forward(self, way, at):
        @pl.when(way[2])
        def _():
            self.copy(way, at).wait_recv()

        way[0][at] = way[0][at] + self.own[at]

        @pl.when(way[3])
        def _():
            self.copy(way, at).start()

    def slots(self):
        return self.own.shape[0] + self.lag * (self.line - 1)

    def serve(self, slot):
        for way, hops in zip(self.ways, (self.z, self.line - 1 - self.z)):
            at = slot - self.lag * hops

            @pl.when(jnp.logical_and(at >= 0, at < self.own.shape[0]))
            def _():
                self.forward(way, at)

    def serve_many(self, begin, count):
        def slot(at, carry):
            self.serve(at)
            return carry

        lax.fori_loop(begin, begin + count, slot, 0)

    def total(self, at, joined):
        own = self.own[at].astype(f32)
        both = self.ways[0][0][at].astype(f32) + self.ways[1][0][at].astype(f32)
        return jnp.where(joined, both - own, own).astype(bf16)

    def finish(self):
        for way in self.ways:

            @pl.when(way[3])
            def _():
                def wait(at, carry):
                    self.copy(way, at).wait_send()
                    return carry

                lax.fori_loop(0, self.own.shape[0], wait, 0)


class Scatter:
    def __init__(self, x_first, part, from_core, from_first, from_second, send, recv):
        y, x, core, z = place()
        self.part, self.recvs = part, (from_core, from_first, from_second)
        along_x, along_y = device(y, 1 - x, core, z), device(1 - y, x, core, z)
        self.core, self.x, self.y, self.x_first = core, x, y, x_first
        if x_first:
            sources = (part.at[:, :, 1 - core], from_core.at[:, 1 - x], from_first.at[1 - y])
            targets = (device(y, x, 1 - core, z), along_x, along_y)
        else:
            sources = (part.at[:, :, 1 - core], from_core.at[1 - y], from_first.at[1 - x])
            targets = (device(y, x, 1 - core, z), along_y, along_x)
        self.copies = [
            remote(sources[i], self.recvs[i], send.at[i], recv.at[i], targets[i]) for i in range(3)
        ]

    def start(self):
        self.copies[0].start()

    def first(self):
        self.copies[0].wait()
        self.recvs[0][...] = self.recvs[0][...] + self.part[:, :, self.core]
        self.copies[1].start()

    def second(self):
        self.copies[1].wait_recv()
        kept = self.recvs[0][:, self.x] if self.x_first else self.recvs[0][self.y]
        self.recvs[1][...] = self.recvs[1][...] + kept
        self.copies[2].start()

    def done(self):
        self.copies[2].wait_recv()
        kept = self.recvs[1][self.y] if self.x_first else self.recvs[1][self.x]
        return self.recvs[2][...].astype(f32) + kept.astype(f32)

    def finish(self):
        for copy in self.copies[1:]:
            copy.wait_send()


class LineScatter:
    def __init__(self, blocks, near, far, send, recv):
        y, x, core, z = place()
        self.blocks, self.near, self.far = blocks, near, far
        self.high, self.low = z // 2, z % 2
        self.copies = [
            remote(blocks.at[:, 1 - self.low], near, send.at[0], recv.at[0], device(y, x, core, z + 1 - 2 * self.low)),
            remote(near.at[1 - self.high], far, send.at[1], recv.at[1], device(y, x, core, (z + 2) % 4)),
        ]

    def start(self):
        self.copies[0].start()

    def middle(self):
        self.copies[0].wait_recv()
        self.near[...] = self.near[...] + self.blocks[:, self.low]
        self.copies[1].start()

    def done(self):
        self.copies[1].wait_recv()
        return self.near[self.high].astype(f32) + self.far[...].astype(f32)

    def finish(self):
        for copy in self.copies:
            copy.wait_send()


def line_scatter_blocks(blocks, rows, line):
    step = rows.shape[1] // line
    for z in range(line):
        mine = rows[:, z * step : (z + 1) * step]
        if step % LANES:
            top = rows.shape[0] // 2
            mine = jnp.concatenate([mine[:top], mine[top:]], axis=1)
        blocks[z // 2, z % 2] = mine.astype(bf16)


def unfold(total, out):
    if total.shape[1] == out.shape[1]:
        out[...] = total
    else:
        top, step = total.shape[0], out.shape[1]
        out[:top, :] = total[:, :step]
        out[top:, :] = total[:, step:]


def block_shape(rows, width, line):
    step = width // line
    return (rows, step) if step % LANES == 0 else (rows // 2, step * 2)


def scatter_scratch(rows, width):
    shapes = [(2, 2, rows, width), (2, rows, width), (rows, width)]
    return [pltpu.VMEM(shape, bf16) for shape in shapes] + [pltpu.SemaphoreType.DMA((3,))] * 2


def line_scratch(rows, width, line):
    block = block_shape(rows, width, line)
    return [pltpu.VMEM(n + block, bf16) for n in ((2, 2), (2,), ())] + [pltpu.SemaphoreType.DMA((2,))] * 2


class Neighbours:
    def __init__(self, line):
        y, x, core, z = place()
        self.core = device(y, x, 1 - core, z)
        places = [((y + dy) % 2, (x + dx) % 2) for dy, dx in ((0, 1), (1, 0), (1, 1))]
        self.plane = [(py * 2 + px, device(py, px, core, z)) for py, px in places]
        self.line = [((z + d) % line, device(y, x, core, (z + d) % line)) for d in range(1, line)]

    def everyone(self):
        return [self.core] + [to for _, to in self.plane] + [to for _, to in self.line]


class Total:
    counts = lambda line: (2, 6, 2 * (line - 1), line - 1, 3, 1)

    def __init__(self, line, near, table, norms, table_out, norms_out, mine, from_core, from_plane, from_line, gathered,
                 core_norms, plane_norms, line_norms, *sems):
        y, x, core, z = place()
        plane = y * 2 + x
        pairs = [(sems[2 * i], sems[2 * i + 1]) for i in range(6)]
        self.running = []

        def start(stage, moves):
            send, recv = pairs[stage]
            self.running = [remote(src, dst, send.at[i], recv.at[i], to) for i, (src, dst, to) in enumerate(moves)]
            for copy in self.running:
                copy.start()

        def to_core():
            mine[...] = table[...]
            core_norms[0] = norms[...]
            start(0, [(mine.at[1 - core], from_core, near.core), (core_norms.at[0], core_norms.at[1], near.core)])

        def to_plane():
            from_core[...] = from_core[...] + mine[core]
            plane_norms[plane] = core_norms[0] + core_norms[1]
            kept = plane_norms.at[plane]
            start(1, [(from_core.at[p], from_plane.at[i], to) for i, (p, to) in enumerate(near.plane)]
                  + [(kept, kept, to) for _, to in near.plane])

        def to_line():
            total = from_core[plane].astype(f32)
            for i in range(3):
                total = total + from_plane[i].astype(f32)
            mine[0, 0] = total.astype(bf16)
            line_norms[z] = plane_norms[0] + plane_norms[1] + plane_norms[2] + plane_norms[3]
            kept = line_norms.at[z]
            start(2, [(mine.at[0, 0, p], from_line.at[i], to) for i, (p, to) in enumerate(near.line)]
                  + [(kept, kept, to) for _, to in near.line])

        def back_line():
            total = mine[0, 0, z].astype(f32)
            for i in range(line - 1):
                total = total + from_line[i].astype(f32)
            gathered[core, plane, z] = total.astype(bf16)
            all_norms = line_norms[0]
            for i in range(1, line):
                all_norms = all_norms + line_norms[i]
            norms_out[...] = all_norms
            block = gathered.at[core, plane, z]
            start(3, [(block, block, to) for _, to in near.line])

        def back_plane():
            block = gathered.at[core, plane]
            start(4, [(block, block, to) for _, to in near.plane])

        def back_core():
            block = gathered.at[core]
            start(5, [(block, block, near.core)])

        def close():
            table_out[...] = gathered[...]

        self.stages = [to_core, to_plane, to_line, back_line, back_plane, back_core, close]

    def advance(self):
        for copy in self.running:
            copy.wait()
        self.running = []
        self.stages.pop(0)()

    @staticmethod
    def scratch(line, shape, norms):
        vmem = pltpu.VMEM
        return [
            vmem(shape, bf16), vmem(shape[1:], bf16), vmem((3,) + shape[2:], bf16), vmem((line - 1,) + shape[3:], bf16),
            vmem(shape, bf16), vmem((2,) + norms, f32), vmem((4,) + norms, f32), vmem((line,) + norms, f32),
        ] + [pltpu.SemaphoreType.DMA((n,)) for n in Total.counts(line) for _ in range(2)]


def closing_kernel(line, table_ref, norms_ref, x_any, gq_any, c_any, gk_any, gv_any, up_ref, down_ref, last_ref,
                   table_out, norms_out, up_out, down_out, query_out, key_out, value_out,
                   x, gq, c, gk, gv, load_sems, *scratch):
    scratch = list(scratch)
    take = lambda n: [scratch.pop(0) for _ in range(n)]
    pairs = ((x_any, x), (gq_any, gq), (c_any, c), (gk_any, gk), (gv_any, gv))
    loads = [pltpu.make_async_copy(src, dst, load_sems.at[i]) for i, (src, dst) in enumerate(pairs)]
    for load in loads:
        load.start()
    near = Neighbours(line)
    greet(near.everyone())
    total = Total(line, near, table_ref, norms_ref, table_out, norms_out, *take(8 + 12))
    total.advance()
    down_job, down_line = Scatter(False, last_ref, *take(5)), LineScatter(*take(5))
    down_job.start()
    across = []
    for rows, out in [(up_ref, up_out), (down_ref, down_out)]:
        for chunk in range(rows.shape[0]):
            job = LineScatter(*take(5))
            line_scatter_blocks(job.blocks, rows[chunk], line)
            job.start()
            across.append((job, out.at[chunk]))
    total.advance()
    down_job.first()
    jobs = []
    for i, (left, right) in enumerate(((x, gq), (c, gk), (c, gv))):
        part = take(1)[0]
        jobs.append((Scatter(i % 2 == 0, part, *take(5)), LineScatter(*take(5)), (query_out, key_out, value_out)[i]))
        for load in ((loads[0], loads[1]), (loads[2], loads[3]), (loads[4],))[i]:
            load.wait()
        part[...] = dot_tn(left[...], right[...]).astype(bf16).reshape(part.shape)
        jobs[i][0].start()
        if i > 0:
            jobs[i - 1][0].first()
    for job, _ in across:
        job.middle()
    total.advance()
    jobs[2][0].first()
    down_job.second()
    total.advance()
    jobs[0][0].second()
    for job, out in across:
        unfold(job.done(), out)
    total.advance()
    jobs[1][0].second()
    jobs[2][0].second()
    jobs.append((down_job, down_line, down_out.at[down_ref.shape[0]]))
    line_scatter_blocks(down_line.blocks, down_job.done(), line)
    down_line.start()
    total.advance()
    for job, line_job, _ in jobs[:3]:
        line_scatter_blocks(line_job.blocks, job.done(), line)
        line_job.start()
    total.advance()
    for _, line_job, _ in jobs:
        line_job.middle()
    for _, line_job, out in jobs:
        unfold(line_job.done(), out)
    for job, _ in across:
        job.finish()
    for job, line_job, _ in jobs:
        job.finish()
        line_job.finish()


def closing(table, norms, x, gq, c, gk, gv, up_rows, down_rows, down_last):
    line = lax.axis_size("seq")
    longest, comp = table.shape
    width = x.shape[1]
    shape = (2, 4, line, longest // (8 * line), comp)
    rows = width // 8
    vmem, anywhere = pl.BlockSpec(memory_space=pltpu.VMEM), pl.BlockSpec(memory_space=pl.ANY)
    out = lambda *dims: jax.ShapeDtypeStruct(dims, f32)
    (ups, _, wide), (downs, tall, _) = up_rows.shape, down_rows.shape
    scratch = [pltpu.VMEM(v.shape, bf16) for v in (x, gq, c, gk, gv)] + [pltpu.SemaphoreType.DMA((5,))]
    scratch += Total.scratch(line, shape, norms.shape)
    scratch += scatter_scratch(tall, width) + line_scratch(tall, width, line)
    for _ in range(ups):
        scratch += line_scratch(rows, wide, line)
    for _ in range(downs):
        scratch += line_scratch(tall, width, line)
    for _ in range(3):
        scratch += [pltpu.VMEM((2, 2, 2, rows, width), bf16)] + scatter_scratch(rows, width) + line_scratch(rows, width, line)
    table_out, *rest = pl.pallas_call(
        functools.partial(closing_kernel, line),
        in_specs=[vmem] * 2 + [anywhere] * 5 + [vmem] * 3,
        out_specs=[vmem] * 7,
        out_shape=[jax.ShapeDtypeStruct(shape, bf16), out(*norms.shape), out(ups, rows, wide // line), out(downs + 1, tall, width // line)]
        + [out(rows, width // line)] * 3,
        scratch_shapes=scratch,
        compiler_params=params(collective_id=3, has_side_effects=True),
        name="closing",
    )(table.reshape(shape), norms, x, gq, c, gk, gv, up_rows, down_rows, down_last)
    return [table_out] + rest


def front_kernel(start_ref, compress_ref, x_ref, wq_ref, table_ref, c_ref, q_ref, wide):
    step = pl.program_id(0)

    longest = compress_ref.shape[0]

    @pl.when(step == 0)
    def _():
        wide[:longest, :] = compress_ref[...].astype(f32)
        wide[longest:, :] = jnp.zeros((TILE, wide.shape[1]), f32)

    rows = x_ref.shape[1]
    begin, shift = aligned(start_ref[step])
    window = wide[pl.ds(begin, rows + TILE), :]
    table = pltpu.roll(window, lax.rem(rows + TILE - shift, rows + TILE), 0)[:rows].astype(bf16)
    table_ref[0] = table
    x = x_ref[0]
    c_ref[0] = dot_tn(table, x).astype(bf16)
    q_ref[0] = (dot(x, wq_ref[...]) * SCALE).astype(bf16)


def front(starts, compress, x, wq):
    sets, rows, width = x.shape
    longest, comp = compress.shape
    grid_spec = pltpu.PrefetchScalarGridSpec(
        num_scalar_prefetch=1,
        grid=(sets,),
        in_specs=[whole(compress.shape), per_set((rows, width)), whole(wq.shape)],
        out_specs=[per_set((rows, comp)), per_set((comp, width)), per_set((rows, width))],
        scratch_shapes=[pltpu.VMEM((longest + TILE, comp), f32)],
    )
    return pl.pallas_call(
        front_kernel,
        grid_spec=grid_spec,
        out_shape=[
            jax.ShapeDtypeStruct((sets, rows, comp), bf16),
            jax.ShapeDtypeStruct((sets, comp, width), bf16),
            jax.ShapeDtypeStruct((sets, rows, width), bf16),
        ],
        compiler_params=params(),
        name="front",
    )(starts, compress, x, wq)


def head_blocks(pair, first_half):
    zero = jnp.zeros_like(pair)
    return jnp.concatenate([jnp.where(first_half, pair, zero), jnp.where(first_half, zero, pair)], axis=0)


def norm_forward(v):
    average = jnp.mean(v, axis=-1, keepdims=True)
    centered = v - average
    variance = jnp.mean(centered * centered, axis=-1, keepdims=True)
    inverse = lax.rsqrt(variance + EPS)
    return centered * inverse, inverse


def norm_backward(dz, z, inverse):
    return (dz - jnp.mean(dz, axis=-1, keepdims=True) - z * jnp.mean(dz * z, axis=-1, keepdims=True)) * inverse


PIECES = 4
LAG = 2
HALVES = 2


def layer_kernel(
    line, long_ref, offset_ref, compress_ref, c_ref, x_any, cot_ref, gain1_ref, bias1_ref, gain2_ref, bias2_ref, wq_any, wk_any, wv_any, wo_any, up_any, down_any,
    kc_ref, vc_ref, csum_ref, mixed_ref, hidden_ref, out_ref, gdown_ref, gatt_ref, go_ref, table_any, q_any,
    e_any, act_any, gup_any, output_grad_ref, sums_ref,
    xs, qs, wq, wk, wv, wo, up, down, e_buf, act, gup, z_first, rinv_ref, held, output_grad, weight_sems, x_sems, out_sems,
    *linked,
):
    step = pl.program_id(0)
    last = pl.num_programs(0) - 1
    sets, rows, width = xs.shape
    comp = kc_ref.shape[1]
    units = up.shape[1]
    chunk = 768
    loads = [
        pltpu.make_async_copy(src, dst, weight_sems.at[i])
        for i, (src, dst) in enumerate(
            ((wq_any, wq), (wk_any, wk), (wv_any, wv), (wo_any, wo), (up_any, up), (down_any, down))
        )
    ]
    x_loads = [pltpu.make_async_copy(x_any.at[s], xs.at[s], x_sems.at[s]) for s in range(sets)]
    q_store = pltpu.make_async_copy(qs, q_any, out_sems.at[3])
    e_store = pltpu.make_async_copy(e_buf, e_any.at[step], out_sems.at[0])
    act_store = pltpu.make_async_copy(act, act_any.at[step], out_sems.at[1])
    gup_store = pltpu.make_async_copy(gup, gup_any.at[step], out_sems.at[2])

    if line:
        tables, own, from_left, from_right, table_sems, *sems = linked
        sums = LineSum(line, LAG, own, from_left, from_right, sems)
        ahead = PIECES + LAG * (line - 1)
        t_stores = [pltpu.make_async_copy(tables.at[s], table_any.at[s], table_sems.at[s]) for s in range(sets)]

    def first_use(load):
        @pl.when(step == 0)
        def _():
            load.wait()

    @pl.when(step == 0)
    def _():
        for load in x_loads:
            load.start()
        sums_ref[...] = jnp.zeros_like(sums_ref)
        output_grad[...] = jnp.zeros_like(output_grad)
        if line:
            longest = compress_ref.shape[0]
            sums.greet()
            sums.prepare()
            grid = (rows, rows)
            ahead_by = lax.broadcasted_iota(jnp.int32, grid, 1) - lax.broadcasted_iota(jnp.int32, grid, 0)
        slot = 0
        for s in range(sets):
            x_loads[s].wait()
            if s == 0:
                loads[0].start()
            if line:
                table = jnp.zeros((rows, comp), f32)
                start = own_start(long_ref, offset_ref, s, rows, longest // 4)
                for at in range(0, longest, rows):
                    chosen = jnp.where(ahead_by == start - at, 1.0, 0.0).astype(bf16)
                    table = table + dot(chosen, compress_ref[at : at + rows, :])
                table = table.astype(bf16)
                tables[s] = table
                t_stores[s].start()
                own[s * PIECES : (s + 1) * PIECES] = (
                    dot_tn(table, xs[s]).astype(bf16).reshape(PIECES, comp // PIECES, width)
                )
                sums.serve(slot)
                slot += 1
        for load in loads[1:]:
            load.start()
        loads[0].wait()
        for s in range(sets):
            qs[s] = (dot(xs[s], wq[...]) * SCALE).astype(bf16)
            if line:
                sums.serve(slot)
                slot += 1
        q_store.start()
        if line:
            sums.serve_many(slot, ahead - slot)

    def serve(part):
        if line:
            count = PIECES // 4

            @pl.when(step < last)
            def _():
                sums.serve_many(ahead + step * PIECES + part * count, count)

    if line:
        joined = long_ref[step] > 0
        for piece in range(PIECES):
            size = comp // PIECES
            csum_ref[0, piece * size : (piece + 1) * size, :] = sums.total(step * PIECES + piece, joined)
    else:
        csum_ref[0] = c_ref[0]
    first_use(loads[1])
    first_use(loads[2])
    c = csum_ref[0]
    kc_ref[0] = dot(c, wk[...]).astype(bf16)
    vc_ref[0] = dot(c, wv[...]).astype(bf16)
    half = lax.broadcasted_iota(jnp.int32, (comp, LANES), 1) < DH
    ones = head_blocks(jnp.ones((comp, LANES), bf16), half)

    @pl.when(step > 0)
    def _():
        e_store.wait()

    for pair in range(width // LANES):
        lanes = pl.ds(pair * LANES, LANES)
        keys = head_blocks(kc_ref[0, :, lanes], half)
        values = jnp.concatenate([head_blocks(vc_ref[0, :, lanes], half), ones], axis=1)
        scores = dot_nt(qs[step, :, lanes], keys)
        parts = []
        for head in range(2):
            mine = scores[:, head * comp : (head + 1) * comp]
            top = jnp.max(mine, axis=-1, keepdims=True)
            parts.append(jnp.exp(mine - top).astype(bf16))
        e = jnp.concatenate(parts, axis=1)
        e_buf[:, pl.ds(pair * 2 * comp, 2 * comp)] = e
        total = dot(e, values)
        rinv = 1.0 / total[:, LANES:]
        rinv_ref[:, lanes] = rinv
        mixed_ref[0, :, lanes] = (total[:, :LANES] * rinv).astype(bf16)
    e_store.start()
    first_use(loads[3])
    serve(0)
    gain1, bias1, gain2, bias2 = (ref[...].reshape(1, width) for ref in (gain1_ref, bias1_ref, gain2_ref, bias2_ref))
    size = rows // HALVES
    halves = [pl.ds(h * size, size) for h in range(HALVES)]
    inverse1 = []
    for part in halves:
        z1, inv1 = norm_forward(xs[step, part, :].astype(f32) + dot(mixed_ref[0, part, :], wo[...]))
        inverse1.append(inv1)
        z_first[part, :] = z1
        hidden = z1 * gain1 + bias1
        hidden_ref[0, part, :] = hidden.astype(bf16)
        held[part, :] = hidden
    first_use(loads[4])
    first_use(loads[5])

    @pl.when(step > 0)
    def _():
        act_store.wait()
        gup_store.wait()

    for part in halves:
        hidden_low = hidden_ref[0, part, :]
        for at in range(0, units, chunk):
            span = pl.ds(at, chunk)
            upward = dot(hidden_low, up[:, span])
            cdf = 0.5 + 0.5 * lax.erf(upward * (0.5**0.5))
            density = jnp.exp(upward * upward * -0.5) * 0.3989422804014327
            act[part, span] = (upward * cdf).astype(bf16)
            gup[part, span] = (cdf + upward * density).astype(bf16)
    act_store.start()
    serve(1)
    sums2 = []
    for part in halves:
        z2, inv2 = norm_forward(held[part, :] + dot(act[part, :], down[...]))
        out_ref[0, part, :] = (z2 * gain2 + bias2).astype(bf16)
        dy = cot_ref[0, part, :].astype(f32)
        gsecond = norm_backward(dy * gain2, z2, inv2)
        sums2.append((jnp.sum(dy * z2, axis=0, keepdims=True), jnp.sum(dy, axis=0, keepdims=True)))
        gdown_ref[0, part, :] = gsecond.astype(bf16)
        held[part, :] = gsecond
    for part in halves:
        gdown = gdown_ref[0, part, :]
        for at in range(0, units, chunk):
            span = pl.ds(at, chunk)
            gact = dot_nt(gdown, down[span, :])
            gup[part, span] = (gact * gup[part, span].astype(f32)).astype(bf16)
    gup_store.start()
    serve(2)
    sums1 = []
    for part, inv1 in zip(halves, inverse1):
        ghidden = held[part, :] + dot_nt(gup[part, :], up[...])
        z1 = z_first[part, :]
        sums1.append((jnp.sum(ghidden * z1, axis=0, keepdims=True), jnp.sum(ghidden, axis=0, keepdims=True)))
        gatt_ref[0, part, :] = norm_backward(ghidden * gain1, z1, inv1).astype(bf16)
    for part in halves:
        go_ref[0, part, :] = (dot_nt(gatt_ref[0, part, :], wo[...]) * rinv_ref[part, :]).astype(bf16)
    output_grad[...] += dot_tn(mixed_ref[0], gatt_ref[0])
    for i, pieces in enumerate((sums1, sums2)):
        for j in range(2):
            sums_ref[2 * i + j : 2 * i + j + 1, :] += sum(piece[j] for piece in pieces)
    serve(3)

    @pl.when(step == last)
    def _():
        output_grad_ref[...] = output_grad[...].astype(bf16)
        e_store.wait()
        act_store.wait()
        gup_store.wait()
        q_store.wait()
        if line:
            for store in t_stores:
                store.wait()
            sums.finish()


def layer(set_kind, row_offset, compress, c, x, cot, weights, norms, line):
    sets, rows, width = x.shape
    longest, comp = compress.shape
    wq, wk, wv, wo, up, down = weights
    units = up.shape[1]
    tokens = per_set((rows, width))
    short = per_set((comp, width))
    anywhere = pl.BlockSpec(memory_space=pl.ANY)
    smem = pl.BlockSpec(memory_space=pltpu.SMEM)
    shape = lambda *dims, kind=bf16: jax.ShapeDtypeStruct(dims, kind)
    dma = lambda n: pltpu.SemaphoreType.DMA((n,))
    linked = []
    if line:
        count = sets * PIECES
        linked = [pltpu.VMEM((sets, rows, comp), bf16)]
        linked += [pltpu.VMEM((count, comp // PIECES, width), bf16)] * 3 + [dma(sets)] + [dma(count)] * 4
    more = dict(collective_id=0, has_side_effects=True) if line else {}
    return pl.pallas_call(
        functools.partial(layer_kernel, line),
        grid=(sets,),
        in_specs=[smem, smem, whole(compress.shape), anywhere if line else short, anywhere, tokens]
        + [whole((width,))] * 4
        + [anywhere] * 6,
        out_specs=[short] * 3 + [tokens] * 6 + [anywhere] * 5 + [whole((width, width)), whole((8, width))],
        out_shape=[shape(sets, comp, width)] * 3
        + [shape(sets, rows, width)] * 6
        + [shape(sets, rows, comp), shape(sets, rows, width)]
        + [shape(sets, rows, width // DH * comp)]
        + [shape(sets, rows, units)] * 2
        + [shape(width, width), shape(8, width, kind=f32)],
        scratch_shapes=[pltpu.VMEM(x.shape, bf16)] * 2
        + [pltpu.VMEM(w.shape, bf16) for w in weights]
        + [pltpu.VMEM((rows, width // DH * comp), bf16)]
        + [pltpu.VMEM((rows, units), bf16)] * 2
        + [pltpu.VMEM((rows, width), f32)] * 3
        + [pltpu.VMEM((width, width), f32), dma(6), dma(sets), dma(4)]
        + linked,
        compiler_params=params(**more),
        name="layer",
    )(set_kind, row_offset, compress, c, x, cot, *norms, *weights)


def pair_back(pair, e_ref, go_ref, mixed_ref, q_ref, kc_ref, vc_ref, gq_ref, gkt, gvt, half, minus):
    comp = kc_ref.shape[0]
    lanes = pl.ds(pair * LANES, LANES)
    e = e_ref[:, pl.ds(pair * 2 * comp, 2 * comp)]
    keys = head_blocks(kc_ref[:, lanes], half)
    values = jnp.concatenate([head_blocks(vc_ref[:, lanes], half), minus], axis=1)
    go = go_ref[:, lanes]
    delta = (go.astype(f32) * mixed_ref[:, lanes].astype(f32)).astype(bf16)
    gp = dot_nt(jnp.concatenate([go, delta], axis=1), values)
    gs = (gp * e.astype(f32)).astype(bf16)
    gq_ref[:, lanes] = (dot(gs, keys) * SCALE).astype(bf16)
    for into, left, right in ((gkt, q_ref[:, lanes], gs), (gvt, go, e)):
        both = dot_tn(left, right)
        at = pair * LANES
        into[at : at + DH, :] = both[:DH, :comp].astype(bf16)
        into[at + DH : at + LANES, :] = both[DH:, comp:].astype(bf16)


CHUNKS = 3
HERE = 1
BACK_PIECES = 4
BACK_LAG = 2


def back_kernel(
    line, long_ref, hidden_any, gup_any, act_any, gdown_any, output_any, e_any, go_any, mixed_any, q_any, kc_any, vc_any, wk_any, wv_any,
    gq_any, gk_any, gv_any, g_any, output_out, up_out, down_out, up_rows, down_rows, down_last,
    hidden, gdown, feed, wk, wv, e, go, mixed, q, kc, vc, gq, gkt, gvt, gk, gv, own, from_left, from_right,
    up_part, down_part, output_part, load_sems, feed_sems, set_sems, out_sems, g_sem, *scratch,
):
    scratch = list(scratch)
    take = lambda n: [scratch.pop(0) for _ in range(n)]
    sets, rows, width = q_any.shape
    comp = kc_any.shape[1]
    units = gup_any.shape[1]
    sums = LineSum(line, BACK_LAG, own, from_left, from_right, take(4))

    def copies(pairs, sems):
        return [pltpu.make_async_copy(src, dst, sems.at[i]) for i, (src, dst) in enumerate(pairs)]

    def feed_loads(chunk, which):
        if which == 0:
            wide, count, source = units // line, line, gup_any
        else:
            wide, count, source = units // 8, 8, act_any
        step = wide // CHUNKS
        return copies(
            [(source.at[:, pl.ds(i * wide + chunk * step, step)], feed.at[which, :, pl.ds(i * step, step)]) for i in range(count)],
            feed_sems.at[which],
        )

    def set_loads(s):
        at = s % 2
        return copies(
            [(e_any.at[s], e.at[at]), (go_any.at[s], go.at[at]), (mixed_any.at[s], mixed.at[at]), (q_any.at[s], q.at[at]),
             (kc_any.at[s], kc.at[at]), (vc_any.at[s], vc.at[at])],
            set_sems.at[at],
        )

    def set_stores(s):
        at = s % 2
        return copies([(gq.at[at], gq_any.at[s]), (gk.at[at], gk_any.at[s]), (gv.at[at], gv_any.at[s])], out_sems.at[at])

    def begin(some):
        for copy in some:
            copy.start()

    def end(some):
        for copy in some:
            copy.wait()

    weights = copies(((output_any, output_part), (hidden_any, hidden), (gdown_any, gdown), (wk_any, wk), (wv_any, wv)), load_sems)
    begin(weights[:1])
    begin(set_loads(0))
    begin(weights[3:])
    near = Neighbours(line)
    greet(near.everyone())
    sums.prepare()

    jobs = {"o": (Scatter(True, output_part, *take(5)), LineScatter(*take(5)), output_out)}
    for chunk in range(CHUNKS):
        for which, part in ((0, up_part), (1, down_part)):
            job = Scatter(which == 0, part.at[chunk % 2], *take(5))
            if chunk < HERE:
                jobs[which, chunk] = (job, LineScatter(*take(5)), (up_out, down_out)[which])
            elif (which, chunk) != (1, CHUNKS - 1):
                jobs[which, chunk] = (job, None, (up_rows, down_rows)[which].at[chunk - HERE])
            else:
                jobs[which, chunk] = (job, None, None)

    def across(name):
        job, line_job, _ = jobs[name]
        line_scatter_blocks(line_job.blocks, job.done(), line)
        line_job.start()

    def feed_grad(chunk, which, then):
        end(feed_loads(chunk, which))
        if chunk == 0:
            weights[1 + which].wait()
        for some in then:
            begin(some)
        if which == 0:
            grad = dot_tn(hidden[...], feed[0])
        else:
            grad = dot_tn(feed[1], gdown[...])
        if jobs[which, chunk][2] is None:
            down_last[...] = grad.astype(bf16).reshape(down_last.shape)
            return
        part = (up_part, down_part)[which]
        part[chunk % 2] = grad.astype(bf16).reshape(part.shape[1:])
        jobs[which, chunk][0].start()

    half = lax.broadcasted_iota(jnp.int32, (comp, LANES), 1) < DH
    minus = head_blocks(jnp.full((comp, LANES), -1.0, bf16), half)

    def heads(s, then=()):
        at = s % 2
        end(set_loads(s))
        if s > 1:
            end(set_stores(s - 2))
        for some in then:
            begin(some)
        for pair in range(width // LANES):
            pair_back(pair, e.at[at], go.at[at], mixed.at[at], q.at[at], kc.at[at], vc.at[at], gq.at[at], gkt, gvt, half, minus)

    def joins(s):
        if s == 0:
            end(weights[3:])
        g = dot(wk[...], gkt[...]) + dot(wv[...], gvt[...])
        own[s * BACK_PIECES : (s + 1) * BACK_PIECES] = g.astype(bf16).reshape(BACK_PIECES, width // BACK_PIECES, comp)
        gk[s % 2] = gkt[...].T
        gv[s % 2] = gvt[...].T
        begin(set_stores(s))

    slots = iter(range(sums.slots()))

    def serve(count):
        first = next(slots)
        for _ in range(count - 1):
            next(slots)
        sums.serve_many(first, count)

    o, (u0, u1, u2), (d0, d1, d2) = jobs["o"][0], [jobs[0, i][0] for i in range(3)], [jobs[1, i][0] for i in range(3)]
    weights[0].wait()
    o.start()
    heads(0, [weights[1:2], feed_loads(0, 0)])
    o.first()
    joins(0)
    serve(2)
    feed_grad(0, 0, [set_loads(1)])
    serve(2)
    heads(1, [weights[2:3], feed_loads(0, 1)])
    u0.first()
    o.second()
    joins(1)
    serve(2)
    feed_grad(0, 1, [feed_loads(1, 0), set_loads(2)])
    serve(2)
    feed_grad(1, 0, [feed_loads(1, 1)])
    d0.first()
    u0.second()
    heads(2, [set_loads(3)])
    u1.first()
    joins(2)
    serve(2)
    feed_grad(1, 1, [feed_loads(2, 0)])
    d0.second()
    serve(2)
    heads(3, [feed_loads(2, 1)])
    d1.first()
    joins(3)
    serve(2)
    feed_grad(2, 0, [])
    u1.second()
    serve(2)
    feed_grad(2, 1, [])
    u2.first()
    d1.second()
    serve(6)
    for name in ("o", (0, 0), (1, 0)):
        across(name)
    u2.second()
    for name in ("o", (0, 0), (1, 0)):
        jobs[name][1].middle()
    for s in range(sets):
        for piece in range(s * BACK_PIECES, (s + 1) * BACK_PIECES):
            own[piece] = sums.total(piece, long_ref[s] > 0)
    g_store = pltpu.make_async_copy(own, g_any, g_sem.at[0])
    g_store.start()
    for name in jobs:
        job, line_job, out = jobs[name]
        if line_job is not None:
            unfold(line_job.done(), out)
        elif out is not None:
            out[...] = job.done().astype(bf16)
    for name in jobs:
        job, line_job, out = jobs[name]
        if out is None:
            continue
        job.finish()
        if line_job is not None:
            line_job.finish()
    for s in range(sets - 2, sets):
        end(set_stores(s))
    g_store.wait()
    sums.finish()


def back(set_kind, hidden, gup, act, gdown, output_part, e, go, mixed, q, kc, vc, wk, wv):
    line = lax.axis_size("seq")
    sets, rows, width = q.shape
    comp = kc.shape[1]
    tokens, units = gup.shape
    eighth = width // 8
    wide, tall = units // CHUNKS, units // 8 // CHUNKS
    count = sets * BACK_PIECES
    dma = lambda *n: pltpu.SemaphoreType.DMA(n)
    vmem, anywhere = pl.BlockSpec(memory_space=pltpu.VMEM), pl.BlockSpec(memory_space=pl.ANY)
    shape = lambda *dims, kind=bf16: jax.ShapeDtypeStruct(dims, kind)
    buffer = lambda *dims, kind=bf16: pltpu.VMEM(dims, kind)
    scratch = [buffer(tokens, width)] * 2 + [buffer(2, tokens, wide)] + [buffer(width, width)] * 2
    scratch += [buffer(2, rows, e.shape[2])] + [buffer(2, rows, width)] * 3 + [buffer(2, comp, width)] * 2
    scratch += [buffer(2, rows, width)] + [buffer(width, comp)] * 2 + [buffer(2, comp, width)] * 2
    scratch += [buffer(count, width // BACK_PIECES, comp)] * 3
    scratch += [buffer(2, 2, 2, 2, eighth, wide), buffer(2, 2, 2, 2, tall, width), buffer(2, 2, 2, eighth, width)]
    scratch += [dma(5), dma(2, 8), dma(2, 6), dma(2, 3), dma(1)] + [dma(count)] * 4
    scratch += scatter_scratch(eighth, width) + line_scratch(eighth, width, line)
    for chunk in range(CHUNKS):
        for size in ((eighth, wide), (tall, width)):
            scratch += scatter_scratch(*size)
            if chunk < HERE:
                scratch += line_scratch(*size, line)
    return pl.pallas_call(
        functools.partial(back_kernel, line),
        in_specs=[pl.BlockSpec(memory_space=pltpu.SMEM)] + [anywhere] * 13,
        out_specs=[anywhere] * 4 + [vmem] * 6,
        out_shape=[
            shape(sets, rows, width), shape(sets, comp, width), shape(sets, comp, width),
            shape(count, width // BACK_PIECES, comp),
            shape(eighth, width // line, kind=f32),
            shape(eighth, wide // line * HERE, kind=f32), shape(tall * HERE, width // line, kind=f32),
            shape(CHUNKS - HERE, eighth, wide), shape(CHUNKS - HERE - 1, tall, width), shape(2, 2, 2, tall, width),
        ],
        scratch_shapes=scratch,
        compiler_params=params(collective_id=1, has_side_effects=True),
        name="back",
    )(set_kind, hidden, gup, act, gdown, output_part.reshape(2, 2, 2, eighth, width), e, go, mixed, q, kc, vc, wk, wv)


def attention_back_kernel(
    e_ref, go_ref, mixed_ref, q_ref, kc_ref, vc_ref, wk_ref, wv_ref,
    gq_ref, gk_ref, gv_ref, g_ref,
    gkt, gvt,
):
    width = q_ref.shape[2]
    comp = kc_ref.shape[1]
    half = lax.broadcasted_iota(jnp.int32, (comp, LANES), 1) < DH
    minus = head_blocks(jnp.full((comp, LANES), -1.0, bf16), half)
    refs = [ref.at[0] for ref in (e_ref, go_ref, mixed_ref, q_ref, kc_ref, vc_ref, gq_ref)]
    for pair in range(width // LANES):
        pair_back(pair, *refs, gkt, gvt, half, minus)
    g_ref[0] = (dot(wk_ref[...], gkt[...]) + dot(wv_ref[...], gvt[...])).astype(bf16)
    gk_ref[0] = gkt[...].T
    gv_ref[0] = gvt[...].T


def attention_back(e, go, mixed, q, kc, vc, wk, wv):
    sets, rows, width = q.shape
    comp = kc.shape[1]
    outs = [
        ((rows, width), bf16),
        ((comp, width), bf16),
        ((comp, width), bf16),
        ((width, comp), bf16),
    ]
    tokens = per_set((rows, width))
    short = per_set((comp, width))
    return pl.pallas_call(
        attention_back_kernel,
        grid=(sets,),
        in_specs=[per_set(e.shape[1:])] + [tokens] * 3 + [short] * 2
        + [whole(w.shape) for w in (wk, wv)],
        out_specs=[per_set(shape) for shape, _ in outs],
        out_shape=[jax.ShapeDtypeStruct((sets,) + shape, kind) for shape, kind in outs],
        scratch_shapes=[pltpu.VMEM((width, comp), bf16)] * 2,
        compiler_params=params(),
        name="attention_back",
    )(e, go, mixed, q, kc, vc, wk, wv)


def feed_grads_kernel(hidden_ref, gup_ref, act_ref, gdown_ref, up_out, down_out):
    up_out[...] = dot_tn(hidden_ref[...], gup_ref[...]).astype(bf16)
    down_out[...] = dot_tn(act_ref[...], gdown_ref[...]).astype(bf16)


def feed_grads(hidden, gup, act, gdown):
    tokens, width = hidden.shape
    units = gup.shape[1]
    chunk = 512
    return pl.pallas_call(
        feed_grads_kernel,
        grid=(units // chunk,),
        in_specs=[
            whole((tokens, width)),
            pl.BlockSpec((tokens, chunk), lambda i: (0, i)),
            pl.BlockSpec((tokens, chunk), lambda i: (0, i)),
            whole((tokens, width)),
        ],
        out_specs=[
            pl.BlockSpec((width, chunk), lambda i: (0, i)),
            pl.BlockSpec((chunk, width), lambda i: (i, 0)),
        ],
        out_shape=[jax.ShapeDtypeStruct((width, units), bf16), jax.ShapeDtypeStruct((units, width), bf16)],
        compiler_params=params(),
        name="feed_grads",
    )(hidden, gup, act, gdown)


def square_grad_kernel(left_ref, right_ref, out_ref):
    out_ref[...] = dot_tn(left_ref[...], right_ref[...]).astype(bf16)


def square_grad(left, right):
    count, width = left.shape
    return pl.pallas_call(
        square_grad_kernel,
        grid=(1,),
        in_specs=[whole((count, width)), whole((count, width))],
        out_specs=whole((width, width)),
        out_shape=jax.ShapeDtypeStruct((width, width), bf16),
        compiler_params=params(),
        name="square_grad",
    )(left, right)


def last_kernel(kind_ref, offset_ref, table_any, x_any, g_any, gfirst_any, gq_any, wq_any, out_any, compress_ref,
                table, x, g, gfirst, gq, wq, out, total, load_sems, weight_sem, out_sems):
    sets, rows, _ = x.shape
    longest = compress_ref.shape[0]
    pairs = ((g_any, g), (x_any, x), (gq_any, gq), (table_any, table), (gfirst_any, gfirst))
    loads = [[pltpu.make_async_copy(src.at[s], dst.at[s], load_sems.at[s, i]) for i, (src, dst) in enumerate(pairs)] for s in range(sets)]
    stores = [pltpu.make_async_copy(out.at[s], out_any.at[s], out_sems.at[s]) for s in range(sets)]
    weight = pltpu.make_async_copy(wq_any, wq, weight_sem.at[0])
    for load in loads[0]:
        load.start()
    weight.start()
    for s in range(1, sets):
        for load in loads[s]:
            load.start()
    total[...] = jnp.zeros_like(total)
    for s in range(sets):
        for load in loads[s]:
            load.wait()
        if s == 0:
            weight.wait()
        out[s] = gfirst[s].astype(f32) + (dot_nt(table[s], g[s]) + dot_nt(gq[s], wq[...]))
        stores[s].start()
        terms = dot(x[s], g[s])
        begin, shift = aligned(own_start(kind_ref, offset_ref, s, rows, longest // 4))
        padded = jnp.concatenate([terms, jnp.zeros((TILE, terms.shape[1]), f32)], axis=0)
        total[pl.ds(begin, rows + TILE), :] += pltpu.roll(padded, shift, 0)
    compress_ref[...] = total[:longest, :].astype(compress_ref.dtype)
    for store in stores:
        store.wait()


def last(kinds, offsets, table, x, g, gfirst, gq, wq, longest, kind):
    sets, rows, width = x.shape
    comp = table.shape[2]
    anywhere, smem = pl.BlockSpec(memory_space=pl.ANY), pl.BlockSpec(memory_space=pltpu.SMEM)
    dma = lambda *n: pltpu.SemaphoreType.DMA(n)
    return pl.pallas_call(
        last_kernel,
        in_specs=[smem] * 2 + [anywhere] * 6,
        out_specs=[anywhere, pl.BlockSpec(memory_space=pltpu.VMEM)],
        out_shape=[
            jax.ShapeDtypeStruct((sets, rows, width), f32),
            jax.ShapeDtypeStruct((longest, comp), kind),
        ],
        scratch_shapes=[pltpu.VMEM(v.shape, v.dtype) for v in (table, x, g, gfirst, gq, wq)]
        + [pltpu.VMEM(x.shape, f32), pltpu.VMEM((longest + TILE, comp), f32), dma(sets, 5), dma(1), dma(sets)],
        compiler_params=params(),
        name="last",
    )(kinds, offsets, table, x, g, gfirst, gq, wq)


def finish_kernel(layer_any, table, norms, up_first, up_more, down_first, down_more, *refs):
    squares, (layer_out, table_out, up_out, down_out), outs, (held, sems) = refs[:4], refs[4:8], refs[8:-2], refs[-2:]
    sets = range(held.shape[0])
    loads = [pltpu.make_async_copy(layer_any.at[i], held.at[i], sems.at[0, i]) for i in sets]
    stores = [pltpu.make_async_copy(held.at[i], layer_out.at[i], sems.at[1, i]) for i in sets]
    for load in loads:
        load.start()
    for load, store in zip(loads, stores):
        load.wait()
        store.start()
    table_out[...] = table[...].astype(f32)
    wide, tall = up_first.shape[1], down_first.shape[0]
    up_out[:, :wide] = up_first[...]
    down_out[:tall, :] = down_first[...]
    for i in range(up_more.shape[0]):
        up_out[:, (i + 1) * wide : (i + 2) * wide] = up_more[i]
    for i in range(down_more.shape[0]):
        down_out[(i + 1) * tall : (i + 2) * tall, :] = down_more[i]
    for i in range(4):
        outs[i][...] = squares[i][...]
        outs[4 + i][...] = norms[i, :]
    for store in stores:
        store.wait()


def finish(layer_out, table, norms, up_first, up_more, down_first, down_more, squares):
    vmem, anywhere = pl.BlockSpec(memory_space=pltpu.VMEM), pl.BlockSpec(memory_space=pl.ANY)
    width = norms.shape[1]
    out = lambda *dims: jax.ShapeDtypeStruct(dims, f32)
    return pl.pallas_call(
        finish_kernel,
        in_specs=[anywhere] + [vmem] * 10,
        out_specs=[anywhere] + [vmem] * 11,
        out_shape=[
            jax.ShapeDtypeStruct(layer_out.shape, layer_out.dtype),
            out(*table.shape),
            out(up_first.shape[0], up_first.shape[1] * (1 + up_more.shape[0])),
            out(down_first.shape[0] * (1 + down_more.shape[0]), down_first.shape[1]),
        ]
        + [out(*v.shape) for v in squares]
        + [out(width)] * 4,
        scratch_shapes=[pltpu.VMEM(layer_out.shape, layer_out.dtype), pltpu.SemaphoreType.DMA((2, layer_out.shape[0]))],
        compiler_params=params(),
        name="finish",
    )(layer_out, table, norms, up_first, up_more, down_first, down_more, *squares)


def sequence_sum(part, is_long, row_count, shortest):
    seq_count = lax.axis_size("seq")
    total = lax.psum(part, "seq")
    span = shortest // row_count
    if span > 1:
        groups = [list(range(i, i + span)) for i in range(0, seq_count, span)]
        part = lax.psum(part, "seq", axis_index_groups=groups)
    return jnp.where(is_long[:, None, None], total, part)


def table_start(set_kind, row_offset, block_index, row_count, shortest):
    position = block_index * row_count
    member = position // shortest
    chosen = jnp.sum(jnp.where(jnp.arange(4)[None, :] == member, row_offset, 0), axis=1)
    return jnp.where(set_kind > 0, position, chosen + position % shortest)


def local(
    inputs, cotangent, set_kind, row_offset, query_w, key_w, value_w, output_w, up_w, down_w, compress,
    first_gain, first_bias, second_gain, second_bias,
):
    sets, rows, width = inputs.shape
    longest, comp = compress.shape
    shortest = longest // 4
    ranked = lax.axis_index("seq")
    tokens = sets * rows
    is_long = set_kind > 0
    norms = (first_gain, first_bias, second_gain, second_bias)
    linked = lax.axis_size("batch") == 8 and lax.axis_size("seq") == 4 and rows == shortest
    weights = (query_w, key_w, value_w, output_w, up_w, down_w)
    if linked:
        summed, line = inputs, lax.axis_size("seq")
    else:
        starts = table_start(set_kind, row_offset, ranked, rows, shortest).astype(jnp.int32)
        table, part, _ = front(starts, compress, inputs, query_w)
        summed, line = sequence_sum(part, is_long, rows, shortest), 0
    (kc, vc, summed, mixed, hidden, layer_out, gdown, gatt, go, new_table, queries, e, act, gup, output_part, norm_sums) = layer(
        set_kind, row_offset, compress, summed, inputs, cotangent, weights, norms, line
    )
    flat = lambda v: v.reshape(-1, v.shape[-1])
    if linked:
        gq, gk, gv, g, output_grad, up_first, down_first, up_rows, down_rows, down_last = back(
            set_kind, flat(hidden), flat(gup), flat(act), flat(gdown), output_part, e, go, mixed, queries, kc, vc, key_w, value_w
        )
        g = g.reshape(sets, width, comp)
        input_grad, compress_part = last(set_kind, row_offset, new_table, inputs, g, gatt, gq, query_w, longest, bf16)
        table_sum, norm_total, up_more, down_more, *squares = closing(
            compress_part, norm_sums, flat(inputs), flat(gq), flat(summed), flat(gk), flat(gv), up_rows, down_rows, down_last
        )
        layer_out, compress_grad, up_grad, down_grad, *rest = finish(
            layer_out, table_sum, norm_total, up_first, up_more, down_first, down_more, squares + [output_grad]
        )
        compress_grad = compress_grad.reshape(longest, comp)
        weights, norm_grads = tuple(rest[:4]) + (up_grad, down_grad), rest[4:]
    else:
        up_part, down_part = feed_grads(flat(hidden), flat(gup), flat(act), flat(gdown))
        gq, gk, gv, g_part = attention_back(e, go, mixed, queries, kc, vc, key_w, value_w)
        g = sequence_sum(g_part, is_long, rows, shortest)
        query_part = square_grad(flat(inputs), flat(gq))
        key_part = square_grad(flat(summed), flat(gk))
        value_part = square_grad(flat(summed), flat(gv))
        input_grad, compress_part = last(set_kind, row_offset, table, inputs, g, gatt, gq, query_w, longest, f32)

        def scattered(v):
            v = lax.psum_scatter(v, "seq", scatter_dimension=1, tiled=True)
            return lax.psum_scatter(v, "batch", scatter_dimension=0, tiled=True).astype(f32)

        parts = (query_part, key_part, value_part, output_part, up_part, down_part)
        weights = tuple(scattered(v) for v in parts)
        compress_grad, norm_grads = lax.psum((compress_part, norm_sums), ("batch", "seq"))
    return (layer_out, input_grad) + weights + (compress_grad,) + tuple(norm_grads[i] for i in range(4))


def solution(mesh):
    tokens = P("batch", "seq", None)
    in_specs = (tokens, tokens, P("batch"), P("batch", None)) + (P(),) * 11
    out_specs = (tokens, tokens) + (P("batch", "seq"),) * 6 + (P(),) * 5
    return jax.shard_map(local, mesh=mesh, in_specs=in_specs, out_specs=out_specs, check_vma=False)
```

```python
import functools

import jax
import jax.numpy as jnp
from jax import lax
from jax.experimental import pallas as pl
from jax.experimental.pallas import tpu as pltpu
from jax.sharding import PartitionSpec as P

DH = 64
LANES = 128
TILE = 8
SCALE = DH ** (-0.5)
EPS = 1e-05
MESH = pl.DeviceIdType.MESH
VMEM_LIMIT = 63 * 1024 * 1024
bf16 = jnp.bfloat16
f32 = jnp.float32


def dot(left, right):
    return lax.dot_general(left, right, (((1,), (0,)), ((), ())), preferred_element_type=f32)


def dot_nt(left, right):
    return lax.dot_general(left, right, (((1,), (1,)), ((), ())), preferred_element_type=f32)


def dot_tn(left, right):
    return lax.dot_general(left, right, (((0,), (0,)), ((), ())), preferred_element_type=f32)


def params(**more):
    return pltpu.CompilerParams(vmem_limit_bytes=VMEM_LIMIT, **more)


def whole(shape):
    return pl.BlockSpec(shape, lambda *_: (0,) * len(shape), pipeline_mode=pl.Buffered(1))


def per_set(shape):
    return pl.BlockSpec((1,) + tuple(shape), lambda s, *_: (s,) + (0,) * len(shape))


def own_start(kinds, offsets, at, row_count, shortest):
    position = lax.axis_index("seq") * row_count
    return jnp.where(kinds[at] > 0, position, offsets[at, position // shortest] + position % shortest)


def aligned(start):
    begin = start // TILE * TILE
    return pl.multiple_of(begin, TILE), start - begin


def place():
    batch = lax.axis_index("batch")
    return batch // 4, batch // 2 % 2, batch % 2, lax.axis_index("seq")


def device(y, x, core, z):
    return ((y * 2 + x) * 2 + core, z)


def greet(others):
    barrier = pltpu.get_barrier_semaphore()
    for other in others:
        pl.semaphore_signal(barrier, inc=1, device_id=other, device_id_type=MESH)
    pl.semaphore_wait(barrier, len(others))


def remote(src, dst, send_sem, recv_sem, target):
    return pltpu.make_async_remote_copy(src, dst, send_sem, recv_sem, device_id=target, device_id_type=MESH)


class LineSum:
    def __init__(self, line, lag, own, from_left, from_right, sems):
        y, x, core, self.z = place()
        self.line, self.lag, self.own = line, lag, own
        self.right = device(y, x, core, (self.z + 1) % line)
        self.left = device(y, x, core, (self.z + line - 1) % line)
        inner, outer = self.z > 0, self.z < line - 1
        self.ways = (
            (from_left, self.right, inner, outer, sems[0], sems[1]),
            (from_right, self.left, outer, inner, sems[2], sems[3]),
        )

    def greet(self):
        barrier = pltpu.get_barrier_semaphore()
        for way in self.ways:

            @pl.when(way[3])
            def _():
                pl.semaphore_signal(barrier, inc=1, device_id=way[1], device_id_type=MESH)

        both = jnp.logical_and(self.z > 0, self.z < self.line - 1).astype(jnp.int32)
        pl.semaphore_wait(barrier, 1 + both)

    def prepare(self):
        for way in self.ways:

            @pl.when(jnp.logical_not(way[2]))
            def _():
                way[0][...] = jnp.zeros_like(way[0])

    def copy(self, way, at):
        held, target, _, _, send, recv = way
        return remote(held.at[at], held.at[at], send.at[at], recv.at[at], target)

    def forward(self, way, at):
        @pl.when(way[2])
        def _():
            self.copy(way, at).wait_recv()

        way[0][at] = way[0][at] + self.own[at]

        @pl.when(way[3])
        def _():
            self.copy(way, at).start()

    def slots(self):
        return self.own.shape[0] + self.lag * (self.line - 1)

    def serve(self, slot):
        for way, hops in zip(self.ways, (self.z, self.line - 1 - self.z)):
            at = slot - self.lag * hops

            @pl.when(jnp.logical_and(at >= 0, at < self.own.shape[0]))
            def _():
                self.forward(way, at)

    def serve_many(self, begin, count):
        def slot(at, carry):
            self.serve(at)
            return carry

        lax.fori_loop(begin, begin + count, slot, 0)

    def total(self, at, joined):
        own = self.own[at].astype(f32)
        both = self.ways[0][0][at].astype(f32) + self.ways[1][0][at].astype(f32)
        return jnp.where(joined, both - own, own).astype(bf16)

    def finish(self):
        for way in self.ways:

            @pl.when(way[3])
            def _():
                def wait(at, carry):
                    self.copy(way, at).wait_send()
                    return carry

                lax.fori_loop(0, self.own.shape[0], wait, 0)


class Scatter:
    def __init__(self, x_first, part, from_core, from_first, from_second, send, recv):
        y, x, core, z = place()
        self.part, self.recvs = part, (from_core, from_first, from_second)
        along_x, along_y = device(y, 1 - x, core, z), device(1 - y, x, core, z)
        self.core, self.x, self.y, self.x_first = core, x, y, x_first
        if x_first:
            sources = (part.at[:, :, 1 - core], from_core.at[:, 1 - x], from_first.at[1 - y])
            targets = (device(y, x, 1 - core, z), along_x, along_y)
        else:
            sources = (part.at[:, :, 1 - core], from_core.at[1 - y], from_first.at[1 - x])
            targets = (device(y, x, 1 - core, z), along_y, along_x)
        self.copies = [
            remote(sources[i], self.recvs[i], send.at[i], recv.at[i], targets[i]) for i in range(3)
        ]

    def start(self):
        self.copies[0].start()

    def first(self):
        self.copies[0].wait()
        self.recvs[0][...] = self.recvs[0][...] + self.part[:, :, self.core]
        self.copies[1].start()

    def second(self):
        self.copies[1].wait_recv()
        kept = self.recvs[0][:, self.x] if self.x_first else self.recvs[0][self.y]
        self.recvs[1][...] = self.recvs[1][...] + kept
        self.copies[2].start()

    def done(self):
        self.copies[2].wait_recv()
        kept = self.recvs[1][self.y] if self.x_first else self.recvs[1][self.x]
        return self.recvs[2][...].astype(f32) + kept.astype(f32)

    def finish(self):
        for copy in self.copies[1:]:
            copy.wait_send()


class LineScatter:
    def __init__(self, blocks, near, far, send, recv):
        y, x, core, z = place()
        self.blocks, self.near, self.far = blocks, near, far
        self.high, self.low = z // 2, z % 2
        self.copies = [
            remote(blocks.at[:, 1 - self.low], near, send.at[0], recv.at[0], device(y, x, core, z + 1 - 2 * self.low)),
            remote(near.at[1 - self.high], far, send.at[1], recv.at[1], device(y, x, core, (z + 2) % 4)),
        ]

    def start(self):
        self.copies[0].start()

    def middle(self):
        self.copies[0].wait_recv()
        self.near[...] = self.near[...] + self.blocks[:, self.low]
        self.copies[1].start()

    def done(self):
        self.copies[1].wait_recv()
        return self.near[self.high].astype(f32) + self.far[...].astype(f32)

    def finish(self):
        for copy in self.copies:
            copy.wait_send()


def line_scatter_blocks(blocks, rows, line):
    step = rows.shape[1] // line
    for z in range(line):
        mine = rows[:, z * step : (z + 1) * step]
        if step % LANES:
            top = rows.shape[0] // 2
            mine = jnp.concatenate([mine[:top], mine[top:]], axis=1)
        blocks[z // 2, z % 2] = mine.astype(bf16)


def unfold(total, out):
    if total.shape[1] == out.shape[1]:
        out[...] = total
    else:
        top, step = total.shape[0], out.shape[1]
        out[:top, :] = total[:, :step]
        out[top:, :] = total[:, step:]


def block_shape(rows, width, line):
    step = width // line
    return (rows, step) if step % LANES == 0 else (rows // 2, step * 2)


def scatter_scratch(rows, width, *count):
    shapes = [(2, 2, rows, width), (2, rows, width), (rows, width)]
    return [pltpu.VMEM(count + shape, bf16) for shape in shapes] + [pltpu.SemaphoreType.DMA(count + (3,))] * 2


def line_scratch(rows, width, line):
    block = block_shape(rows, width, line)
    return [pltpu.VMEM(n + block, bf16) for n in ((2, 2), (2,), ())] + [pltpu.SemaphoreType.DMA((2,))] * 2


class Neighbours:
    def __init__(self, line):
        y, x, core, z = place()
        self.core = device(y, x, 1 - core, z)
        places = [((y + dy) % 2, (x + dx) % 2) for dy, dx in ((0, 1), (1, 0), (1, 1))]
        self.plane = [(py * 2 + px, device(py, px, core, z)) for py, px in places]
        self.line = [((z + d) % line, device(y, x, core, (z + d) % line)) for d in range(1, line)]

    def everyone(self):
        return [self.core] + [to for _, to in self.plane] + [to for _, to in self.line]


class Total:
    counts = lambda line: (2, 6, 2 * (line - 1), line - 1, 3, 1)

    def __init__(self, line, near, table, norms, table_out, norms_out, mine, from_core, from_plane, from_line, gathered,
                 core_norms, plane_norms, line_norms, *sems):
        y, x, core, z = place()
        plane = y * 2 + x
        pairs = [(sems[2 * i], sems[2 * i + 1]) for i in range(6)]
        self.running = []

        def start(stage, moves):
            send, recv = pairs[stage]
            self.running = [remote(src, dst, send.at[i], recv.at[i], to) for i, (src, dst, to) in enumerate(moves)]
            for copy in self.running:
                copy.start()

        def to_core():
            mine[...] = table[...]
            core_norms[0] = norms[...]
            start(0, [(mine.at[1 - core], from_core, near.core), (core_norms.at[0], core_norms.at[1], near.core)])

        def to_plane():
            from_core[...] = from_core[...] + mine[core]
            plane_norms[plane] = core_norms[0] + core_norms[1]
            kept = plane_norms.at[plane]
            start(1, [(from_core.at[p], from_plane.at[i], to) for i, (p, to) in enumerate(near.plane)]
                  + [(kept, kept, to) for _, to in near.plane])

        def to_line():
            total = from_core[plane].astype(f32)
            for i in range(3):
                total = total + from_plane[i].astype(f32)
            mine[0, 0] = total.astype(bf16)
            line_norms[z] = plane_norms[0] + plane_norms[1] + plane_norms[2] + plane_norms[3]
            kept = line_norms.at[z]
            start(2, [(mine.at[0, 0, p], from_line.at[i], to) for i, (p, to) in enumerate(near.line)]
                  + [(kept, kept, to) for _, to in near.line])

        def back_line():
            total = mine[0, 0, z].astype(f32)
            for i in range(line - 1):
                total = total + from_line[i].astype(f32)
            gathered[core, plane, z] = total.astype(bf16)
            all_norms = line_norms[0]
            for i in range(1, line):
                all_norms = all_norms + line_norms[i]
            norms_out[...] = all_norms
            block = gathered.at[core, plane, z]
            start(3, [(block, block, to) for _, to in near.line])

        def back_plane():
            block = gathered.at[core, plane]
            start(4, [(block, block, to) for _, to in near.plane])

        def back_core():
            block = gathered.at[core]
            start(5, [(block, block, near.core)])

        def close():
            table_out[...] = gathered[...]

        self.stages = [to_core, to_plane, to_line, back_line, back_plane, back_core, close]

    def advance(self):
        for copy in self.running:
            copy.wait()
        self.running = []
        self.stages.pop(0)()

    @staticmethod
    def scratch(line, shape, norms):
        vmem = pltpu.VMEM
        return [
            vmem(shape, bf16), vmem(shape[1:], bf16), vmem((3,) + shape[2:], bf16), vmem((line - 1,) + shape[3:], bf16),
            vmem(shape, bf16), vmem((2,) + norms, f32), vmem((4,) + norms, f32), vmem((line,) + norms, f32),
        ] + [pltpu.SemaphoreType.DMA((n,)) for n in Total.counts(line) for _ in range(2)]


def closing_kernel(line, table_ref, norms_ref, x_any, gq_any, c_any, gk_any, gv_any, up_ref, down_ref, last_ref,
                   table_out, norms_out, up_out, down_out, query_out, key_out, value_out,
                   x, gq, c, gk, gv, load_sems, *scratch):
    scratch = list(scratch)
    take = lambda n: [scratch.pop(0) for _ in range(n)]
    pairs = ((x_any, x), (gq_any, gq), (c_any, c), (gk_any, gk), (gv_any, gv))
    loads = [pltpu.make_async_copy(src, dst, load_sems.at[i]) for i, (src, dst) in enumerate(pairs)]
    for load in loads:
        load.start()
    near = Neighbours(line)
    greet(near.everyone())
    total = Total(line, near, table_ref, norms_ref, table_out, norms_out, *take(8 + 12))
    total.advance()
    down_job, down_line = Scatter(False, last_ref, *take(5)), LineScatter(*take(5))
    down_job.start()
    across = []
    for rows, out in [(up_ref, up_out), (down_ref, down_out)]:
        for chunk in range(rows.shape[0]):
            job = LineScatter(*take(5))
            line_scatter_blocks(job.blocks, rows[chunk], line)
            job.start()
            across.append((job, out.at[chunk]))
    total.advance()
    down_job.first()
    jobs = []
    for i, (left, right) in enumerate(((x, gq), (c, gk), (c, gv))):
        part = take(1)[0]
        jobs.append((Scatter(i % 2 == 0, part, *take(5)), LineScatter(*take(5)), (query_out, key_out, value_out)[i]))
        for load in ((loads[0], loads[1]), (loads[2], loads[3]), (loads[4],))[i]:
            load.wait()
        narrow = part.shape[:-1] + (2 * LANES,)

        def columns(j, carry):
            span = pl.ds(pl.multiple_of(j * 2 * LANES, LANES), 2 * LANES)
            part[:, :, :, :, span] = dot_tn(left[...], right[:, span]).astype(bf16).reshape(narrow)
            return carry

        lax.fori_loop(0, part.shape[-1] // (2 * LANES), columns, 0)
        jobs[i][0].start()
        if i > 0:
            jobs[i - 1][0].first()
    for job, _ in across:
        job.middle()
    total.advance()
    jobs[2][0].first()
    down_job.second()
    total.advance()
    jobs[0][0].second()
    for job, out in across:
        unfold(job.done(), out)
    total.advance()
    jobs[1][0].second()
    jobs[2][0].second()
    jobs.append((down_job, down_line, down_out.at[down_ref.shape[0]]))
    line_scatter_blocks(down_line.blocks, down_job.done(), line)
    down_line.start()
    total.advance()
    for job, line_job, _ in jobs[:3]:
        line_scatter_blocks(line_job.blocks, job.done(), line)
        line_job.start()
    total.advance()
    for _, line_job, _ in jobs:
        line_job.middle()
    for _, line_job, out in jobs:
        unfold(line_job.done(), out)
    for job, _ in across:
        job.finish()
    for job, line_job, _ in jobs:
        job.finish()
        line_job.finish()


def closing(table, norms, x, gq, c, gk, gv, up_rows, down_rows, down_last):
    line = lax.axis_size("seq")
    longest, comp = table.shape
    width = x.shape[1]
    shape = (2, 4, line, longest // (8 * line), comp)
    rows = width // 8
    vmem, anywhere = pl.BlockSpec(memory_space=pltpu.VMEM), pl.BlockSpec(memory_space=pl.ANY)
    out = lambda *dims: jax.ShapeDtypeStruct(dims, f32)
    (ups, _, wide), (downs, tall, _) = up_rows.shape, down_rows.shape
    scratch = [pltpu.VMEM(v.shape, bf16) for v in (x, gq, c, gk, gv)] + [pltpu.SemaphoreType.DMA((5,))]
    scratch += Total.scratch(line, shape, norms.shape)
    scratch += scatter_scratch(tall, width) + line_scratch(tall, width, line)
    for _ in range(ups):
        scratch += line_scratch(rows, wide, line)
    for _ in range(downs):
        scratch += line_scratch(tall, width, line)
    for _ in range(3):
        scratch += [pltpu.VMEM((2, 2, 2, rows, width), bf16)] + scatter_scratch(rows, width) + line_scratch(rows, width, line)
    table_out, *rest = pl.pallas_call(
        functools.partial(closing_kernel, line),
        in_specs=[vmem] * 2 + [anywhere] * 5 + [vmem] * 3,
        out_specs=[vmem] * 7,
        out_shape=[jax.ShapeDtypeStruct(shape, bf16), out(*norms.shape), out(ups, rows, wide // line), out(downs + 1, tall, width // line)]
        + [out(rows, width // line)] * 3,
        scratch_shapes=scratch,
        compiler_params=params(collective_id=3, has_side_effects=True),
        name="closing",
    )(table.reshape(shape), norms, x, gq, c, gk, gv, up_rows, down_rows, down_last)
    return [table_out] + rest


def front_kernel(start_ref, compress_ref, x_ref, wq_ref, table_ref, c_ref, q_ref, wide):
    step = pl.program_id(0)

    longest = compress_ref.shape[0]

    @pl.when(step == 0)
    def _():
        wide[:longest, :] = compress_ref[...].astype(f32)
        wide[longest:, :] = jnp.zeros((TILE, wide.shape[1]), f32)

    rows = x_ref.shape[1]
    begin, shift = aligned(start_ref[step])
    window = wide[pl.ds(begin, rows + TILE), :]
    table = pltpu.roll(window, lax.rem(rows + TILE - shift, rows + TILE), 0)[:rows].astype(bf16)
    table_ref[0] = table
    x = x_ref[0]
    c_ref[0] = dot_tn(table, x).astype(bf16)
    q_ref[0] = (dot(x, wq_ref[...]) * SCALE).astype(bf16)


def front(starts, compress, x, wq):
    sets, rows, width = x.shape
    longest, comp = compress.shape
    grid_spec = pltpu.PrefetchScalarGridSpec(
        num_scalar_prefetch=1,
        grid=(sets,),
        in_specs=[whole(compress.shape), per_set((rows, width)), whole(wq.shape)],
        out_specs=[per_set((rows, comp)), per_set((comp, width)), per_set((rows, width))],
        scratch_shapes=[pltpu.VMEM((longest + TILE, comp), f32)],
    )
    return pl.pallas_call(
        front_kernel,
        grid_spec=grid_spec,
        out_shape=[
            jax.ShapeDtypeStruct((sets, rows, comp), bf16),
            jax.ShapeDtypeStruct((sets, comp, width), bf16),
            jax.ShapeDtypeStruct((sets, rows, width), bf16),
        ],
        compiler_params=params(),
        name="front",
    )(starts, compress, x, wq)


def head_blocks(pair, first_half):
    zero = jnp.zeros_like(pair)
    return jnp.concatenate([jnp.where(first_half, pair, zero), jnp.where(first_half, zero, pair)], axis=0)


def norm_forward(v):
    average = jnp.mean(v, axis=-1, keepdims=True)
    centered = v - average
    variance = jnp.mean(centered * centered, axis=-1, keepdims=True)
    inverse = lax.rsqrt(variance + EPS)
    return centered * inverse, inverse


def norm_backward(dz, z, inverse):
    return (dz - jnp.mean(dz, axis=-1, keepdims=True) - z * jnp.mean(dz * z, axis=-1, keepdims=True)) * inverse


PIECES = 4
LAG = 2
HALVES = 2


def layer_kernel(
    line, long_ref, offset_ref, compress_ref, c_ref, x_any, cot_ref, gain1_ref, bias1_ref, gain2_ref, bias2_ref, wq_any, wk_any, wv_any, wo_any, up_any, down_any,
    kc_ref, vc_ref, csum_ref, mixed_ref, hidden_ref, out_ref, gdown_ref, gatt_ref, go_ref, table_any, q_any,
    e_any, act_any, gup_any, output_grad_ref, sums_ref,
    xs, qs, wq, wk, wv, wo, up, down, e_buf, act, gup, z_first, rinv_ref, held, output_grad, weight_sems, x_sems, out_sems,
    *linked,
):
    step = pl.program_id(0)
    last = pl.num_programs(0) - 1
    sets, rows, width = xs.shape
    comp = kc_ref.shape[1]
    units = up.shape[1]
    chunk = 768
    loads = [
        pltpu.make_async_copy(src, dst, weight_sems.at[i])
        for i, (src, dst) in enumerate(
            ((wq_any, wq), (wk_any, wk), (wv_any, wv), (wo_any, wo), (up_any, up), (down_any, down))
        )
    ]
    x_loads = [pltpu.make_async_copy(x_any.at[s], xs.at[s], x_sems.at[s]) for s in range(sets)]
    q_store = pltpu.make_async_copy(qs, q_any, out_sems.at[3])
    e_store = pltpu.make_async_copy(e_buf, e_any.at[step], out_sems.at[0])
    act_store = pltpu.make_async_copy(act, act_any.at[step], out_sems.at[1])
    gup_store = pltpu.make_async_copy(gup, gup_any.at[step], out_sems.at[2])

    if line:
        tables, own, from_left, from_right, table_sems, *sems = linked
        sums = LineSum(line, LAG, own, from_left, from_right, sems)
        ahead = PIECES + LAG * (line - 1)
        t_stores = [pltpu.make_async_copy(tables.at[s], table_any.at[s], table_sems.at[s]) for s in range(sets)]

    def first_use(load):
        @pl.when(step == 0)
        def _():
            load.wait()

    @pl.when(step == 0)
    def _():
        for load in x_loads:
            load.start()
        sums_ref[...] = jnp.zeros_like(sums_ref)
        output_grad[...] = jnp.zeros_like(output_grad)
        if line:
            longest = compress_ref.shape[0]
            sums.greet()
            sums.prepare()
            grid = (rows, rows)
            ahead_by = lax.broadcasted_iota(jnp.int32, grid, 1) - lax.broadcasted_iota(jnp.int32, grid, 0)

        def summarize(s, carry):
            pltpu.make_async_copy(x_any.at[s], xs.at[s], x_sems.at[s]).wait()

            @pl.when(s == 0)
            def _():
                loads[0].start()

            if line:
                table = jnp.zeros((rows, comp), f32)
                start = own_start(long_ref, offset_ref, s, rows, longest // 4)
                for at in range(0, longest, rows):
                    chosen = jnp.where(ahead_by == start - at, 1.0, 0.0).astype(bf16)
                    table = table + dot(chosen, compress_ref[at : at + rows, :])
                table = table.astype(bf16)
                tables[s] = table
                pltpu.make_async_copy(tables.at[s], table_any.at[s], table_sems.at[s]).start()
                c = dot_tn(table, xs[s]).astype(bf16)
                own[pl.ds(s * PIECES, PIECES)] = c.reshape(PIECES, comp // PIECES, width)
                sums.serve(s)
            return carry

        lax.fori_loop(0, sets, summarize, 0)
        for load in loads[1:]:
            load.start()
        loads[0].wait()

        def query(s, carry):
            qs[s] = (dot(xs[s], wq[...]) * SCALE).astype(bf16)
            if line:
                sums.serve(sets + s)
            return carry

        lax.fori_loop(0, sets, query, 0)
        q_store.start()
        if line:
            sums.serve_many(2 * sets, ahead - 2 * sets)

    def serve(part):
        if line:
            count = PIECES // 4

            @pl.when(step < last)
            def _():
                sums.serve_many(ahead + step * PIECES + part * count, count)

    if line:
        joined = long_ref[step] > 0
        for piece in range(PIECES):
            size = comp // PIECES
            csum_ref[0, piece * size : (piece + 1) * size, :] = sums.total(step * PIECES + piece, joined)
    else:
        csum_ref[0] = c_ref[0]
    first_use(loads[1])
    first_use(loads[2])
    c = csum_ref[0]
    kc_ref[0] = dot(c, wk[...]).astype(bf16)
    vc_ref[0] = dot(c, wv[...]).astype(bf16)
    half = lax.broadcasted_iota(jnp.int32, (comp, LANES), 1) < DH
    ones = head_blocks(jnp.ones((comp, LANES), bf16), half)

    @pl.when(step > 0)
    def _():
        e_store.wait()

    for pair in range(width // LANES):
        lanes = pl.ds(pair * LANES, LANES)
        keys = head_blocks(kc_ref[0, :, lanes], half)
        values = jnp.concatenate([head_blocks(vc_ref[0, :, lanes], half), ones], axis=1)
        scores = dot_nt(qs[step, :, lanes], keys)
        parts = []
        for head in range(2):
            mine = scores[:, head * comp : (head + 1) * comp]
            top = jnp.max(mine, axis=-1, keepdims=True)
            parts.append(jnp.exp(mine - top).astype(bf16))
        e = jnp.concatenate(parts, axis=1)
        e_buf[:, pl.ds(pair * 2 * comp, 2 * comp)] = e
        total = dot(e, values)
        rinv = 1.0 / total[:, LANES:]
        rinv_ref[:, lanes] = rinv
        mixed_ref[0, :, lanes] = (total[:, :LANES] * rinv).astype(bf16)
    e_store.start()
    first_use(loads[3])
    serve(0)
    gain1, bias1, gain2, bias2 = (ref[...].reshape(1, width) for ref in (gain1_ref, bias1_ref, gain2_ref, bias2_ref))
    size = rows // HALVES
    halves = [pl.ds(h * size, size) for h in range(HALVES)]
    inverse1 = []
    for part in halves:
        z1, inv1 = norm_forward(xs[step, part, :].astype(f32) + dot(mixed_ref[0, part, :], wo[...]))
        inverse1.append(inv1)
        z_first[part, :] = z1
        hidden = z1 * gain1 + bias1
        hidden_ref[0, part, :] = hidden.astype(bf16)
        held[part, :] = hidden
    first_use(loads[4])
    first_use(loads[5])

    @pl.when(step > 0)
    def _():
        act_store.wait()
        gup_store.wait()

    for part in halves:
        hidden_low = hidden_ref[0, part, :]
        for at in range(0, units, chunk):
            span = pl.ds(at, chunk)
            upward = dot(hidden_low, up[:, span])
            cdf = 0.5 + 0.5 * lax.erf(upward * (0.5**0.5))
            density = jnp.exp(upward * upward * -0.5) * 0.3989422804014327
            act[part, span] = (upward * cdf).astype(bf16)
            gup[part, span] = (cdf + upward * density).astype(bf16)
    act_store.start()
    serve(1)
    sums2 = []
    for part in halves:
        z2, inv2 = norm_forward(held[part, :] + dot(act[part, :], down[...]))
        out_ref[0, part, :] = (z2 * gain2 + bias2).astype(bf16)
        dy = cot_ref[0, part, :].astype(f32)
        gsecond = norm_backward(dy * gain2, z2, inv2)
        sums2.append((jnp.sum(dy * z2, axis=0, keepdims=True), jnp.sum(dy, axis=0, keepdims=True)))
        gdown_ref[0, part, :] = gsecond.astype(bf16)
        held[part, :] = gsecond
    for part in halves:
        gdown = gdown_ref[0, part, :]
        for at in range(0, units, chunk):
            span = pl.ds(at, chunk)
            gact = dot_nt(gdown, down[span, :])
            gup[part, span] = (gact * gup[part, span].astype(f32)).astype(bf16)
    gup_store.start()
    serve(2)
    sums1 = []
    for part, inv1 in zip(halves, inverse1):
        ghidden = held[part, :] + dot_nt(gup[part, :], up[...])
        z1 = z_first[part, :]
        sums1.append((jnp.sum(ghidden * z1, axis=0, keepdims=True), jnp.sum(ghidden, axis=0, keepdims=True)))
        gatt_ref[0, part, :] = norm_backward(ghidden * gain1, z1, inv1).astype(bf16)
    for part in halves:
        go_ref[0, part, :] = (dot_nt(gatt_ref[0, part, :], wo[...]) * rinv_ref[part, :]).astype(bf16)
    output_grad[...] += dot_tn(mixed_ref[0], gatt_ref[0])
    for i, pieces in enumerate((sums1, sums2)):
        for j in range(2):
            sums_ref[2 * i + j : 2 * i + j + 1, :] += sum(piece[j] for piece in pieces)
    serve(3)

    @pl.when(step == last)
    def _():
        output_grad_ref[...] = output_grad[...].astype(bf16)
        e_store.wait()
        act_store.wait()
        gup_store.wait()
        q_store.wait()
        if line:
            for store in t_stores:
                store.wait()
            sums.finish()


def layer(set_kind, row_offset, compress, c, x, cot, weights, norms, line):
    sets, rows, width = x.shape
    longest, comp = compress.shape
    wq, wk, wv, wo, up, down = weights
    units = up.shape[1]
    tokens = per_set((rows, width))
    short = per_set((comp, width))
    anywhere = pl.BlockSpec(memory_space=pl.ANY)
    smem = pl.BlockSpec(memory_space=pltpu.SMEM)
    shape = lambda *dims, kind=bf16: jax.ShapeDtypeStruct(dims, kind)
    dma = lambda n: pltpu.SemaphoreType.DMA((n,))
    linked = []
    if line:
        count = sets * PIECES
        linked = [pltpu.VMEM((sets, rows, comp), bf16)]
        linked += [pltpu.VMEM((count, comp // PIECES, width), bf16)] * 3 + [dma(sets)] + [dma(count)] * 4
    more = dict(collective_id=0, has_side_effects=True) if line else {}
    return pl.pallas_call(
        functools.partial(layer_kernel, line),
        grid=(sets,),
        in_specs=[smem, smem, whole(compress.shape), anywhere if line else short, anywhere, tokens]
        + [whole((width,))] * 4
        + [anywhere] * 6,
        out_specs=[short] * 3 + [tokens] * 6 + [anywhere] * 5 + [whole((width, width)), whole((8, width))],
        out_shape=[shape(sets, comp, width)] * 3
        + [shape(sets, rows, width)] * 6
        + [shape(sets, rows, comp), shape(sets, rows, width)]
        + [shape(sets, rows, width // DH * comp)]
        + [shape(sets, rows, units)] * 2
        + [shape(width, width), shape(8, width, kind=f32)],
        scratch_shapes=[pltpu.VMEM(x.shape, bf16)] * 2
        + [pltpu.VMEM(w.shape, bf16) for w in weights]
        + [pltpu.VMEM((rows, width // DH * comp), bf16)]
        + [pltpu.VMEM((rows, units), bf16)] * 2
        + [pltpu.VMEM((rows, width), f32)] * 3
        + [pltpu.VMEM((width, width), f32), dma(6), dma(sets), dma(4)]
        + linked,
        compiler_params=params(**more),
        name="layer",
    )(set_kind, row_offset, compress, c, x, cot, *norms, *weights)


def pair_back(pair, e_ref, go_ref, mixed_ref, q_ref, kc_ref, vc_ref, gq_ref, gkt, gvt, half, minus):
    comp = kc_ref.shape[0]
    lanes = pl.ds(pair * LANES, LANES)
    e = e_ref[:, pl.ds(pair * 2 * comp, 2 * comp)]
    keys = head_blocks(kc_ref[:, lanes], half)
    values = jnp.concatenate([head_blocks(vc_ref[:, lanes], half), minus], axis=1)
    go = go_ref[:, lanes]
    delta = (go.astype(f32) * mixed_ref[:, lanes].astype(f32)).astype(bf16)
    gp = dot_nt(jnp.concatenate([go, delta], axis=1), values)
    gs = (gp * e.astype(f32)).astype(bf16)
    gq_ref[:, lanes] = (dot(gs, keys) * SCALE).astype(bf16)
    for into, left, right in ((gkt, q_ref[:, lanes], gs), (gvt, go, e)):
        both = dot_tn(left, right)
        at = pair * LANES
        into[at : at + DH, :] = both[:DH, :comp].astype(bf16)
        into[at + DH : at + LANES, :] = both[DH:, comp:].astype(bf16)


CHUNKS = 3
HERE = 1
BACK_PIECES = 4
BACK_LAG = 2


def back_kernel(
    line, long_ref, hidden_any, gup_any, act_any, gdown_any, output_any, e_any, go_any, mixed_any, q_any, kc_any, vc_any, wk_any, wv_any,
    gq_any, gk_any, gv_any, g_any, output_out, up_out, down_out, up_rows, down_rows, down_last,
    hidden, gdown, feed, wk, wv, e, go, mixed, q, kc, vc, gq, gkt, gvt, gk, gv, own, from_left, from_right,
    up_part, down_part, output_part, load_sems, feed_sems, set_sems, out_sems, g_sem, *scratch,
):
    scratch = list(scratch)
    take = lambda n: [scratch.pop(0) for _ in range(n)]
    sets, rows, width = q_any.shape
    comp = kc_any.shape[1]
    units = gup_any.shape[1]
    sums = LineSum(line, BACK_LAG, own, from_left, from_right, take(4))

    def copies(pairs, sems):
        return [pltpu.make_async_copy(src, dst, sems.at[i]) for i, (src, dst) in enumerate(pairs)]

    def feed_loads(chunk, which):
        if which == 0:
            wide, count, source = units // line, line, gup_any
        else:
            wide, count, source = units // 8, 8, act_any
        step = wide // CHUNKS
        return copies(
            [
                (source.at[:, pl.ds(pl.multiple_of(i * wide + chunk * step, LANES), step)], feed.at[which, :, pl.ds(i * step, step)])
                for i in range(count)
            ],
            feed_sems.at[which],
        )

    def set_loads(s):
        at = s % 2
        return copies(
            [(e_any.at[s], e.at[at]), (go_any.at[s], go.at[at]), (mixed_any.at[s], mixed.at[at]), (q_any.at[s], q.at[at]),
             (kc_any.at[s], kc.at[at]), (vc_any.at[s], vc.at[at])],
            set_sems.at[at],
        )

    def set_stores(s):
        at = s % 2
        return copies([(gq.at[at], gq_any.at[s]), (gk.at[at], gk_any.at[s]), (gv.at[at], gv_any.at[s])], out_sems.at[at])

    def begin(some):
        for copy in some:
            copy.start()

    def end(some):
        for copy in some:
            copy.wait()

    weights = copies(((output_any, output_part), (hidden_any, hidden), (gdown_any, gdown), (wk_any, wk), (wv_any, wv)), load_sems)
    begin(weights[:1])
    begin(set_loads(0))
    begin(weights[3:])
    near = Neighbours(line)
    greet(near.everyone())
    sums.prepare()

    jobs = {"o": (Scatter(True, output_part, *take(5)), LineScatter(*take(5)), output_out)}
    lines = [LineScatter(*take(5)), LineScatter(*take(5))]
    kept = (take(5), take(5))

    def scatter_job(which, chunk):
        buffers = [ref.at[chunk] for ref in kept[which]]
        return Scatter(which == 0, (up_part, down_part)[which].at[chunk % 2], *buffers)

    for chunk in range(CHUNKS):
        for which in range(2):
            if chunk < HERE:
                jobs[which, chunk] = (scatter_job(which, chunk), lines[which], (up_out, down_out)[which])
            elif (which, chunk) != (1, CHUNKS - 1):
                jobs[which, chunk] = (scatter_job(which, chunk), None, (up_rows, down_rows)[which].at[chunk - HERE])

    def across(name):
        job, line_job, _ = jobs[name]
        line_scatter_blocks(line_job.blocks, job.done(), line)
        line_job.start()

    def feed_grad(chunk, which):
        if which == 0:
            up_part[chunk % 2] = dot_tn(hidden[...], feed[0]).astype(bf16).reshape(up_part.shape[1:])
        else:
            down_part[chunk % 2] = dot_tn(feed[1], gdown[...]).astype(bf16).reshape(down_part.shape[1:])

    half = lax.broadcasted_iota(jnp.int32, (comp, LANES), 1) < DH
    minus = head_blocks(jnp.full((comp, LANES), -1.0, bf16), half)

    def heads(s, pairs):
        at = s % 2
        for pair in pairs:
            pair_back(pair, e.at[at], go.at[at], mixed.at[at], q.at[at], kc.at[at], vc.at[at], gq.at[at], gkt, gvt, half, minus)

    def joins(s):
        g = dot(wk[...], gkt[...]) + dot(wv[...], gvt[...])
        own[pl.ds(s * BACK_PIECES, BACK_PIECES)] = g.astype(bf16).reshape(BACK_PIECES, width // BACK_PIECES, comp)
        gk[s % 2] = gkt[...].T
        gv[s % 2] = gvt[...].T
        begin(set_stores(s))

    o, (u0, u1, u2), (d0, d1) = jobs["o"][0], [jobs[0, i][0] for i in range(3)], [jobs[1, i][0] for i in range(2)]
    weights[0].wait()
    o.start()

    def steps(s, by_set):
        for at, due in by_set.items():

            @pl.when(s == at)
            def _():
                for one in due:
                    one()

    def work(s, carry):
        end(set_loads(s))

        @pl.when(s > 1)
        def _():
            end(set_stores(s - 2))

        steps(s, {
            0: [lambda: begin(weights[1:2]), lambda: begin(feed_loads(0, 0))],
            1: [lambda: begin(feed_loads(1, 0)), lambda: begin(weights[2:3]), lambda: begin(feed_loads(0, 1))],
            2: [lambda: begin(feed_loads(1, 1)), lambda: begin(set_loads(3))],
            3: [lambda: begin(feed_loads(2, 0)), lambda: begin(feed_loads(2, 1))],
        })
        pairs = width // LANES
        heads(s, range(pairs // 2))
        steps(s, {0: [o.first], 1: [u0.first], 2: [d0.first], 3: [d1.first]})
        heads(s, range(pairs // 2, pairs))
        steps(s, {0: [lambda: end(weights[3:])], 1: [o.second], 2: [u0.second], 3: [u1.second, d0.second]})
        joins(s)
        sums.serve_many(s * BACK_PIECES, 2)

        @pl.when(s != 2)
        def _():
            chunk = s - s // 3
            end(feed_loads(chunk, 0))
            steps(s, {0: [lambda: end(weights[1:2]), lambda: begin(set_loads(1))], 1: [lambda: begin(set_loads(2))]})
            feed_grad(chunk, 0)
            scatter_job(0, chunk).start()
            sums.serve_many(s * BACK_PIECES + 2, 2)

        @pl.when(s > 0)
        def _():
            end(feed_loads(s - 1, 1))
            steps(s, {1: [lambda: end(weights[2:3])]})
            feed_grad(s - 1, 1)

            @pl.when(s < sets - 1)
            def _():
                scatter_job(1, s - 1).start()

        steps(s, {1: [u1.first], 2: [lambda: sums.serve_many(2 * BACK_PIECES + 2, 2)], 3: [u2.first]})
        return carry

    lax.fori_loop(0, sets, work, 0)
    down_last[...] = down_part[(CHUNKS - 1) % 2]
    served = sets * BACK_PIECES
    sums.serve_many(served, 2)
    d1.second()
    sums.serve_many(served + 2, sums.slots() - served - 2)
    for name in ("o", (0, 0), (1, 0)):
        across(name)
    u2.second()
    for name in ("o", (0, 0), (1, 0)):
        jobs[name][1].middle()
    for s in range(sets):
        for piece in range(s * BACK_PIECES, (s + 1) * BACK_PIECES):
            own[piece] = sums.total(piece, long_ref[s] > 0)
    g_store = pltpu.make_async_copy(own, g_any, g_sem.at[0])
    g_store.start()
    for name in jobs:
        job, line_job, out = jobs[name]
        if line_job is not None:
            unfold(line_job.done(), out)
        else:
            out[...] = job.done().astype(bf16)
    for name in jobs:
        job, line_job, _ = jobs[name]
        job.finish()
        if line_job is not None:
            line_job.finish()
    for s in range(sets - 2, sets):
        end(set_stores(s))
    g_store.wait()
    sums.finish()


def back(set_kind, hidden, gup, act, gdown, output_part, e, go, mixed, q, kc, vc, wk, wv):
    line = lax.axis_size("seq")
    sets, rows, width = q.shape
    comp = kc.shape[1]
    tokens, units = gup.shape
    eighth = width // 8
    wide, tall = units // CHUNKS, units // 8 // CHUNKS
    count = sets * BACK_PIECES
    dma = lambda *n: pltpu.SemaphoreType.DMA(n)
    vmem, anywhere = pl.BlockSpec(memory_space=pltpu.VMEM), pl.BlockSpec(memory_space=pl.ANY)
    shape = lambda *dims, kind=bf16: jax.ShapeDtypeStruct(dims, kind)
    buffer = lambda *dims, kind=bf16: pltpu.VMEM(dims, kind)
    scratch = [buffer(tokens, width)] * 2 + [buffer(2, tokens, wide)] + [buffer(width, width)] * 2
    scratch += [buffer(2, rows, e.shape[2])] + [buffer(2, rows, width)] * 3 + [buffer(2, comp, width)] * 2
    scratch += [buffer(2, rows, width)] + [buffer(width, comp)] * 2 + [buffer(2, comp, width)] * 2
    scratch += [buffer(count, width // BACK_PIECES, comp)] * 3
    scratch += [buffer(2, 2, 2, 2, eighth, wide), buffer(2, 2, 2, 2, tall, width), buffer(2, 2, 2, eighth, width)]
    scratch += [dma(5), dma(2, 8), dma(2, 6), dma(2, 3), dma(1)] + [dma(count)] * 4
    scratch += scatter_scratch(eighth, width)
    for size in ((eighth, width), (eighth, wide), (tall, width)):
        scratch += line_scratch(*size, line)
    scratch += scatter_scratch(eighth, wide, CHUNKS) + scatter_scratch(tall, width, CHUNKS - 1)
    return pl.pallas_call(
        functools.partial(back_kernel, line),
        in_specs=[pl.BlockSpec(memory_space=pltpu.SMEM)] + [anywhere] * 13,
        out_specs=[anywhere] * 4 + [vmem] * 6,
        out_shape=[
            shape(sets, rows, width), shape(sets, comp, width), shape(sets, comp, width),
            shape(count, width // BACK_PIECES, comp),
            shape(eighth, width // line, kind=f32),
            shape(eighth, wide // line * HERE, kind=f32), shape(tall * HERE, width // line, kind=f32),
            shape(CHUNKS - HERE, eighth, wide), shape(CHUNKS - HERE - 1, tall, width), shape(2, 2, 2, tall, width),
        ],
        scratch_shapes=scratch,
        compiler_params=params(collective_id=1, has_side_effects=True),
        name="back",
    )(set_kind, hidden, gup, act, gdown, output_part.reshape(2, 2, 2, eighth, width), e, go, mixed, q, kc, vc, wk, wv)


def attention_back_kernel(
    e_ref, go_ref, mixed_ref, q_ref, kc_ref, vc_ref, wk_ref, wv_ref,
    gq_ref, gk_ref, gv_ref, g_ref,
    gkt, gvt,
):
    width = q_ref.shape[2]
    comp = kc_ref.shape[1]
    half = lax.broadcasted_iota(jnp.int32, (comp, LANES), 1) < DH
    minus = head_blocks(jnp.full((comp, LANES), -1.0, bf16), half)
    refs = [ref.at[0] for ref in (e_ref, go_ref, mixed_ref, q_ref, kc_ref, vc_ref, gq_ref)]
    for pair in range(width // LANES):
        pair_back(pair, *refs, gkt, gvt, half, minus)
    g_ref[0] = (dot(wk_ref[...], gkt[...]) + dot(wv_ref[...], gvt[...])).astype(bf16)
    gk_ref[0] = gkt[...].T
    gv_ref[0] = gvt[...].T


def attention_back(e, go, mixed, q, kc, vc, wk, wv):
    sets, rows, width = q.shape
    comp = kc.shape[1]
    outs = [
        ((rows, width), bf16),
        ((comp, width), bf16),
        ((comp, width), bf16),
        ((width, comp), bf16),
    ]
    tokens = per_set((rows, width))
    short = per_set((comp, width))
    return pl.pallas_call(
        attention_back_kernel,
        grid=(sets,),
        in_specs=[per_set(e.shape[1:])] + [tokens] * 3 + [short] * 2
        + [whole(w.shape) for w in (wk, wv)],
        out_specs=[per_set(shape) for shape, _ in outs],
        out_shape=[jax.ShapeDtypeStruct((sets,) + shape, kind) for shape, kind in outs],
        scratch_shapes=[pltpu.VMEM((width, comp), bf16)] * 2,
        compiler_params=params(),
        name="attention_back",
    )(e, go, mixed, q, kc, vc, wk, wv)


def feed_grads_kernel(hidden_ref, gup_ref, act_ref, gdown_ref, up_out, down_out):
    up_out[...] = dot_tn(hidden_ref[...], gup_ref[...]).astype(bf16)
    down_out[...] = dot_tn(act_ref[...], gdown_ref[...]).astype(bf16)


def feed_grads(hidden, gup, act, gdown):
    tokens, width = hidden.shape
    units = gup.shape[1]
    chunk = 512
    return pl.pallas_call(
        feed_grads_kernel,
        grid=(units // chunk,),
        in_specs=[
            whole((tokens, width)),
            pl.BlockSpec((tokens, chunk), lambda i: (0, i)),
            pl.BlockSpec((tokens, chunk), lambda i: (0, i)),
            whole((tokens, width)),
        ],
        out_specs=[
            pl.BlockSpec((width, chunk), lambda i: (0, i)),
            pl.BlockSpec((chunk, width), lambda i: (i, 0)),
        ],
        out_shape=[jax.ShapeDtypeStruct((width, units), bf16), jax.ShapeDtypeStruct((units, width), bf16)],
        compiler_params=params(),
        name="feed_grads",
    )(hidden, gup, act, gdown)


def square_grad_kernel(left_ref, right_ref, out_ref):
    out_ref[...] = dot_tn(left_ref[...], right_ref[...]).astype(bf16)


def square_grad(left, right):
    count, width = left.shape
    return pl.pallas_call(
        square_grad_kernel,
        grid=(1,),
        in_specs=[whole((count, width)), whole((count, width))],
        out_specs=whole((width, width)),
        out_shape=jax.ShapeDtypeStruct((width, width), bf16),
        compiler_params=params(),
        name="square_grad",
    )(left, right)


def last_kernel(kind_ref, offset_ref, table_any, x_any, g_any, gfirst_any, gq_any, wq_any, out_any, compress_ref,
                table, x, g, gfirst, gq, wq, out, total, load_sems, weight_sem, out_sems):
    sets, rows, _ = x.shape
    longest = compress_ref.shape[0]
    pairs = ((g_any, g), (x_any, x), (gq_any, gq), (table_any, table), (gfirst_any, gfirst))
    loads = [[pltpu.make_async_copy(src.at[s], dst.at[s], load_sems.at[s, i]) for i, (src, dst) in enumerate(pairs)] for s in range(sets)]
    stores = [pltpu.make_async_copy(out.at[s], out_any.at[s], out_sems.at[s]) for s in range(sets)]
    weight = pltpu.make_async_copy(wq_any, wq, weight_sem.at[0])
    for load in loads[0]:
        load.start()
    weight.start()
    for s in range(1, sets):
        for load in loads[s]:
            load.start()
    total[...] = jnp.zeros_like(total)
    weight.wait()

    def work(s, carry):
        for i, (src, dst) in enumerate(pairs):
            pltpu.make_async_copy(src.at[s], dst.at[s], load_sems.at[s, i]).wait()
        out[s] = gfirst[s].astype(f32) + (dot_nt(table[s], g[s]) + dot_nt(gq[s], wq[...]))
        pltpu.make_async_copy(out.at[s], out_any.at[s], out_sems.at[s]).start()
        terms = dot(x[s], g[s])
        begin, shift = aligned(own_start(kind_ref, offset_ref, s, rows, longest // 4))
        padded = jnp.concatenate([terms, jnp.zeros((TILE, terms.shape[1]), f32)], axis=0)
        total[pl.ds(begin, rows + TILE), :] += pltpu.roll(padded, shift, 0)
        return carry

    lax.fori_loop(0, sets, work, 0)
    compress_ref[...] = total[:longest, :].astype(compress_ref.dtype)
    for store in stores:
        store.wait()


def last(kinds, offsets, table, x, g, gfirst, gq, wq, longest, kind):
    sets, rows, width = x.shape
    comp = table.shape[2]
    anywhere, smem = pl.BlockSpec(memory_space=pl.ANY), pl.BlockSpec(memory_space=pltpu.SMEM)
    dma = lambda *n: pltpu.SemaphoreType.DMA(n)
    return pl.pallas_call(
        last_kernel,
        in_specs=[smem] * 2 + [anywhere] * 6,
        out_specs=[anywhere, pl.BlockSpec(memory_space=pltpu.VMEM)],
        out_shape=[
            jax.ShapeDtypeStruct((sets, rows, width), f32),
            jax.ShapeDtypeStruct((longest, comp), kind),
        ],
        scratch_shapes=[pltpu.VMEM(v.shape, v.dtype) for v in (table, x, g, gfirst, gq, wq)]
        + [pltpu.VMEM(x.shape, f32), pltpu.VMEM((longest + TILE, comp), f32), dma(sets, 5), dma(1), dma(sets)],
        compiler_params=params(),
        name="last",
    )(kinds, offsets, table, x, g, gfirst, gq, wq)


def finish_kernel(layer_any, table, norms, up_first, up_more, down_first, down_more, *refs):
    squares, (layer_out, table_out, up_out, down_out), outs, (held, sems) = refs[:4], refs[4:8], refs[8:-2], refs[-2:]
    sets = range(held.shape[0])
    loads = [pltpu.make_async_copy(layer_any.at[i], held.at[i], sems.at[0, i]) for i in sets]
    stores = [pltpu.make_async_copy(held.at[i], layer_out.at[i], sems.at[1, i]) for i in sets]
    for load in loads:
        load.start()
    for load, store in zip(loads, stores):
        load.wait()
        store.start()
    table_out[...] = table[...].astype(f32)
    wide, tall = up_first.shape[1], down_first.shape[0]
    up_out[:, :wide] = up_first[...]
    down_out[:tall, :] = down_first[...]
    for i in range(up_more.shape[0]):
        up_out[:, (i + 1) * wide : (i + 2) * wide] = up_more[i]
    for i in range(down_more.shape[0]):
        down_out[(i + 1) * tall : (i + 2) * tall, :] = down_more[i]
    for i in range(4):
        outs[i][...] = squares[i][...]
        outs[4 + i][...] = norms[i, :]
    for store in stores:
        store.wait()


def finish(layer_out, table, norms, up_first, up_more, down_first, down_more, squares):
    vmem, anywhere = pl.BlockSpec(memory_space=pltpu.VMEM), pl.BlockSpec(memory_space=pl.ANY)
    width = norms.shape[1]
    out = lambda *dims: jax.ShapeDtypeStruct(dims, f32)
    return pl.pallas_call(
        finish_kernel,
        in_specs=[anywhere] + [vmem] * 10,
        out_specs=[anywhere] + [vmem] * 11,
        out_shape=[
            jax.ShapeDtypeStruct(layer_out.shape, layer_out.dtype),
            out(*table.shape),
            out(up_first.shape[0], up_first.shape[1] * (1 + up_more.shape[0])),
            out(down_first.shape[0] * (1 + down_more.shape[0]), down_first.shape[1]),
        ]
        + [out(*v.shape) for v in squares]
        + [out(width)] * 4,
        scratch_shapes=[pltpu.VMEM(layer_out.shape, layer_out.dtype), pltpu.SemaphoreType.DMA((2, layer_out.shape[0]))],
        compiler_params=params(),
        name="finish",
    )(layer_out, table, norms, up_first, up_more, down_first, down_more, *squares)


def sequence_sum(part, is_long, row_count, shortest):
    seq_count = lax.axis_size("seq")
    total = lax.psum(part, "seq")
    span = shortest // row_count
    if span > 1:
        groups = [list(range(i, i + span)) for i in range(0, seq_count, span)]
        part = lax.psum(part, "seq", axis_index_groups=groups)
    return jnp.where(is_long[:, None, None], total, part)


def table_start(set_kind, row_offset, block_index, row_count, shortest):
    position = block_index * row_count
    member = position // shortest
    chosen = jnp.sum(jnp.where(jnp.arange(4)[None, :] == member, row_offset, 0), axis=1)
    return jnp.where(set_kind > 0, position, chosen + position % shortest)


def local(
    inputs, cotangent, set_kind, row_offset, query_w, key_w, value_w, output_w, up_w, down_w, compress,
    first_gain, first_bias, second_gain, second_bias,
):
    sets, rows, width = inputs.shape
    longest, comp = compress.shape
    shortest = longest // 4
    ranked = lax.axis_index("seq")
    tokens = sets * rows
    is_long = set_kind > 0
    norms = (first_gain, first_bias, second_gain, second_bias)
    linked = lax.axis_size("batch") == 8 and lax.axis_size("seq") == 4 and rows == shortest
    weights = (query_w, key_w, value_w, output_w, up_w, down_w)
    if linked:
        summed, line = inputs, lax.axis_size("seq")
    else:
        starts = table_start(set_kind, row_offset, ranked, rows, shortest).astype(jnp.int32)
        table, part, _ = front(starts, compress, inputs, query_w)
        summed, line = sequence_sum(part, is_long, rows, shortest), 0
    (kc, vc, summed, mixed, hidden, layer_out, gdown, gatt, go, new_table, queries, e, act, gup, output_part, norm_sums) = layer(
        set_kind, row_offset, compress, summed, inputs, cotangent, weights, norms, line
    )
    flat = lambda v: v.reshape(-1, v.shape[-1])
    if linked:
        gq, gk, gv, g, output_grad, up_first, down_first, up_rows, down_rows, down_last = back(
            set_kind, flat(hidden), flat(gup), flat(act), flat(gdown), output_part, e, go, mixed, queries, kc, vc, key_w, value_w
        )
        g = g.reshape(sets, width, comp)
        input_grad, compress_part = last(set_kind, row_offset, new_table, inputs, g, gatt, gq, query_w, longest, bf16)
        table_sum, norm_total, up_more, down_more, *squares = closing(
            compress_part, norm_sums, flat(inputs), flat(gq), flat(summed), flat(gk), flat(gv), up_rows, down_rows, down_last
        )
        layer_out, compress_grad, up_grad, down_grad, *rest = finish(
            layer_out, table_sum, norm_total, up_first, up_more, down_first, down_more, squares + [output_grad]
        )
        compress_grad = compress_grad.reshape(longest, comp)
        weights, norm_grads = tuple(rest[:4]) + (up_grad, down_grad), rest[4:]
    else:
        up_part, down_part = feed_grads(flat(hidden), flat(gup), flat(act), flat(gdown))
        gq, gk, gv, g_part = attention_back(e, go, mixed, queries, kc, vc, key_w, value_w)
        g = sequence_sum(g_part, is_long, rows, shortest)
        query_part = square_grad(flat(inputs), flat(gq))
        key_part = square_grad(flat(summed), flat(gk))
        value_part = square_grad(flat(summed), flat(gv))
        input_grad, compress_part = last(set_kind, row_offset, table, inputs, g, gatt, gq, query_w, longest, f32)

        def scattered(v):
            v = lax.psum_scatter(v, "seq", scatter_dimension=1, tiled=True)
            return lax.psum_scatter(v, "batch", scatter_dimension=0, tiled=True).astype(f32)

        parts = (query_part, key_part, value_part, output_part, up_part, down_part)
        weights = tuple(scattered(v) for v in parts)
        compress_grad, norm_grads = lax.psum((compress_part, norm_sums), ("batch", "seq"))
    return (layer_out, input_grad) + weights + (compress_grad,) + tuple(norm_grads[i] for i in range(4))


def solution(mesh):
    tokens = P("batch", "seq", None)
    in_specs = (tokens, tokens, P("batch"), P("batch", None)) + (P(),) * 11
    out_specs = (tokens, tokens) + (P("batch", "seq"),) * 6 + (P(),) * 5
    return jax.shard_map(local, mesh=mesh, in_specs=in_specs, out_specs=out_specs, check_vma=False)
```

```python
import functools

import jax
import jax.numpy as jnp
from jax import lax
from jax.experimental import pallas as pl
from jax.experimental.pallas import tpu as pltpu
from jax.sharding import PartitionSpec as P

DH = 64
LANES = 128
TILE = 8
SCALE = DH ** (-0.5)
EPS = 1e-05
MESH = pl.DeviceIdType.MESH
VMEM_LIMIT = 63 * 1024 * 1024
bf16 = jnp.bfloat16
f32 = jnp.float32


def dot(left, right):
    return lax.dot_general(left, right, (((1,), (0,)), ((), ())), preferred_element_type=f32)


def dot_nt(left, right):
    return lax.dot_general(left, right, (((1,), (1,)), ((), ())), preferred_element_type=f32)


def dot_tn(left, right):
    return lax.dot_general(left, right, (((0,), (0,)), ((), ())), preferred_element_type=f32)


def params(**more):
    return pltpu.CompilerParams(vmem_limit_bytes=VMEM_LIMIT, **more)


def whole(shape):
    return pl.BlockSpec(shape, lambda *_: (0,) * len(shape), pipeline_mode=pl.Buffered(1))


def per_set(shape):
    return pl.BlockSpec((1,) + tuple(shape), lambda s, *_: (s,) + (0,) * len(shape))


def own_start(kinds, offsets, at, row_count, shortest):
    position = lax.axis_index("seq") * row_count
    return jnp.where(kinds[at] > 0, position, offsets[at, position // shortest] + position % shortest)


def aligned(start):
    begin = start // TILE * TILE
    return pl.multiple_of(begin, TILE), start - begin


def place():
    batch = lax.axis_index("batch")
    return batch // 4, batch // 2 % 2, batch % 2, lax.axis_index("seq")


def device(y, x, core, z):
    return ((y * 2 + x) * 2 + core, z)


def greet(others):
    barrier = pltpu.get_barrier_semaphore()
    for other in others:
        pl.semaphore_signal(barrier, inc=1, device_id=other, device_id_type=MESH)
    pl.semaphore_wait(barrier, len(others))


def remote(src, dst, send_sem, recv_sem, target):
    return pltpu.make_async_remote_copy(src, dst, send_sem, recv_sem, device_id=target, device_id_type=MESH)


class LineSum:
    def __init__(self, line, lag, own, from_left, from_right, sems):
        y, x, core, self.z = place()
        self.line, self.lag, self.own = line, lag, own
        self.right = device(y, x, core, (self.z + 1) % line)
        self.left = device(y, x, core, (self.z + line - 1) % line)
        inner, outer = self.z > 0, self.z < line - 1
        self.ways = (
            (from_left, self.right, inner, outer, sems[0], sems[1]),
            (from_right, self.left, outer, inner, sems[2], sems[3]),
        )

    def greet(self):
        barrier = pltpu.get_barrier_semaphore()
        for way in self.ways:

            @pl.when(way[3])
            def _():
                pl.semaphore_signal(barrier, inc=1, device_id=way[1], device_id_type=MESH)

        both = jnp.logical_and(self.z > 0, self.z < self.line - 1).astype(jnp.int32)
        pl.semaphore_wait(barrier, 1 + both)

    def prepare(self):
        for way in self.ways:

            @pl.when(jnp.logical_not(way[2]))
            def _():
                way[0][...] = jnp.zeros_like(way[0])

    def copy(self, way, at):
        held, target, _, _, send, recv = way
        return remote(held.at[at], held.at[at], send.at[at], recv.at[at], target)

    def forward(self, way, at):
        @pl.when(way[2])
        def _():
            self.copy(way, at).wait_recv()

        way[0][at] = way[0][at] + self.own[at]

        @pl.when(way[3])
        def _():
            self.copy(way, at).start()

    def slots(self):
        return self.own.shape[0] + self.lag * (self.line - 1)

    def serve(self, slot):
        for way, hops in zip(self.ways, (self.z, self.line - 1 - self.z)):
            at = slot - self.lag * hops

            @pl.when(jnp.logical_and(at >= 0, at < self.own.shape[0]))
            def _():
                self.forward(way, at)

    def serve_many(self, begin, count):
        def slot(at, carry):
            self.serve(at)
            return carry

        lax.fori_loop(begin, begin + count, slot, 0)

    def total(self, at, joined):
        own = self.own[at].astype(f32)
        both = self.ways[0][0][at].astype(f32) + self.ways[1][0][at].astype(f32)
        return jnp.where(joined, both - own, own).astype(bf16)

    def finish(self):
        for way in self.ways:

            @pl.when(way[3])
            def _():
                def wait(at, carry):
                    self.copy(way, at).wait_send()
                    return carry

                lax.fori_loop(0, self.own.shape[0], wait, 0)


class Scatter:
    def __init__(self, x_first, part, from_core, from_first, from_second, send, recv):
        y, x, core, z = place()
        self.part, self.recvs = part, (from_core, from_first, from_second)
        along_x, along_y = device(y, 1 - x, core, z), device(1 - y, x, core, z)
        self.core, self.x, self.y, self.x_first = core, x, y, x_first
        if x_first:
            sources = (part.at[:, :, 1 - core], from_core.at[:, 1 - x], from_first.at[1 - y])
            targets = (device(y, x, 1 - core, z), along_x, along_y)
        else:
            sources = (part.at[:, :, 1 - core], from_core.at[1 - y], from_first.at[1 - x])
            targets = (device(y, x, 1 - core, z), along_y, along_x)
        self.copies = [
            remote(sources[i], self.recvs[i], send.at[i], recv.at[i], targets[i]) for i in range(3)
        ]

    def start(self):
        self.copies[0].start()

    def first(self):
        self.copies[0].wait()
        self.recvs[0][...] = self.recvs[0][...] + self.part[:, :, self.core]
        self.copies[1].start()

    def second(self):
        self.copies[1].wait_recv()
        kept = self.recvs[0][:, self.x] if self.x_first else self.recvs[0][self.y]
        self.recvs[1][...] = self.recvs[1][...] + kept
        self.copies[2].start()

    def done(self):
        self.copies[2].wait_recv()
        kept = self.recvs[1][self.y] if self.x_first else self.recvs[1][self.x]
        return self.recvs[2][...].astype(f32) + kept.astype(f32)

    def finish(self):
        for copy in self.copies[1:]:
            copy.wait_send()


class LineScatter:
    def __init__(self, blocks, near, far, send, recv):
        y, x, core, z = place()
        self.blocks, self.near, self.far = blocks, near, far
        self.high, self.low = z // 2, z % 2
        self.copies = [
            remote(blocks.at[:, 1 - self.low], near, send.at[0], recv.at[0], device(y, x, core, z + 1 - 2 * self.low)),
            remote(near.at[1 - self.high], far, send.at[1], recv.at[1], device(y, x, core, (z + 2) % 4)),
        ]

    def start(self):
        self.copies[0].start()

    def middle(self):
        self.copies[0].wait_recv()
        self.near[...] = self.near[...] + self.blocks[:, self.low]
        self.copies[1].start()

    def done(self):
        self.copies[1].wait_recv()
        return self.near[self.high].astype(f32) + self.far[...].astype(f32)

    def finish(self):
        for copy in self.copies:
            copy.wait_send()


def line_scatter_blocks(blocks, rows, line):
    step = rows.shape[1] // line
    for z in range(line):
        mine = rows[:, z * step : (z + 1) * step]
        if step % LANES:
            top = rows.shape[0] // 2
            mine = jnp.concatenate([mine[:top], mine[top:]], axis=1)
        blocks[z // 2, z % 2] = mine.astype(bf16)


def unfold(total, out):
    if total.shape[1] == out.shape[1]:
        out[...] = total
    else:
        top, step = total.shape[0], out.shape[1]
        out[:top, :] = total[:, :step]
        out[top:, :] = total[:, step:]


def block_shape(rows, width, line):
    step = width // line
    return (rows, step) if step % LANES == 0 else (rows // 2, step * 2)


def grad_columns(part, left, right):
    step = 2 * LANES

    def columns(j, carry):
        span = pl.ds(pl.multiple_of(j * step, LANES), step)
        part[:, span] = dot_tn(left(), right(span)).astype(bf16)
        return carry

    lax.fori_loop(0, part.shape[-1] // step, columns, 0)


def scatter_scratch(rows, width, *count):
    shapes = [(2, 2, rows, width), (2, rows, width), (rows, width)]
    return [pltpu.VMEM(count + shape, bf16) for shape in shapes] + [pltpu.SemaphoreType.DMA(count + (3,))] * 2


def line_scratch(rows, width, line):
    block = block_shape(rows, width, line)
    return [pltpu.VMEM(n + block, bf16) for n in ((2, 2), (2,), ())] + [pltpu.SemaphoreType.DMA((2,))] * 2


class Neighbours:
    def __init__(self, line):
        y, x, core, z = place()
        self.core = device(y, x, 1 - core, z)
        places = [((y + dy) % 2, (x + dx) % 2) for dy, dx in ((0, 1), (1, 0), (1, 1))]
        self.plane = [(py * 2 + px, device(py, px, core, z)) for py, px in places]
        self.line = [((z + d) % line, device(y, x, core, (z + d) % line)) for d in range(1, line)]

    def everyone(self):
        return [self.core] + [to for _, to in self.plane] + [to for _, to in self.line]


class Total:
    counts = lambda line: (2, 6, 2 * (line - 1), line - 1, 3, 1)

    def __init__(self, line, near, table, norms, table_out, norms_out, mine, from_core, from_plane, from_line, gathered,
                 core_norms, plane_norms, line_norms, *sems):
        y, x, core, z = place()
        plane = y * 2 + x
        pairs = [(sems[2 * i], sems[2 * i + 1]) for i in range(6)]
        self.running = []

        def start(stage, moves):
            send, recv = pairs[stage]
            self.running = [remote(src, dst, send.at[i], recv.at[i], to) for i, (src, dst, to) in enumerate(moves)]
            for copy in self.running:
                copy.start()

        def to_core():
            mine[...] = table[...]
            core_norms[0] = norms[...]
            start(0, [(mine.at[1 - core], from_core, near.core), (core_norms.at[0], core_norms.at[1], near.core)])

        def to_plane():
            from_core[...] = from_core[...] + mine[core]
            plane_norms[plane] = core_norms[0] + core_norms[1]
            kept = plane_norms.at[plane]
            start(1, [(from_core.at[p], from_plane.at[i], to) for i, (p, to) in enumerate(near.plane)]
                  + [(kept, kept, to) for _, to in near.plane])

        def to_line():
            total = from_core[plane].astype(f32)
            for i in range(3):
                total = total + from_plane[i].astype(f32)
            mine[0, 0] = total.astype(bf16)
            line_norms[z] = plane_norms[0] + plane_norms[1] + plane_norms[2] + plane_norms[3]
            kept = line_norms.at[z]
            start(2, [(mine.at[0, 0, p], from_line.at[i], to) for i, (p, to) in enumerate(near.line)]
                  + [(kept, kept, to) for _, to in near.line])

        def back_line():
            total = mine[0, 0, z].astype(f32)
            for i in range(line - 1):
                total = total + from_line[i].astype(f32)
            gathered[core, plane, z] = total.astype(bf16)
            all_norms = line_norms[0]
            for i in range(1, line):
                all_norms = all_norms + line_norms[i]
            norms_out[...] = all_norms
            block = gathered.at[core, plane, z]
            start(3, [(block, block, to) for _, to in near.line])

        def back_plane():
            block = gathered.at[core, plane]
            start(4, [(block, block, to) for _, to in near.plane])

        def back_core():
            block = gathered.at[core]
            start(5, [(block, block, near.core)])

        def close():
            table_out[...] = gathered[...]

        self.stages = [to_core, to_plane, to_line, back_line, back_plane, back_core, close]

    def advance(self):
        for copy in self.running:
            copy.wait()
        self.running = []
        self.stages.pop(0)()

    @staticmethod
    def scratch(line, shape, norms):
        vmem = pltpu.VMEM
        return [
            vmem(shape, bf16), vmem(shape[1:], bf16), vmem((3,) + shape[2:], bf16), vmem((line - 1,) + shape[3:], bf16),
            vmem(shape, bf16), vmem((2,) + norms, f32), vmem((4,) + norms, f32), vmem((line,) + norms, f32),
        ] + [pltpu.SemaphoreType.DMA((n,)) for n in Total.counts(line) for _ in range(2)]


def closing_kernel(line, table_ref, norms_ref, up_ref, down_ref, square_any,
                   table_out, norms_out, up_out, down_out, square_out, square_part, load_sems, *scratch):
    scratch = list(scratch)
    take = lambda n: [scratch.pop(0) for _ in range(n)]
    pairs = [(square_any.at[i], square_part.at[i]) for i in range(3)]
    loads = [pltpu.make_async_copy(src, dst, load_sems.at[i]) for i, (src, dst) in enumerate(pairs)]
    for load in loads:
        load.start()
    near = Neighbours(line)
    greet(near.everyone())
    total = Total(line, near, table_ref, norms_ref, table_out, norms_out, *take(8 + 12))
    total.advance()
    query, key, value = [Scatter(i != 1, square_part.at[i], *take(5)) for i in range(3)]
    square_lines = [LineScatter(*take(5)) for _ in range(3)]
    for load, job in zip(loads, (query, key, value)):
        load.wait()
        job.start()
    across = []
    for rows, out in ((up_ref, up_out), (down_ref, down_out)):
        for chunk in range(rows.shape[0]):
            job = LineScatter(*take(5))
            line_scatter_blocks(job.blocks, rows[chunk], line)
            job.start()
            across.append((job, out.at[chunk]))
    total.advance()
    query.first()
    key.first()
    value.first()
    for job, _ in across:
        job.middle()
    total.advance()
    query.second()
    total.advance()
    key.second()
    for job, out in across:
        unfold(job.done(), out)
    total.advance()
    value.second()
    jobs = [(job, square_lines[i], square_out.at[i]) for i, job in enumerate((query, key, value))]
    for job, line_job, _ in jobs:
        line_scatter_blocks(line_job.blocks, job.done(), line)
        line_job.start()
    total.advance()
    for _, line_job, _ in jobs:
        line_job.middle()
    total.advance()
    for _, line_job, out in jobs:
        unfold(line_job.done(), out)
    for job, _ in across:
        job.finish()
    for job, line_job, _ in jobs:
        job.finish()
        line_job.finish()


def closing(table, norms, up_rows, down_rows, squares):
    line = lax.axis_size("seq")
    longest, comp = table.shape
    shape = (2, 4, line, longest // (8 * line), comp)
    vmem, anywhere = pl.BlockSpec(memory_space=pltpu.VMEM), pl.BlockSpec(memory_space=pl.ANY)
    out = lambda *dims: jax.ShapeDtypeStruct(dims, f32)
    (ups, rows, wide), (downs, tall, width), count = up_rows.shape, down_rows.shape, squares.shape[0]
    squares = squares.reshape(count, 2, 2, 2, rows, width)
    scratch = [pltpu.VMEM(squares.shape, bf16), pltpu.SemaphoreType.DMA((count,))]
    scratch += Total.scratch(line, shape, norms.shape)
    scratch += scatter_scratch(rows, width) * count + line_scratch(rows, width, line) * count
    scratch += line_scratch(rows, wide, line) * ups + line_scratch(tall, width, line) * downs
    return pl.pallas_call(
        functools.partial(closing_kernel, line),
        in_specs=[vmem] * 4 + [anywhere],
        out_specs=[vmem] * 5,
        out_shape=[
            jax.ShapeDtypeStruct(shape, bf16), out(*norms.shape), out(ups, rows, wide // line),
            out(downs, tall, width // line), out(count, rows, width // line),
        ],
        scratch_shapes=scratch,
        compiler_params=params(collective_id=3, has_side_effects=True),
        name="closing",
    )(table.reshape(shape), norms, up_rows, down_rows, squares)


def front_kernel(start_ref, compress_ref, x_ref, wq_ref, table_ref, c_ref, q_ref, wide):
    step = pl.program_id(0)

    longest = compress_ref.shape[0]

    @pl.when(step == 0)
    def _():
        wide[:longest, :] = compress_ref[...].astype(f32)
        wide[longest:, :] = jnp.zeros((TILE, wide.shape[1]), f32)

    rows = x_ref.shape[1]
    begin, shift = aligned(start_ref[step])
    window = wide[pl.ds(begin, rows + TILE), :]
    table = pltpu.roll(window, lax.rem(rows + TILE - shift, rows + TILE), 0)[:rows].astype(bf16)
    table_ref[0] = table
    x = x_ref[0]
    c_ref[0] = dot_tn(table, x).astype(bf16)
    q_ref[0] = (dot(x, wq_ref[...]) * SCALE).astype(bf16)


def front(starts, compress, x, wq):
    sets, rows, width = x.shape
    longest, comp = compress.shape
    grid_spec = pltpu.PrefetchScalarGridSpec(
        num_scalar_prefetch=1,
        grid=(sets,),
        in_specs=[whole(compress.shape), per_set((rows, width)), whole(wq.shape)],
        out_specs=[per_set((rows, comp)), per_set((comp, width)), per_set((rows, width))],
        scratch_shapes=[pltpu.VMEM((longest + TILE, comp), f32)],
    )
    return pl.pallas_call(
        front_kernel,
        grid_spec=grid_spec,
        out_shape=[
            jax.ShapeDtypeStruct((sets, rows, comp), bf16),
            jax.ShapeDtypeStruct((sets, comp, width), bf16),
            jax.ShapeDtypeStruct((sets, rows, width), bf16),
        ],
        compiler_params=params(),
        name="front",
    )(starts, compress, x, wq)


def head_blocks(pair, first_half):
    zero = jnp.zeros_like(pair)
    return jnp.concatenate([jnp.where(first_half, pair, zero), jnp.where(first_half, zero, pair)], axis=0)


def norm_forward(v):
    average = jnp.mean(v, axis=-1, keepdims=True)
    centered = v - average
    variance = jnp.mean(centered * centered, axis=-1, keepdims=True)
    inverse = lax.rsqrt(variance + EPS)
    return centered * inverse, inverse


def norm_backward(dz, z, inverse):
    return (dz - jnp.mean(dz, axis=-1, keepdims=True) - z * jnp.mean(dz * z, axis=-1, keepdims=True)) * inverse


PIECES = 4
LAG = 2
HALVES = 2


def layer_kernel(
    line, long_ref, offset_ref, compress_ref, c_ref, x_any, cot_ref, gain1_ref, bias1_ref, gain2_ref, bias2_ref, wq_any, wk_any, wv_any, wo_any, up_any, down_any,
    kc_ref, vc_ref, csum_ref, mixed_ref, hidden_ref, out_ref, gdown_ref, gatt_ref, go_ref, table_any, q_any,
    e_any, act_any, gup_any, output_grad_ref, sums_ref,
    xs, qs, wq, wk, wv, wo, up, down, e_buf, act, gup, z_first, rinv_ref, held, output_grad, weight_sems, x_sems, out_sems,
    *linked,
):
    step = pl.program_id(0)
    last = pl.num_programs(0) - 1
    sets, rows, width = xs.shape
    comp = kc_ref.shape[1]
    units = up.shape[1]
    chunk = 768
    loads = [
        pltpu.make_async_copy(src, dst, weight_sems.at[i])
        for i, (src, dst) in enumerate(
            ((wq_any, wq), (wk_any, wk), (wv_any, wv), (wo_any, wo), (up_any, up), (down_any, down))
        )
    ]
    x_loads = [pltpu.make_async_copy(x_any.at[s], xs.at[s], x_sems.at[s]) for s in range(sets)]
    q_store = pltpu.make_async_copy(qs, q_any, out_sems.at[3])
    e_store = pltpu.make_async_copy(e_buf, e_any.at[step], out_sems.at[0])
    act_store = pltpu.make_async_copy(act, act_any.at[step], out_sems.at[1])
    gup_store = pltpu.make_async_copy(gup, gup_any.at[step], out_sems.at[2])

    if line:
        tables, own, from_left, from_right, table_sems, *sems = linked
        sums = LineSum(line, LAG, own, from_left, from_right, sems)
        ahead = PIECES + LAG * (line - 1)
        t_stores = [pltpu.make_async_copy(tables.at[s], table_any.at[s], table_sems.at[s]) for s in range(sets)]

    def first_use(load):
        @pl.when(step == 0)
        def _():
            load.wait()

    @pl.when(step == 0)
    def _():
        for load in x_loads:
            load.start()
        sums_ref[...] = jnp.zeros_like(sums_ref)
        output_grad[...] = jnp.zeros_like(output_grad)
        if line:
            longest = compress_ref.shape[0]
            sums.greet()
            sums.prepare()
            grid = (rows, rows)
            ahead_by = lax.broadcasted_iota(jnp.int32, grid, 1) - lax.broadcasted_iota(jnp.int32, grid, 0)

        def summarize(s, carry):
            pltpu.make_async_copy(x_any.at[s], xs.at[s], x_sems.at[s]).wait()

            @pl.when(s == 0)
            def _():
                loads[0].start()

            if line:
                table = jnp.zeros((rows, comp), f32)
                start = own_start(long_ref, offset_ref, s, rows, longest // 4)
                for at in range(0, longest, rows):
                    chosen = jnp.where(ahead_by == start - at, 1.0, 0.0).astype(bf16)
                    table = table + dot(chosen, compress_ref[at : at + rows, :])
                table = table.astype(bf16)
                tables[s] = table
                pltpu.make_async_copy(tables.at[s], table_any.at[s], table_sems.at[s]).start()
                c = dot_tn(table, xs[s]).astype(bf16)
                own[pl.ds(s * PIECES, PIECES)] = c.reshape(PIECES, comp // PIECES, width)
                sums.serve(s)
            return carry

        lax.fori_loop(0, sets, summarize, 0)
        for load in loads[1:]:
            load.start()
        loads[0].wait()

        def query(s, carry):
            qs[s] = (dot(xs[s], wq[...]) * SCALE).astype(bf16)
            if line:
                sums.serve(sets + s)
            return carry

        lax.fori_loop(0, sets, query, 0)
        q_store.start()
        if line:
            sums.serve_many(2 * sets, ahead - 2 * sets)

    def serve(part):
        if line:
            count = PIECES // 4

            @pl.when(step < last)
            def _():
                sums.serve_many(ahead + step * PIECES + part * count, count)

    if line:
        joined = long_ref[step] > 0
        for piece in range(PIECES):
            size = comp // PIECES
            csum_ref[0, piece * size : (piece + 1) * size, :] = sums.total(step * PIECES + piece, joined)
    else:
        csum_ref[0] = c_ref[0]
    first_use(loads[1])
    first_use(loads[2])
    c = csum_ref[0]
    kc_ref[0] = dot(c, wk[...]).astype(bf16)
    vc_ref[0] = dot(c, wv[...]).astype(bf16)
    half = lax.broadcasted_iota(jnp.int32, (comp, LANES), 1) < DH
    ones = head_blocks(jnp.ones((comp, LANES), bf16), half)

    @pl.when(step > 0)
    def _():
        e_store.wait()

    def attend(pair):
        lanes = pl.ds(pl.multiple_of(pair * LANES, LANES), LANES)
        keys = head_blocks(kc_ref[0, :, lanes], half)
        values = jnp.concatenate([head_blocks(vc_ref[0, :, lanes], half), ones], axis=1)
        scores = dot_nt(qs[step, :, lanes], keys)
        parts = []
        for head in range(2):
            mine = scores[:, head * comp : (head + 1) * comp]
            top = jnp.max(mine, axis=-1, keepdims=True)
            parts.append(jnp.exp(mine - top).astype(bf16))
        e = jnp.concatenate(parts, axis=1)
        e_buf[:, pl.ds(pl.multiple_of(pair * 2 * comp, LANES), 2 * comp)] = e
        total = dot(e, values)
        rinv = 1.0 / total[:, LANES:]
        rinv_ref[:, lanes] = rinv
        mixed_ref[0, :, lanes] = (total[:, :LANES] * rinv).astype(bf16)

    pairs = width // LANES // 2

    def some_heads(half_at, carry):
        for i in range(pairs):
            attend(half_at * pairs + i)
        return carry

    lax.fori_loop(0, 2, some_heads, 0)
    e_store.start()
    first_use(loads[3])
    serve(0)
    gain1, bias1, gain2, bias2 = (ref[...].reshape(1, width) for ref in (gain1_ref, bias1_ref, gain2_ref, bias2_ref))
    size = rows // HALVES
    halves = [pl.ds(h * size, size) for h in range(HALVES)]
    inverse1 = []
    for part in halves:
        z1, inv1 = norm_forward(xs[step, part, :].astype(f32) + dot(mixed_ref[0, part, :], wo[...]))
        inverse1.append(inv1)
        z_first[part, :] = z1
        hidden = z1 * gain1 + bias1
        hidden_ref[0, part, :] = hidden.astype(bf16)
        held[part, :] = hidden
    first_use(loads[4])
    first_use(loads[5])

    @pl.when(step > 0)
    def _():
        act_store.wait()
        gup_store.wait()

    for part in halves:
        hidden_low = hidden_ref[0, part, :]
        for at in range(0, units, chunk):
            span = pl.ds(at, chunk)
            upward = dot(hidden_low, up[:, span])
            cdf = 0.5 + 0.5 * lax.erf(upward * (0.5**0.5))
            density = jnp.exp(upward * upward * -0.5) * 0.3989422804014327
            act[part, span] = (upward * cdf).astype(bf16)
            gup[part, span] = (cdf + upward * density).astype(bf16)
    act_store.start()
    serve(1)
    sums2 = []
    for part in halves:
        z2, inv2 = norm_forward(held[part, :] + dot(act[part, :], down[...]))
        out_ref[0, part, :] = (z2 * gain2 + bias2).astype(bf16)
        dy = cot_ref[0, part, :].astype(f32)
        gsecond = norm_backward(dy * gain2, z2, inv2)
        sums2.append((jnp.sum(dy * z2, axis=0, keepdims=True), jnp.sum(dy, axis=0, keepdims=True)))
        gdown_ref[0, part, :] = gsecond.astype(bf16)
        held[part, :] = gsecond
    for part in halves:
        gdown = gdown_ref[0, part, :]
        for at in range(0, units, chunk):
            span = pl.ds(at, chunk)
            gact = dot_nt(gdown, down[span, :])
            gup[part, span] = (gact * gup[part, span].astype(f32)).astype(bf16)
    gup_store.start()
    serve(2)
    sums1 = []
    for part, inv1 in zip(halves, inverse1):
        ghidden = held[part, :] + dot_nt(gup[part, :], up[...])
        z1 = z_first[part, :]
        sums1.append((jnp.sum(ghidden * z1, axis=0, keepdims=True), jnp.sum(ghidden, axis=0, keepdims=True)))
        gatt_ref[0, part, :] = norm_backward(ghidden * gain1, z1, inv1).astype(bf16)
    for part in halves:
        go_ref[0, part, :] = (dot_nt(gatt_ref[0, part, :], wo[...]) * rinv_ref[part, :]).astype(bf16)
    output_grad[...] += dot_tn(mixed_ref[0], gatt_ref[0])
    for i, pieces in enumerate((sums1, sums2)):
        for j in range(2):
            sums_ref[2 * i + j : 2 * i + j + 1, :] += sum(piece[j] for piece in pieces)
    serve(3)

    @pl.when(step == last)
    def _():
        output_grad_ref[...] = output_grad[...].astype(bf16)
        e_store.wait()
        act_store.wait()
        gup_store.wait()
        q_store.wait()
        if line:
            for store in t_stores:
                store.wait()
            sums.finish()


def layer(set_kind, row_offset, compress, c, x, cot, weights, norms, line):
    sets, rows, width = x.shape
    longest, comp = compress.shape
    wq, wk, wv, wo, up, down = weights
    units = up.shape[1]
    tokens = per_set((rows, width))
    short = per_set((comp, width))
    anywhere = pl.BlockSpec(memory_space=pl.ANY)
    smem = pl.BlockSpec(memory_space=pltpu.SMEM)
    shape = lambda *dims, kind=bf16: jax.ShapeDtypeStruct(dims, kind)
    dma = lambda n: pltpu.SemaphoreType.DMA((n,))
    linked = []
    if line:
        count = sets * PIECES
        linked = [pltpu.VMEM((sets, rows, comp), bf16)]
        linked += [pltpu.VMEM((count, comp // PIECES, width), bf16)] * 3 + [dma(sets)] + [dma(count)] * 4
    more = dict(collective_id=0, has_side_effects=True) if line else {}
    return pl.pallas_call(
        functools.partial(layer_kernel, line),
        grid=(sets,),
        in_specs=[smem, smem, whole(compress.shape), anywhere if line else short, anywhere, tokens]
        + [whole((width,))] * 4
        + [anywhere] * 6,
        out_specs=[short] * 3 + [tokens] * 6 + [anywhere] * 5 + [whole((width, width)), whole((8, width))],
        out_shape=[shape(sets, comp, width)] * 3
        + [shape(sets, rows, width)] * 6
        + [shape(sets, rows, comp), shape(sets, rows, width)]
        + [shape(sets, rows, width // DH * comp)]
        + [shape(sets, rows, units)] * 2
        + [shape(width, width), shape(8, width, kind=f32)],
        scratch_shapes=[pltpu.VMEM(x.shape, bf16)] * 2
        + [pltpu.VMEM(w.shape, bf16) for w in weights]
        + [pltpu.VMEM((rows, width // DH * comp), bf16)]
        + [pltpu.VMEM((rows, units), bf16)] * 2
        + [pltpu.VMEM((rows, width), f32)] * 3
        + [pltpu.VMEM((width, width), f32), dma(6), dma(sets), dma(4)]
        + linked,
        compiler_params=params(**more),
        name="layer",
    )(set_kind, row_offset, compress, c, x, cot, *norms, *weights)


def pair_back(pair, e_ref, go_ref, mixed_ref, q_ref, kc_ref, vc_ref, gq_ref, gkt, gvt, half, minus):
    comp = kc_ref.shape[0]
    at = pair * LANES if isinstance(pair, int) else pl.multiple_of(pair * LANES, LANES)
    lanes = pl.ds(at, LANES)
    wide = pair * 2 * comp if isinstance(pair, int) else pl.multiple_of(pair * 2 * comp, LANES)
    e = e_ref[:, pl.ds(wide, 2 * comp)]
    keys = head_blocks(kc_ref[:, lanes], half)
    values = jnp.concatenate([head_blocks(vc_ref[:, lanes], half), minus], axis=1)
    go = go_ref[:, lanes]
    delta = (go.astype(f32) * mixed_ref[:, lanes].astype(f32)).astype(bf16)
    gp = dot_nt(jnp.concatenate([go, delta], axis=1), values)
    gs = (gp * e.astype(f32)).astype(bf16)
    gq_ref[:, lanes] = (dot(gs, keys) * SCALE).astype(bf16)
    for into, left, right in ((gkt, q_ref[:, lanes], gs), (gvt, go, e)):
        both = dot_tn(left, right)
        into[pl.ds(at, DH), :] = both[:DH, :comp].astype(bf16)
        into[pl.ds(at + DH, DH), :] = both[DH:, comp:].astype(bf16)


CHUNKS = 3
HERE = 1
BACK_PIECES = 4
BACK_LAG = 2


def back_kernel(
    line, long_ref, hidden_any, gup_any, act_any, gdown_any, output_any, e_any, go_any, mixed_any, q_any, kc_any, vc_any, wk_any, wv_any, x_any, c_any,
    gq_any, g_any, squares, output_out, up_out, down_out, up_rows, down_rows,
    hidden, gdown, feed, wk, wv, e, go, mixed, q, kc, vc, gq, gkt, gvt, gk, gv, own, from_left, from_right,
    up_part, down_part, output_part, load_sems, feed_sems, set_sems, out_sems, g_sem, late_sems, *scratch,
):
    scratch = list(scratch)
    take = lambda n: [scratch.pop(0) for _ in range(n)]
    sets, rows, width = q_any.shape
    comp = kc_any.shape[1]
    units = gup_any.shape[1]
    sums = LineSum(line, BACK_LAG, own, from_left, from_right, take(4))

    def copies(pairs, sems):
        return [pltpu.make_async_copy(src, dst, sems.at[i]) for i, (src, dst) in enumerate(pairs)]

    def feed_loads(chunk, which):
        if which == 0:
            wide, count, source = units // line, line, gup_any
        else:
            wide, count, source = units // 8, 8, act_any
        step = wide // CHUNKS
        return copies(
            [
                (source.at[:, pl.ds(pl.multiple_of(i * wide + chunk * step, LANES), step)], feed.at[which, :, pl.ds(i * step, step)])
                for i in range(count)
            ],
            feed_sems.at[which],
        )

    def set_loads(s):
        at = s % 2
        return copies(
            [(e_any.at[s], e.at[at]), (go_any.at[s], go.at[at]), (mixed_any.at[s], mixed.at[at]), (q_any.at[s], q.at[at]),
             (kc_any.at[s], kc.at[at]), (vc_any.at[s], vc.at[at])],
            set_sems.at[at],
        )

    def gq_store(s):
        return pltpu.make_async_copy(gq.at[s], gq_any.at[s], out_sems.at[s])

    def begin(some):
        for copy in some:
            copy.start()

    def end(some):
        for copy in some:
            copy.wait()

    weights = copies(((output_any, output_part), (hidden_any, hidden), (gdown_any, gdown), (wk_any, wk), (wv_any, wv)), load_sems)
    begin(weights[:1])
    begin(set_loads(0))
    begin(weights[3:])
    near = Neighbours(line)
    greet(near.everyone())
    sums.prepare()

    jobs = {"o": (Scatter(True, output_part, *take(5)), LineScatter(*take(5)), output_out)}
    lines = [LineScatter(*take(5)), LineScatter(*take(5))]
    kept = (take(5), take(5))

    def scatter_job(which, chunk):
        buffers = [ref.at[chunk] for ref in kept[which]]
        return Scatter(which == 0, (up_part, down_part)[which], *buffers)

    for chunk in range(CHUNKS):
        for which in range(2):
            if chunk < HERE:
                jobs[which, chunk] = (scatter_job(which, chunk), lines[which], (up_out, down_out)[which])
            else:
                jobs[which, chunk] = (scatter_job(which, chunk), None, (up_rows, down_rows)[which].at[chunk - HERE])

    def across(name):
        job, line_job, _ = jobs[name]
        line_scatter_blocks(line_job.blocks, job.done(), line)
        line_job.start()

    def feed_grad(which):
        if which == 0:
            up_part[...] = dot_tn(hidden[...], feed[0]).astype(bf16).reshape(up_part.shape)
        else:
            down_part[...] = dot_tn(feed[1], gdown[...]).astype(bf16).reshape(down_part.shape)

    half = lax.broadcasted_iota(jnp.int32, (comp, LANES), 1) < DH
    minus = head_blocks(jnp.full((comp, LANES), -1.0, bf16), half)

    def heads(s, pairs):
        at = s % 2
        for pair in pairs:
            pair_back(pair, e.at[at], go.at[at], mixed.at[at], q.at[at], kc.at[at], vc.at[at], gq.at[s], gkt, gvt, half, minus)

    def joins(s):
        g = dot(wk[...], gkt[...]) + dot(wv[...], gvt[...])
        own[pl.ds(s * BACK_PIECES, BACK_PIECES)] = g.astype(bf16).reshape(BACK_PIECES, width // BACK_PIECES, comp)
        gk[s] = gkt[...].T
        gv[s] = gvt[...].T
        gq_store(s).start()

    o, (u0, u1, u2), (d0, d1) = jobs["o"][0], [jobs[0, i][0] for i in range(3)], [jobs[1, i][0] for i in range(2)]
    weights[0].wait()
    o.start()

    def steps(s, by_set):
        for at, due in by_set.items():

            @pl.when(s == at)
            def _():
                for one in due:
                    one()

    def work(s, carry):
        end(set_loads(s))
        steps(s, {
            0: [lambda: begin(weights[1:2]), lambda: begin(feed_loads(0, 0))],
            1: [lambda: begin(feed_loads(1, 0)), lambda: begin(weights[2:3]), lambda: begin(feed_loads(0, 1))],
            2: [lambda: begin(feed_loads(1, 1)), lambda: begin(set_loads(3))],
            3: [lambda: begin(feed_loads(2, 0)), lambda: begin(feed_loads(2, 1))],
        })
        pairs = width // LANES // 2

        def some_heads(half_at, carry):
            heads(s, [half_at * pairs + i for i in range(pairs)])

            @pl.when(half_at == 0)
            def _():
                steps(s, {0: [o.first], 1: [u0.first], 2: [d0.first], 3: [d1.first]})

            return carry

        lax.fori_loop(0, 2, some_heads, 0)
        steps(s, {0: [lambda: end(weights[3:])], 1: [o.second], 2: [u0.second], 3: [u1.second, d0.second]})
        joins(s)
        sums.serve_many(s * BACK_PIECES, 2)

        @pl.when(s != 2)
        def _():
            chunk = s - s // 3
            end(feed_loads(chunk, 0))
            steps(s, {0: [lambda: end(weights[1:2]), lambda: begin(set_loads(1))], 1: [lambda: begin(set_loads(2))]})
            feed_grad(0)
            scatter_job(0, chunk).start()
            sums.serve_many(s * BACK_PIECES + 2, 2)

        @pl.when(s > 0)
        def _():
            end(feed_loads(s - 1, 1))
            steps(s, {1: [lambda: end(weights[2:3])]})
            feed_grad(1)

            @pl.when(s < sets - 1)
            def _():
                scatter_job(1, s - 1).start()

        steps(s, {1: [u1.first], 2: [lambda: sums.serve_many(2 * BACK_PIECES + 2, 2)], 3: [begin_late, u2.first]})
        return carry

    late = copies(((x_any, hidden), (c_any, gdown.at[: c_any.shape[0]])), late_sems)

    def begin_late():
        begin(late)

    lax.fori_loop(0, sets, work, 0)
    d2 = jobs[1, 2][0]
    d2.start()
    places = (feed.at[0, :width, :width], feed.at[0, width : 2 * width, :width], feed.at[1, :width, :width])
    flat = lambda ref, span: ref[:, :, span].reshape(-1, span.size)
    sources = ((hidden, gq), (gdown.at[: c_any.shape[0]], gk), (gdown.at[: c_any.shape[0]], gv))
    square_stores = [pltpu.make_async_copy(places[i], squares.at[i], late_sems.at[2 + i]) for i in range(3)]

    def square_grad_part(i):
        left, right = sources[i]
        grad_columns(places[i], lambda: left[...], lambda span: flat(right, span))
        square_stores[i].start()

    served = sets * BACK_PIECES
    sums.serve_many(served, 2)
    late[0].wait()
    square_grad_part(0)
    d2.first()
    d1.second()
    sums.serve_many(served + 2, 1)
    late[1].wait()
    square_grad_part(1)
    sums.serve_many(served + 3, 1)
    square_grad_part(2)
    sums.serve_many(served + 4, 1)
    u2.second()
    sums.serve_many(served + 5, sums.slots() - served - 5)
    d2.second()
    for name in ("o", (0, 0), (1, 0)):
        across(name)
    for s in range(sets):
        for piece in range(s * BACK_PIECES, (s + 1) * BACK_PIECES):
            own[piece] = sums.total(piece, long_ref[s] > 0)
    g_store = pltpu.make_async_copy(own, g_any, g_sem.at[0])
    g_store.start()
    for name in ("o", (0, 0), (1, 0)):
        jobs[name][1].middle()
    for name in jobs:
        job, line_job, out = jobs[name]
        if line_job is not None:
            unfold(line_job.done(), out)
        else:
            out[...] = job.done().astype(bf16)
    for name in jobs:
        job, line_job, _ = jobs[name]
        job.finish()
        if line_job is not None:
            line_job.finish()
    for store in square_stores:
        store.wait()
    for s in range(sets):
        gq_store(s).wait()
    g_store.wait()
    sums.finish()


def back(set_kind, hidden, gup, act, gdown, output_part, e, go, mixed, q, kc, vc, wk, wv, x, c):
    line = lax.axis_size("seq")
    sets, rows, width = q.shape
    comp = kc.shape[1]
    tokens, units = gup.shape
    eighth = width // 8
    wide, tall = units // CHUNKS, units // 8 // CHUNKS
    count = sets * BACK_PIECES
    dma = lambda *n: pltpu.SemaphoreType.DMA(n)
    vmem, anywhere = pl.BlockSpec(memory_space=pltpu.VMEM), pl.BlockSpec(memory_space=pl.ANY)
    shape = lambda *dims, kind=bf16: jax.ShapeDtypeStruct(dims, kind)
    buffer = lambda *dims, kind=bf16: pltpu.VMEM(dims, kind)
    scratch = [buffer(tokens, width)] * 2 + [buffer(2, tokens, wide)] + [buffer(width, width)] * 2
    scratch += [buffer(2, rows, e.shape[2])] + [buffer(2, rows, width)] * 3 + [buffer(2, comp, width)] * 2
    scratch += [buffer(sets, rows, width)] + [buffer(width, comp)] * 2 + [buffer(sets, comp, width)] * 2
    scratch += [buffer(count, width // BACK_PIECES, comp)] * 3
    scratch += [buffer(2, 2, 2, eighth, wide), buffer(2, 2, 2, tall, width), buffer(2, 2, 2, eighth, width)]
    scratch += [dma(5), dma(2, 8), dma(2, 6), dma(sets), dma(1), dma(5)] + [dma(count)] * 4
    scratch += scatter_scratch(eighth, width)
    for size in ((eighth, width), (eighth, wide), (tall, width)):
        scratch += line_scratch(*size, line)
    scratch += scatter_scratch(eighth, wide, CHUNKS) + scatter_scratch(tall, width, CHUNKS)
    return pl.pallas_call(
        functools.partial(back_kernel, line),
        in_specs=[pl.BlockSpec(memory_space=pltpu.SMEM)] + [anywhere] * 15,
        out_specs=[anywhere] * 3 + [vmem] * 5,
        out_shape=[
            shape(sets, rows, width),
            shape(count, width // BACK_PIECES, comp),
            shape(3, width, width),
            shape(eighth, width // line, kind=f32),
            shape(eighth, wide // line * HERE, kind=f32), shape(tall * HERE, width // line, kind=f32),
            shape(CHUNKS - HERE, eighth, wide), shape(CHUNKS - HERE, tall, width),
        ],
        scratch_shapes=scratch,
        compiler_params=params(collective_id=1, has_side_effects=True),
        name="back",
    )(set_kind, hidden, gup, act, gdown, output_part.reshape(2, 2, 2, eighth, width), e, go, mixed, q, kc, vc, wk, wv, x, c)


def attention_back_kernel(
    e_ref, go_ref, mixed_ref, q_ref, kc_ref, vc_ref, wk_ref, wv_ref,
    gq_ref, gk_ref, gv_ref, g_ref,
    gkt, gvt,
):
    width = q_ref.shape[2]
    comp = kc_ref.shape[1]
    half = lax.broadcasted_iota(jnp.int32, (comp, LANES), 1) < DH
    minus = head_blocks(jnp.full((comp, LANES), -1.0, bf16), half)
    refs = [ref.at[0] for ref in (e_ref, go_ref, mixed_ref, q_ref, kc_ref, vc_ref, gq_ref)]
    for pair in range(width // LANES):
        pair_back(pair, *refs, gkt, gvt, half, minus)
    g_ref[0] = (dot(wk_ref[...], gkt[...]) + dot(wv_ref[...], gvt[...])).astype(bf16)
    gk_ref[0] = gkt[...].T
    gv_ref[0] = gvt[...].T


def attention_back(e, go, mixed, q, kc, vc, wk, wv):
    sets, rows, width = q.shape
    comp = kc.shape[1]
    outs = [
        ((rows, width), bf16),
        ((comp, width), bf16),
        ((comp, width), bf16),
        ((width, comp), bf16),
    ]
    tokens = per_set((rows, width))
    short = per_set((comp, width))
    return pl.pallas_call(
        attention_back_kernel,
        grid=(sets,),
        in_specs=[per_set(e.shape[1:])] + [tokens] * 3 + [short] * 2
        + [whole(w.shape) for w in (wk, wv)],
        out_specs=[per_set(shape) for shape, _ in outs],
        out_shape=[jax.ShapeDtypeStruct((sets,) + shape, kind) for shape, kind in outs],
        scratch_shapes=[pltpu.VMEM((width, comp), bf16)] * 2,
        compiler_params=params(),
        name="attention_back",
    )(e, go, mixed, q, kc, vc, wk, wv)


def feed_grads_kernel(hidden_ref, gup_ref, act_ref, gdown_ref, up_out, down_out):
    up_out[...] = dot_tn(hidden_ref[...], gup_ref[...]).astype(bf16)
    down_out[...] = dot_tn(act_ref[...], gdown_ref[...]).astype(bf16)


def feed_grads(hidden, gup, act, gdown):
    tokens, width = hidden.shape
    units = gup.shape[1]
    chunk = 512
    return pl.pallas_call(
        feed_grads_kernel,
        grid=(units // chunk,),
        in_specs=[
            whole((tokens, width)),
            pl.BlockSpec((tokens, chunk), lambda i: (0, i)),
            pl.BlockSpec((tokens, chunk), lambda i: (0, i)),
            whole((tokens, width)),
        ],
        out_specs=[
            pl.BlockSpec((width, chunk), lambda i: (0, i)),
            pl.BlockSpec((chunk, width), lambda i: (i, 0)),
        ],
        out_shape=[jax.ShapeDtypeStruct((width, units), bf16), jax.ShapeDtypeStruct((units, width), bf16)],
        compiler_params=params(),
        name="feed_grads",
    )(hidden, gup, act, gdown)


def square_grad_kernel(left_ref, right_ref, out_ref):
    out_ref[...] = dot_tn(left_ref[...], right_ref[...]).astype(bf16)


def square_grad(left, right):
    count, width = left.shape
    return pl.pallas_call(
        square_grad_kernel,
        grid=(1,),
        in_specs=[whole((count, width)), whole((count, width))],
        out_specs=whole((width, width)),
        out_shape=jax.ShapeDtypeStruct((width, width), bf16),
        compiler_params=params(),
        name="square_grad",
    )(left, right)


def last_kernel(kind_ref, offset_ref, table_any, x_any, g_any, gfirst_any, gq_any, wq_any, out_any, compress_ref,
                table, x, g, gfirst, gq, wq, out, total, load_sems, weight_sem, out_sems):
    sets, rows, _ = x.shape
    longest = compress_ref.shape[0]
    pairs = ((g_any, g), (x_any, x), (gq_any, gq), (table_any, table), (gfirst_any, gfirst))
    loads = [[pltpu.make_async_copy(src.at[s], dst.at[s], load_sems.at[s, i]) for i, (src, dst) in enumerate(pairs)] for s in range(sets)]
    stores = [pltpu.make_async_copy(out.at[s], out_any.at[s], out_sems.at[s]) for s in range(sets)]
    weight = pltpu.make_async_copy(wq_any, wq, weight_sem.at[0])
    for load in loads[0]:
        load.start()
    weight.start()
    for s in range(1, sets):
        for load in loads[s]:
            load.start()
    total[...] = jnp.zeros_like(total)
    weight.wait()

    def work(s, carry):
        for i, (src, dst) in enumerate(pairs):
            pltpu.make_async_copy(src.at[s], dst.at[s], load_sems.at[s, i]).wait()
        out[s] = gfirst[s].astype(f32) + (dot_nt(table[s], g[s]) + dot_nt(gq[s], wq[...]))
        pltpu.make_async_copy(out.at[s], out_any.at[s], out_sems.at[s]).start()
        terms = dot(x[s], g[s])
        begin, shift = aligned(own_start(kind_ref, offset_ref, s, rows, longest // 4))
        padded = jnp.concatenate([terms, jnp.zeros((TILE, terms.shape[1]), f32)], axis=0)
        total[pl.ds(begin, rows + TILE), :] += pltpu.roll(padded, shift, 0)
        return carry

    lax.fori_loop(0, sets, work, 0)
    compress_ref[...] = total[:longest, :].astype(compress_ref.dtype)
    for store in stores:
        store.wait()


def last(kinds, offsets, table, x, g, gfirst, gq, wq, longest, kind):
    sets, rows, width = x.shape
    comp = table.shape[2]
    anywhere, smem = pl.BlockSpec(memory_space=pl.ANY), pl.BlockSpec(memory_space=pltpu.SMEM)
    dma = lambda *n: pltpu.SemaphoreType.DMA(n)
    return pl.pallas_call(
        last_kernel,
        in_specs=[smem] * 2 + [anywhere] * 6,
        out_specs=[anywhere, pl.BlockSpec(memory_space=pltpu.VMEM)],
        out_shape=[
            jax.ShapeDtypeStruct((sets, rows, width), f32),
            jax.ShapeDtypeStruct((longest, comp), kind),
        ],
        scratch_shapes=[pltpu.VMEM(v.shape, v.dtype) for v in (table, x, g, gfirst, gq, wq)]
        + [pltpu.VMEM(x.shape, f32), pltpu.VMEM((longest + TILE, comp), f32), dma(sets, 5), dma(1), dma(sets)],
        compiler_params=params(),
        name="last",
    )(kinds, offsets, table, x, g, gfirst, gq, wq)


def finish_kernel(layer_any, table, norms, up_first, up_more, down_first, down_more, *refs):
    (squares, output), (layer_out, table_out, up_out, down_out), outs, (held, sems) = refs[:2], refs[2:6], refs[6:-2], refs[-2:]
    sets = range(held.shape[0])
    loads = [pltpu.make_async_copy(layer_any.at[i], held.at[i], sems.at[0, i]) for i in sets]
    stores = [pltpu.make_async_copy(held.at[i], layer_out.at[i], sems.at[1, i]) for i in sets]
    for load in loads:
        load.start()
    for load, store in zip(loads, stores):
        load.wait()
        store.start()
    table_out[...] = table[...].astype(f32).reshape(table_out.shape)
    wide, tall = up_first.shape[1], down_first.shape[0]
    up_out[:, :wide] = up_first[...]
    down_out[:, :tall] = down_first[...].T
    for i in range(up_more.shape[0]):
        up_out[:, (i + 1) * wide : (i + 2) * wide] = up_more[i]
    for i in range(down_more.shape[0]):
        down_out[:, (i + 1) * tall : (i + 2) * tall] = down_more[i].T
    for i in range(4):
        outs[i][...] = squares[i] if i < 3 else output[...]
        outs[4 + i][...] = norms[i, :]
    for store in stores:
        store.wait()


def finish(layer_out, table, norms, up_first, up_more, down_first, down_more, squares, output):
    vmem, anywhere = pl.BlockSpec(memory_space=pltpu.VMEM), pl.BlockSpec(memory_space=pl.ANY)
    width = norms.shape[1]
    out = lambda *dims: jax.ShapeDtypeStruct(dims, f32)
    return pl.pallas_call(
        finish_kernel,
        in_specs=[anywhere] + [vmem] * 8,
        out_specs=[anywhere] + [vmem] * 11,
        out_shape=[
            jax.ShapeDtypeStruct(layer_out.shape, layer_out.dtype),
            out(table.size // table.shape[-1], table.shape[-1]),
            out(up_first.shape[0], up_first.shape[1] * (1 + up_more.shape[0])),
            out(down_first.shape[1], down_first.shape[0] * (1 + down_more.shape[0])),
        ]
        + [out(*output.shape)] * 4
        + [out(width)] * 4,
        scratch_shapes=[pltpu.VMEM(layer_out.shape, layer_out.dtype), pltpu.SemaphoreType.DMA((2, layer_out.shape[0]))],
        compiler_params=params(),
        name="finish",
    )(layer_out, table, norms, up_first, up_more, down_first, down_more, squares, output)


def sequence_sum(part, is_long, row_count, shortest):
    seq_count = lax.axis_size("seq")
    total = lax.psum(part, "seq")
    span = shortest // row_count
    if span > 1:
        groups = [list(range(i, i + span)) for i in range(0, seq_count, span)]
        part = lax.psum(part, "seq", axis_index_groups=groups)
    return jnp.where(is_long[:, None, None], total, part)


def table_start(set_kind, row_offset, block_index, row_count, shortest):
    position = block_index * row_count
    member = position // shortest
    chosen = jnp.sum(jnp.where(jnp.arange(4)[None, :] == member, row_offset, 0), axis=1)
    return jnp.where(set_kind > 0, position, chosen + position % shortest)


def local(
    inputs, cotangent, set_kind, row_offset, query_w, key_w, value_w, output_w, up_w, down_w, compress,
    first_gain, first_bias, second_gain, second_bias,
):
    sets, rows, width = inputs.shape
    longest, comp = compress.shape
    shortest = longest // 4
    ranked = lax.axis_index("seq")
    tokens = sets * rows
    is_long = set_kind > 0
    norms = (first_gain, first_bias, second_gain, second_bias)
    linked = lax.axis_size("batch") == 8 and lax.axis_size("seq") == 4 and rows == shortest
    weights = (query_w, key_w, value_w, output_w, up_w, down_w)
    if linked:
        summed, line = inputs, lax.axis_size("seq")
    else:
        starts = table_start(set_kind, row_offset, ranked, rows, shortest).astype(jnp.int32)
        table, part, _ = front(starts, compress, inputs, query_w)
        summed, line = sequence_sum(part, is_long, rows, shortest), 0
    (kc, vc, summed, mixed, hidden, layer_out, gdown, gatt, go, new_table, queries, e, act, gup, output_part, norm_sums) = layer(
        set_kind, row_offset, compress, summed, inputs, cotangent, weights, norms, line
    )
    flat = lambda v: v.reshape(-1, v.shape[-1])
    if linked:
        gq, g, squares, output_grad, up_first, down_first, up_rows, down_rows = back(
            set_kind, flat(hidden), flat(gup), flat(act), flat(gdown), output_part, e, go, mixed, queries, kc, vc, key_w, value_w,
            flat(inputs), flat(summed),
        )
        g = g.reshape(sets, width, comp)
        input_grad, compress_part = last(set_kind, row_offset, new_table, inputs, g, gatt, gq, query_w, longest, bf16)
        table_sum, norm_total, up_more, down_more, squares = closing(
            compress_part, norm_sums, up_rows, down_rows, squares
        )
        layer_out, compress_grad, up_grad, down_grad, *rest = finish(
            layer_out, table_sum, norm_total, up_first, up_more, down_first, down_more, squares, output_grad
        )
        weights, norm_grads = tuple(rest[:4]) + (up_grad, down_grad.T), rest[4:]
    else:
        up_part, down_part = feed_grads(flat(hidden), flat(gup), flat(act), flat(gdown))
        gq, gk, gv, g_part = attention_back(e, go, mixed, queries, kc, vc, key_w, value_w)
        g = sequence_sum(g_part, is_long, rows, shortest)
        query_part = square_grad(flat(inputs), flat(gq))
        key_part = square_grad(flat(summed), flat(gk))
        value_part = square_grad(flat(summed), flat(gv))
        input_grad, compress_part = last(set_kind, row_offset, table, inputs, g, gatt, gq, query_w, longest, f32)

        def scattered(v):
            v = lax.psum_scatter(v, "seq", scatter_dimension=1, tiled=True)
            return lax.psum_scatter(v, "batch", scatter_dimension=0, tiled=True).astype(f32)

        parts = (query_part, key_part, value_part, output_part, up_part, down_part)
        weights = tuple(scattered(v) for v in parts)
        compress_grad, norm_grads = lax.psum((compress_part, norm_sums), ("batch", "seq"))
    return (layer_out, input_grad) + weights + (compress_grad,) + tuple(norm_grads[i] for i in range(4))


def solution(mesh):
    tokens = P("batch", "seq", None)
    in_specs = (tokens, tokens, P("batch"), P("batch", None)) + (P(),) * 11
    out_specs = (tokens, tokens) + (P("batch", "seq"),) * 6 + (P(),) * 5
    return jax.shard_map(local, mesh=mesh, in_specs=in_specs, out_specs=out_specs, check_vma=False)
```

```python
import functools

import jax
import jax.numpy as jnp
from jax import lax
from jax.experimental import pallas as pl
from jax.experimental.pallas import tpu as pltpu
from jax.sharding import PartitionSpec as P

DH = 64
LANES = 128
TILE = 8
SCALE = DH ** (-0.5)
EPS = 1e-05
MESH = pl.DeviceIdType.MESH
VMEM_LIMIT = 63 * 1024 * 1024
bf16 = jnp.bfloat16
f32 = jnp.float32


def dot(left, right):
    return lax.dot_general(left, right, (((1,), (0,)), ((), ())), preferred_element_type=f32)


def dot_nt(left, right):
    return lax.dot_general(left, right, (((1,), (1,)), ((), ())), preferred_element_type=f32)


def dot_tn(left, right):
    return lax.dot_general(left, right, (((0,), (0,)), ((), ())), preferred_element_type=f32)


def params(**more):
    return pltpu.CompilerParams(vmem_limit_bytes=VMEM_LIMIT, **more)


def whole(shape):
    return pl.BlockSpec(shape, lambda *_: (0,) * len(shape), pipeline_mode=pl.Buffered(1))


def per_set(shape):
    return pl.BlockSpec((1,) + tuple(shape), lambda s, *_: (s,) + (0,) * len(shape))


def own_start(kinds, offsets, at, row_count, shortest):
    position = lax.axis_index("seq") * row_count
    return jnp.where(kinds[at] > 0, position, offsets[at, position // shortest] + position % shortest)


def aligned(start):
    begin = start // TILE * TILE
    return pl.multiple_of(begin, TILE), start - begin


def place():
    batch = lax.axis_index("batch")
    return batch // 4, batch // 2 % 2, batch % 2, lax.axis_index("seq")


def device(y, x, core, z):
    return ((y * 2 + x) * 2 + core, z)


def greet(others):
    barrier = pltpu.get_barrier_semaphore()
    for other in others:
        pl.semaphore_signal(barrier, inc=1, device_id=other, device_id_type=MESH)
    pl.semaphore_wait(barrier, len(others))


def remote(src, dst, send_sem, recv_sem, target):
    return pltpu.make_async_remote_copy(src, dst, send_sem, recv_sem, device_id=target, device_id_type=MESH)


class LineSum:
    def __init__(self, line, lag, own, from_left, from_right, sems):
        y, x, core, self.z = place()
        self.line, self.lag, self.own = line, lag, own
        self.right = device(y, x, core, (self.z + 1) % line)
        self.left = device(y, x, core, (self.z + line - 1) % line)
        inner, outer = self.z > 0, self.z < line - 1
        self.ways = (
            (from_left, self.right, inner, outer, sems[0], sems[1]),
            (from_right, self.left, outer, inner, sems[2], sems[3]),
        )

    def greet(self):
        barrier = pltpu.get_barrier_semaphore()
        for way in self.ways:

            @pl.when(way[3])
            def _():
                pl.semaphore_signal(barrier, inc=1, device_id=way[1], device_id_type=MESH)

        both = jnp.logical_and(self.z > 0, self.z < self.line - 1).astype(jnp.int32)
        pl.semaphore_wait(barrier, 1 + both)

    def prepare(self):
        for way in self.ways:

            @pl.when(jnp.logical_not(way[2]))
            def _():
                way[0][...] = jnp.zeros_like(way[0])

    def copy(self, way, at):
        held, target, _, _, send, recv = way
        return remote(held.at[at], held.at[at], send.at[at], recv.at[at], target)

    def forward(self, way, at):
        @pl.when(way[2])
        def _():
            self.copy(way, at).wait_recv()

        way[0][at] = way[0][at] + self.own[at]

        @pl.when(way[3])
        def _():
            self.copy(way, at).start()

    def slots(self):
        return self.own.shape[0] + self.lag * (self.line - 1)

    def serve(self, slot):
        for way, hops in zip(self.ways, (self.z, self.line - 1 - self.z)):
            at = slot - self.lag * hops

            @pl.when(jnp.logical_and(at >= 0, at < self.own.shape[0]))
            def _():
                self.forward(way, at)

    def serve_many(self, begin, count):
        def slot(at, carry):
            self.serve(at)
            return carry

        lax.fori_loop(begin, begin + count, slot, 0)

    def total(self, at, joined):
        own = self.own[at].astype(f32)
        both = self.ways[0][0][at].astype(f32) + self.ways[1][0][at].astype(f32)
        return jnp.where(joined, both - own, own).astype(bf16)

    def finish(self):
        for way in self.ways:

            @pl.when(way[3])
            def _():
                def wait(at, carry):
                    self.copy(way, at).wait_send()
                    return carry

                lax.fori_loop(0, self.own.shape[0], wait, 0)


class Scatter:
    def __init__(self, x_first, part, from_core, from_first, from_second, send, recv):
        y, x, core, z = place()
        self.part, self.recvs = part, (from_core, from_first, from_second)
        along_x, along_y = device(y, 1 - x, core, z), device(1 - y, x, core, z)
        self.core, self.x, self.y, self.x_first = core, x, y, x_first
        if x_first:
            sources = (part.at[:, :, 1 - core], from_core.at[:, 1 - x], from_first.at[1 - y])
            targets = (device(y, x, 1 - core, z), along_x, along_y)
        else:
            sources = (part.at[:, :, 1 - core], from_core.at[1 - y], from_first.at[1 - x])
            targets = (device(y, x, 1 - core, z), along_y, along_x)
        self.copies = [
            remote(sources[i], self.recvs[i], send.at[i], recv.at[i], targets[i]) for i in range(3)
        ]

    def start(self):
        self.copies[0].start()

    def first(self):
        self.copies[0].wait()
        self.recvs[0][...] = self.recvs[0][...] + self.part[:, :, self.core]
        self.copies[1].start()

    def second(self):
        self.copies[1].wait_recv()
        kept = self.recvs[0][:, self.x] if self.x_first else self.recvs[0][self.y]
        self.recvs[1][...] = self.recvs[1][...] + kept
        self.copies[2].start()

    def done(self):
        self.copies[2].wait_recv()
        kept = self.recvs[1][self.y] if self.x_first else self.recvs[1][self.x]
        return self.recvs[2][...].astype(f32) + kept.astype(f32)

    def finish(self):
        for copy in self.copies[1:]:
            copy.wait_send()


class LineScatter:
    def __init__(self, blocks, near, far, send, recv):
        y, x, core, z = place()
        self.blocks, self.near, self.far = blocks, near, far
        self.high, self.low = z // 2, z % 2
        self.copies = [
            remote(blocks.at[:, 1 - self.low], near, send.at[0], recv.at[0], device(y, x, core, z + 1 - 2 * self.low)),
            remote(near.at[1 - self.high], far, send.at[1], recv.at[1], device(y, x, core, (z + 2) % 4)),
        ]

    def start(self):
        self.copies[0].start()

    def middle(self):
        self.copies[0].wait_recv()
        self.near[...] = self.near[...] + self.blocks[:, self.low]
        self.copies[1].start()

    def done(self):
        self.copies[1].wait_recv()
        return self.near[self.high].astype(f32) + self.far[...].astype(f32)

    def finish(self):
        for copy in self.copies:
            copy.wait_send()


def line_scatter_blocks(blocks, rows, line):
    step = rows.shape[1] // line
    for z in range(line):
        mine = rows[:, z * step : (z + 1) * step]
        if step % LANES:
            top = rows.shape[0] // 2
            mine = jnp.concatenate([mine[:top], mine[top:]], axis=1)
        blocks[z // 2, z % 2] = mine.astype(bf16)


def unfold(total, out):
    if total.shape[1] == out.shape[1]:
        out[...] = total
    else:
        top, step = total.shape[0], out.shape[1]
        out[:top, :] = total[:, :step]
        out[top:, :] = total[:, step:]


def block_shape(rows, width, line):
    step = width // line
    return (rows, step) if step % LANES == 0 else (rows // 2, step * 2)


def grad_columns(part, left, right):
    step = 2 * LANES

    def columns(j, carry):
        span = pl.ds(pl.multiple_of(j * step, LANES), step)
        part[:, span] = dot_tn(left(), right(span)).astype(bf16)
        return carry

    lax.fori_loop(0, part.shape[-1] // step, columns, 0)


def scatter_scratch(rows, width, *count):
    shapes = [(2, 2, rows, width), (2, rows, width), (rows, width)]
    return [pltpu.VMEM(count + shape, bf16) for shape in shapes] + [pltpu.SemaphoreType.DMA(count + (3,))] * 2


def line_scratch(rows, width, line):
    block = block_shape(rows, width, line)
    return [pltpu.VMEM(n + block, bf16) for n in ((2, 2), (2,), ())] + [pltpu.SemaphoreType.DMA((2,))] * 2


class Neighbours:
    def __init__(self, line):
        y, x, core, z = place()
        self.core = device(y, x, 1 - core, z)
        places = [((y + dy) % 2, (x + dx) % 2) for dy, dx in ((0, 1), (1, 0), (1, 1))]
        self.plane = [(py * 2 + px, device(py, px, core, z)) for py, px in places]
        self.line = [((z + d) % line, device(y, x, core, (z + d) % line)) for d in range(1, line)]

    def everyone(self):
        return [self.core] + [to for _, to in self.plane] + [to for _, to in self.line]


class Total:
    counts = lambda line: (2, 6, 2 * (line - 1), line - 1, 3, 1)

    def __init__(self, line, near, table, norms, table_out, norms_out, mine, from_core, from_plane, from_line, gathered,
                 core_norms, plane_norms, line_norms, *sems):
        y, x, core, z = place()
        plane = y * 2 + x
        pairs = [(sems[2 * i], sems[2 * i + 1]) for i in range(6)]
        self.running = []

        def start(stage, moves):
            send, recv = pairs[stage]
            self.running = [remote(src, dst, send.at[i], recv.at[i], to) for i, (src, dst, to) in enumerate(moves)]
            for copy in self.running:
                copy.start()

        def to_core():
            mine[...] = table[...]
            core_norms[0] = norms[...]
            start(0, [(mine.at[1 - core], from_core, near.core), (core_norms.at[0], core_norms.at[1], near.core)])

        def to_plane():
            from_core[...] = from_core[...] + mine[core]
            plane_norms[plane] = core_norms[0] + core_norms[1]
            kept = plane_norms.at[plane]
            start(1, [(from_core.at[p], from_plane.at[i], to) for i, (p, to) in enumerate(near.plane)]
                  + [(kept, kept, to) for _, to in near.plane])

        def to_line():
            total = from_core[plane].astype(f32)
            for i in range(3):
                total = total + from_plane[i].astype(f32)
            mine[0, 0] = total.astype(bf16)
            line_norms[z] = plane_norms[0] + plane_norms[1] + plane_norms[2] + plane_norms[3]
            kept = line_norms.at[z]
            start(2, [(mine.at[0, 0, p], from_line.at[i], to) for i, (p, to) in enumerate(near.line)]
                  + [(kept, kept, to) for _, to in near.line])

        def back_line():
            total = mine[0, 0, z].astype(f32)
            for i in range(line - 1):
                total = total + from_line[i].astype(f32)
            gathered[core, plane, z] = total.astype(bf16)
            all_norms = line_norms[0]
            for i in range(1, line):
                all_norms = all_norms + line_norms[i]
            norms_out[...] = all_norms
            block = gathered.at[core, plane, z]
            start(3, [(block, block, to) for _, to in near.line])

        def back_plane():
            block = gathered.at[core, plane]
            start(4, [(block, block, to) for _, to in near.plane])

        def back_core():
            block = gathered.at[core]
            start(5, [(block, block, near.core)])

        def close():
            table_out[...] = gathered[...]

        self.stages = [to_core, to_plane, to_line, back_line, back_plane, back_core, close]

    def advance(self):
        for copy in self.running:
            copy.wait()
        self.running = []
        self.stages.pop(0)()

    @staticmethod
    def scratch(line, shape, norms):
        vmem = pltpu.VMEM
        return [
            vmem(shape, bf16), vmem(shape[1:], bf16), vmem((3,) + shape[2:], bf16), vmem((line - 1,) + shape[3:], bf16),
            vmem(shape, bf16), vmem((2,) + norms, f32), vmem((4,) + norms, f32), vmem((line,) + norms, f32),
        ] + [pltpu.SemaphoreType.DMA((n,)) for n in Total.counts(line) for _ in range(2)]


def closing_kernel(line, table_ref, norms_ref, up_ref, down_ref, square_any,
                   table_out, norms_out, up_out, down_out, square_out, square_part, load_sems, *scratch):
    scratch = list(scratch)
    take = lambda n: [scratch.pop(0) for _ in range(n)]
    pairs = [(square_any.at[i], square_part.at[i]) for i in range(3)]
    loads = [pltpu.make_async_copy(src, dst, load_sems.at[i]) for i, (src, dst) in enumerate(pairs)]
    for load in loads:
        load.start()
    near = Neighbours(line)
    greet(near.everyone())
    total = Total(line, near, table_ref, norms_ref, table_out, norms_out, *take(8 + 12))
    total.advance()
    query, key, value = [Scatter(i != 1, square_part.at[i], *take(5)) for i in range(3)]
    square_lines = [LineScatter(*take(5)) for _ in range(3)]
    for load, job in zip(loads, (query, key, value)):
        load.wait()
        job.start()
    across = []
    for rows, out in ((up_ref, up_out), (down_ref, down_out)):
        for chunk in range(rows.shape[0]):
            job = LineScatter(*take(5))
            line_scatter_blocks(job.blocks, rows[chunk], line)
            job.start()
            across.append((job, out.at[chunk]))
    total.advance()
    query.first()
    key.first()
    value.first()
    for job, _ in across:
        job.middle()
    total.advance()
    query.second()
    key.second()
    total.advance()
    for job, out in across:
        unfold(job.done(), out)
    value.second()
    total.advance()
    jobs = [(job, square_lines[i], square_out.at[i]) for i, job in enumerate((query, key, value))]
    for job, line_job, _ in jobs:
        line_scatter_blocks(line_job.blocks, job.done(), line)
        line_job.start()
    total.advance()
    for _, line_job, _ in jobs:
        line_job.middle()
    total.advance()
    for _, line_job, out in jobs:
        unfold(line_job.done(), out)
    for job, _ in across:
        job.finish()
    for job, line_job, _ in jobs:
        job.finish()
        line_job.finish()


def closing(table, norms, up_rows, down_rows, squares):
    line = lax.axis_size("seq")
    longest, comp = table.shape
    shape = (2, 4, line, longest // (8 * line), comp)
    vmem, anywhere = pl.BlockSpec(memory_space=pltpu.VMEM), pl.BlockSpec(memory_space=pl.ANY)
    out = lambda *dims: jax.ShapeDtypeStruct(dims, f32)
    (ups, rows, wide), (downs, tall, width), count = up_rows.shape, down_rows.shape, squares.shape[0]
    squares = squares.reshape(count, 2, 2, 2, rows, width)
    scratch = [pltpu.VMEM(squares.shape, bf16), pltpu.SemaphoreType.DMA((count,))]
    scratch += Total.scratch(line, shape, norms.shape)
    scratch += scatter_scratch(rows, width) * count + line_scratch(rows, width, line) * count
    scratch += line_scratch(rows, wide, line) * ups + line_scratch(tall, width, line) * downs
    return pl.pallas_call(
        functools.partial(closing_kernel, line),
        in_specs=[vmem] * 4 + [anywhere],
        out_specs=[vmem] * 5,
        out_shape=[
            jax.ShapeDtypeStruct(shape, bf16), out(*norms.shape), out(ups, rows, wide // line),
            out(downs, tall, width // line), out(count, rows, width // line),
        ],
        scratch_shapes=scratch,
        compiler_params=params(collective_id=3, has_side_effects=True),
        name="closing",
    )(table.reshape(shape), norms, up_rows, down_rows, squares)


def front_kernel(start_ref, compress_ref, x_ref, wq_ref, table_ref, c_ref, q_ref, wide):
    step = pl.program_id(0)

    longest = compress_ref.shape[0]

    @pl.when(step == 0)
    def _():
        wide[:longest, :] = compress_ref[...].astype(f32)
        wide[longest:, :] = jnp.zeros((TILE, wide.shape[1]), f32)

    rows = x_ref.shape[1]
    begin, shift = aligned(start_ref[step])
    window = wide[pl.ds(begin, rows + TILE), :]
    table = pltpu.roll(window, lax.rem(rows + TILE - shift, rows + TILE), 0)[:rows].astype(bf16)
    table_ref[0] = table
    x = x_ref[0]
    c_ref[0] = dot_tn(table, x).astype(bf16)
    q_ref[0] = (dot(x, wq_ref[...]) * SCALE).astype(bf16)


def front(starts, compress, x, wq):
    sets, rows, width = x.shape
    longest, comp = compress.shape
    grid_spec = pltpu.PrefetchScalarGridSpec(
        num_scalar_prefetch=1,
        grid=(sets,),
        in_specs=[whole(compress.shape), per_set((rows, width)), whole(wq.shape)],
        out_specs=[per_set((rows, comp)), per_set((comp, width)), per_set((rows, width))],
        scratch_shapes=[pltpu.VMEM((longest + TILE, comp), f32)],
    )
    return pl.pallas_call(
        front_kernel,
        grid_spec=grid_spec,
        out_shape=[
            jax.ShapeDtypeStruct((sets, rows, comp), bf16),
            jax.ShapeDtypeStruct((sets, comp, width), bf16),
            jax.ShapeDtypeStruct((sets, rows, width), bf16),
        ],
        compiler_params=params(),
        name="front",
    )(starts, compress, x, wq)


def head_blocks(pair, first_half):
    zero = jnp.zeros_like(pair)
    return jnp.concatenate([jnp.where(first_half, pair, zero), jnp.where(first_half, zero, pair)], axis=0)


def norm_forward(v):
    average = jnp.mean(v, axis=-1, keepdims=True)
    centered = v - average
    variance = jnp.mean(centered * centered, axis=-1, keepdims=True)
    inverse = lax.rsqrt(variance + EPS)
    return centered * inverse, inverse


def norm_backward(dz, z, inverse):
    return (dz - jnp.mean(dz, axis=-1, keepdims=True) - z * jnp.mean(dz * z, axis=-1, keepdims=True)) * inverse


PIECES = 4
LAG = 2
HALVES = 2


def layer_kernel(
    line, long_ref, offset_ref, compress_ref, c_ref, x_any, cot_ref, gain1_ref, bias1_ref, gain2_ref, bias2_ref, wq_any, wk_any, wv_any, wo_any, up_any, down_any,
    kc_ref, vc_ref, csum_ref, mixed_ref, hidden_ref, out_ref, gdown_ref, gatt_ref, go_ref, table_any, q_any,
    e_any, act_any, gup_any, output_grad_ref, sums_ref,
    xs, qs, wq, wk, wv, wo, up, down, e_buf, act, gup, z_first, rinv_ref, held, output_grad, weight_sems, x_sems, out_sems,
    *linked,
):
    step = pl.program_id(0)
    last = pl.num_programs(0) - 1
    sets, rows, width = xs.shape
    comp = kc_ref.shape[1]
    units = up.shape[1]
    chunk = 768
    loads = [
        pltpu.make_async_copy(src, dst, weight_sems.at[i])
        for i, (src, dst) in enumerate(
            ((wq_any, wq), (wk_any, wk), (wv_any, wv), (wo_any, wo), (up_any, up), (down_any, down))
        )
    ]
    x_loads = [pltpu.make_async_copy(x_any.at[s], xs.at[s], x_sems.at[s]) for s in range(sets)]
    q_store = pltpu.make_async_copy(qs, q_any, out_sems.at[3])
    e_store = pltpu.make_async_copy(e_buf, e_any.at[step], out_sems.at[0])
    act_store = pltpu.make_async_copy(act, act_any.at[step], out_sems.at[1])
    gup_store = pltpu.make_async_copy(gup, gup_any.at[step], out_sems.at[2])

    if line:
        tables, own, from_left, from_right, table_sems, *sems = linked
        sums = LineSum(line, LAG, own, from_left, from_right, sems)
        ahead = PIECES + LAG * (line - 1)
        t_stores = [pltpu.make_async_copy(tables.at[s], table_any.at[s], table_sems.at[s]) for s in range(sets)]

    def first_use(load):
        @pl.when(step == 0)
        def _():
            load.wait()

    @pl.when(step == 0)
    def _():
        for load in x_loads:
            load.start()
        sums_ref[...] = jnp.zeros_like(sums_ref)
        output_grad[...] = jnp.zeros_like(output_grad)
        if line:
            longest = compress_ref.shape[0]
            sums.greet()
            sums.prepare()
            grid = (rows, rows)
            ahead_by = lax.broadcasted_iota(jnp.int32, grid, 1) - lax.broadcasted_iota(jnp.int32, grid, 0)

        def summarize(s, carry):
            pltpu.make_async_copy(x_any.at[s], xs.at[s], x_sems.at[s]).wait()

            @pl.when(s == 0)
            def _():
                loads[0].start()

            if line:
                table = jnp.zeros((rows, comp), f32)
                start = own_start(long_ref, offset_ref, s, rows, longest // 4)
                for at in range(0, longest, rows):
                    chosen = jnp.where(ahead_by == start - at, 1.0, 0.0).astype(bf16)
                    table = table + dot(chosen, compress_ref[at : at + rows, :])
                table = table.astype(bf16)
                tables[s] = table
                pltpu.make_async_copy(tables.at[s], table_any.at[s], table_sems.at[s]).start()
                c = dot_tn(table, xs[s]).astype(bf16)
                own[pl.ds(s * PIECES, PIECES)] = c.reshape(PIECES, comp // PIECES, width)
                sums.serve(s)
            return carry

        lax.fori_loop(0, sets, summarize, 0)
        for load in loads[1:]:
            load.start()
        loads[0].wait()

        def query(s, carry):
            qs[s] = (dot(xs[s], wq[...]) * SCALE).astype(bf16)
            if line:
                sums.serve(sets + s)
            return carry

        lax.fori_loop(0, sets, query, 0)
        q_store.start()
        if line:
            sums.serve_many(2 * sets, ahead - 2 * sets)

    def serve(part):
        if line:
            count = PIECES // 4

            @pl.when(step < last)
            def _():
                sums.serve_many(ahead + step * PIECES + part * count, count)

    if line:
        joined = long_ref[step] > 0
        for piece in range(PIECES):
            size = comp // PIECES
            csum_ref[0, piece * size : (piece + 1) * size, :] = sums.total(step * PIECES + piece, joined)
    else:
        csum_ref[0] = c_ref[0]
    first_use(loads[1])
    first_use(loads[2])
    c = csum_ref[0]
    kc_ref[0] = dot(c, wk[...]).astype(bf16)
    vc_ref[0] = dot(c, wv[...]).astype(bf16)
    half = lax.broadcasted_iota(jnp.int32, (comp, LANES), 1) < DH
    ones = head_blocks(jnp.ones((comp, LANES), bf16), half)

    @pl.when(step > 0)
    def _():
        e_store.wait()

    def attend(pair):
        lanes = pl.ds(pl.multiple_of(pair * LANES, LANES), LANES)
        keys = head_blocks(kc_ref[0, :, lanes], half)
        values = jnp.concatenate([head_blocks(vc_ref[0, :, lanes], half), ones], axis=1)
        scores = dot_nt(qs[step, :, lanes], keys)
        parts = []
        for head in range(2):
            mine = scores[:, head * comp : (head + 1) * comp]
            top = jnp.max(mine, axis=-1, keepdims=True)
            parts.append(jnp.exp(mine - top).astype(bf16))
        e = jnp.concatenate(parts, axis=1)
        e_buf[:, pl.ds(pl.multiple_of(pair * 2 * comp, LANES), 2 * comp)] = e
        total = dot(e, values)
        rinv = 1.0 / total[:, LANES:]
        rinv_ref[:, lanes] = rinv
        mixed_ref[0, :, lanes] = (total[:, :LANES] * rinv).astype(bf16)

    pairs = width // LANES // 2

    def some_heads(half_at, carry):
        for i in range(pairs):
            attend(half_at * pairs + i)
        return carry

    lax.fori_loop(0, 2, some_heads, 0)
    e_store.start()
    first_use(loads[3])
    serve(0)
    gain1, bias1, gain2, bias2 = (ref[...].reshape(1, width) for ref in (gain1_ref, bias1_ref, gain2_ref, bias2_ref))
    size = rows // HALVES
    halves = [pl.ds(h * size, size) for h in range(HALVES)]
    inverse1 = []
    for part in halves:
        z1, inv1 = norm_forward(xs[step, part, :].astype(f32) + dot(mixed_ref[0, part, :], wo[...]))
        inverse1.append(inv1)
        z_first[part, :] = z1
        hidden = z1 * gain1 + bias1
        hidden_ref[0, part, :] = hidden.astype(bf16)
        held[part, :] = hidden
    first_use(loads[4])
    first_use(loads[5])

    @pl.when(step > 0)
    def _():
        act_store.wait()
        gup_store.wait()

    for part in halves:
        hidden_low = hidden_ref[0, part, :]
        for at in range(0, units, chunk):
            span = pl.ds(at, chunk)
            upward = dot(hidden_low, up[:, span])
            cdf = 0.5 + 0.5 * lax.erf(upward * (0.5**0.5))
            density = jnp.exp(upward * upward * -0.5) * 0.3989422804014327
            act[part, span] = (upward * cdf).astype(bf16)
            gup[part, span] = (cdf + upward * density).astype(bf16)
    act_store.start()
    serve(1)
    sums2 = []
    for part in halves:
        z2, inv2 = norm_forward(held[part, :] + dot(act[part, :], down[...]))
        out_ref[0, part, :] = (z2 * gain2 + bias2).astype(bf16)
        dy = cot_ref[0, part, :].astype(f32)
        gsecond = norm_backward(dy * gain2, z2, inv2)
        sums2.append((jnp.sum(dy * z2, axis=0, keepdims=True), jnp.sum(dy, axis=0, keepdims=True)))
        gdown_ref[0, part, :] = gsecond.astype(bf16)
        held[part, :] = gsecond
    for part in halves:
        gdown = gdown_ref[0, part, :]
        for at in range(0, units, chunk):
            span = pl.ds(at, chunk)
            gact = dot_nt(gdown, down[span, :])
            gup[part, span] = (gact * gup[part, span].astype(f32)).astype(bf16)
    gup_store.start()
    serve(2)
    sums1 = []
    for part, inv1 in zip(halves, inverse1):
        ghidden = held[part, :] + dot_nt(gup[part, :], up[...])
        z1 = z_first[part, :]
        sums1.append((jnp.sum(ghidden * z1, axis=0, keepdims=True), jnp.sum(ghidden, axis=0, keepdims=True)))
        gatt_ref[0, part, :] = norm_backward(ghidden * gain1, z1, inv1).astype(bf16)
    for part in halves:
        go_ref[0, part, :] = (dot_nt(gatt_ref[0, part, :], wo[...]) * rinv_ref[part, :]).astype(bf16)
    output_grad[...] += dot_tn(mixed_ref[0], gatt_ref[0])
    for i, pieces in enumerate((sums1, sums2)):
        for j in range(2):
            sums_ref[2 * i + j : 2 * i + j + 1, :] += sum(piece[j] for piece in pieces)
    serve(3)

    @pl.when(step == last)
    def _():
        output_grad_ref[...] = output_grad[...].astype(bf16)
        e_store.wait()
        act_store.wait()
        gup_store.wait()
        q_store.wait()
        if line:
            for store in t_stores:
                store.wait()
            sums.finish()


def layer(set_kind, row_offset, compress, c, x, cot, weights, norms, line):
    sets, rows, width = x.shape
    longest, comp = compress.shape
    wq, wk, wv, wo, up, down = weights
    units = up.shape[1]
    tokens = per_set((rows, width))
    short = per_set((comp, width))
    anywhere = pl.BlockSpec(memory_space=pl.ANY)
    smem = pl.BlockSpec(memory_space=pltpu.SMEM)
    shape = lambda *dims, kind=bf16: jax.ShapeDtypeStruct(dims, kind)
    dma = lambda n: pltpu.SemaphoreType.DMA((n,))
    linked = []
    if line:
        count = sets * PIECES
        linked = [pltpu.VMEM((sets, rows, comp), bf16)]
        linked += [pltpu.VMEM((count, comp // PIECES, width), bf16)] * 3 + [dma(sets)] + [dma(count)] * 4
    more = dict(collective_id=0, has_side_effects=True) if line else {}
    return pl.pallas_call(
        functools.partial(layer_kernel, line),
        grid=(sets,),
        in_specs=[smem, smem, whole(compress.shape), anywhere if line else short, anywhere, tokens]
        + [whole((width,))] * 4
        + [anywhere] * 6,
        out_specs=[short] * 3 + [tokens] * 6 + [anywhere] * 5 + [whole((width, width)), whole((8, width))],
        out_shape=[shape(sets, comp, width)] * 3
        + [shape(sets, rows, width)] * 6
        + [shape(sets, rows, comp), shape(sets, rows, width)]
        + [shape(sets, rows, width // DH * comp)]
        + [shape(sets, rows, units)] * 2
        + [shape(width, width), shape(8, width, kind=f32)],
        scratch_shapes=[pltpu.VMEM(x.shape, bf16)] * 2
        + [pltpu.VMEM(w.shape, bf16) for w in weights]
        + [pltpu.VMEM((rows, width // DH * comp), bf16)]
        + [pltpu.VMEM((rows, units), bf16)] * 2
        + [pltpu.VMEM((rows, width), f32)] * 3
        + [pltpu.VMEM((width, width), f32), dma(6), dma(sets), dma(4)]
        + linked,
        compiler_params=params(**more),
        name="layer",
    )(set_kind, row_offset, compress, c, x, cot, *norms, *weights)


def pair_back(pair, e_ref, go_ref, mixed_ref, q_ref, kc_ref, vc_ref, gq_ref, gkt, gvt, half, minus):
    comp = kc_ref.shape[0]
    at = pair * LANES if isinstance(pair, int) else pl.multiple_of(pair * LANES, LANES)
    lanes = pl.ds(at, LANES)
    wide = pair * 2 * comp if isinstance(pair, int) else pl.multiple_of(pair * 2 * comp, LANES)
    e = e_ref[:, pl.ds(wide, 2 * comp)]
    keys = head_blocks(kc_ref[:, lanes], half)
    values = jnp.concatenate([head_blocks(vc_ref[:, lanes], half), minus], axis=1)
    go = go_ref[:, lanes]
    delta = (go.astype(f32) * mixed_ref[:, lanes].astype(f32)).astype(bf16)
    gp = dot_nt(jnp.concatenate([go, delta], axis=1), values)
    gs = (gp * e.astype(f32)).astype(bf16)
    gq_ref[:, lanes] = (dot(gs, keys) * SCALE).astype(bf16)
    for into, left, right in ((gkt, q_ref[:, lanes], gs), (gvt, go, e)):
        both = dot_tn(left, right)
        into[pl.ds(at, DH), :] = both[:DH, :comp].astype(bf16)
        into[pl.ds(at + DH, DH), :] = both[DH:, comp:].astype(bf16)


CHUNKS = 3
HERE = 1
BACK_PIECES = 4
BACK_LAG = 2


def back_kernel(
    line, long_ref, hidden_any, gup_any, act_any, gdown_any, output_any, e_any, go_any, mixed_any, q_any, kc_any, vc_any, wk_any, wv_any, x_any, c_any,
    gq_any, g_any, squares, output_out, up_out, down_out, up_rows, down_rows,
    hidden, gdown, feed, wk, wv, e, go, mixed, q, kc, vc, gq, gkt, gvt, gk, gv, own, from_left, from_right,
    up_part, down_part, output_part, load_sems, feed_sems, set_sems, out_sems, g_sem, late_sems, *scratch,
):
    scratch = list(scratch)
    take = lambda n: [scratch.pop(0) for _ in range(n)]
    sets, rows, width = q_any.shape
    comp = kc_any.shape[1]
    units = gup_any.shape[1]
    sums = LineSum(line, BACK_LAG, own, from_left, from_right, take(4))

    def copies(pairs, sems):
        return [pltpu.make_async_copy(src, dst, sems.at[i]) for i, (src, dst) in enumerate(pairs)]

    def feed_loads(chunk, which):
        if which == 0:
            wide, count, source = units // line, line, gup_any
        else:
            wide, count, source = units // 8, 8, act_any
        step = wide // CHUNKS
        return copies(
            [
                (source.at[:, pl.ds(pl.multiple_of(i * wide + chunk * step, LANES), step)], feed.at[which, :, pl.ds(i * step, step)])
                for i in range(count)
            ],
            feed_sems.at[which],
        )

    def set_loads(s):
        at = s % 2
        return copies(
            [(e_any.at[s], e.at[at]), (go_any.at[s], go.at[at]), (mixed_any.at[s], mixed.at[at]), (q_any.at[s], q.at[at]),
             (kc_any.at[s], kc.at[at]), (vc_any.at[s], vc.at[at])],
            set_sems.at[at],
        )

    def gq_store(s):
        return pltpu.make_async_copy(gq.at[s], gq_any.at[s], out_sems.at[s])

    def begin(some):
        for copy in some:
            copy.start()

    def end(some):
        for copy in some:
            copy.wait()

    weights = copies(((output_any, output_part), (hidden_any, hidden), (gdown_any, gdown), (wk_any, wk), (wv_any, wv)), load_sems)
    begin(weights[:1])
    begin(set_loads(0))
    begin(weights[3:])
    near = Neighbours(line)
    greet(near.everyone())
    sums.prepare()

    jobs = {"o": (Scatter(True, output_part, *take(5)), LineScatter(*take(5)), output_out)}
    lines = [LineScatter(*take(5)), LineScatter(*take(5))]
    kept = (take(5), take(5))

    def scatter_job(which, chunk):
        buffers = [ref.at[chunk] for ref in kept[which]]
        return Scatter(which == 0, (up_part, down_part)[which], *buffers)

    for chunk in range(CHUNKS):
        for which in range(2):
            if chunk < HERE:
                jobs[which, chunk] = (scatter_job(which, chunk), lines[which], (up_out, down_out)[which])
            else:
                jobs[which, chunk] = (scatter_job(which, chunk), None, (up_rows, down_rows)[which].at[chunk - HERE])

    def across(name):
        job, line_job, _ = jobs[name]
        line_scatter_blocks(line_job.blocks, job.done(), line)
        line_job.start()

    def feed_grad(which):
        if which == 0:
            up_part[...] = dot_tn(hidden[...], feed[0]).astype(bf16).reshape(up_part.shape)
        else:
            down_part[...] = dot_tn(feed[1], gdown[...]).astype(bf16).reshape(down_part.shape)

    half = lax.broadcasted_iota(jnp.int32, (comp, LANES), 1) < DH
    minus = head_blocks(jnp.full((comp, LANES), -1.0, bf16), half)

    def heads(s, pairs):
        at = s % 2
        for pair in pairs:
            pair_back(pair, e.at[at], go.at[at], mixed.at[at], q.at[at], kc.at[at], vc.at[at], gq.at[s], gkt, gvt, half, minus)

    def joins(s):
        g = dot(wk[...], gkt[...]) + dot(wv[...], gvt[...])
        own[pl.ds(s * BACK_PIECES, BACK_PIECES)] = g.astype(bf16).reshape(BACK_PIECES, width // BACK_PIECES, comp)
        gk[s] = gkt[...].T
        gv[s] = gvt[...].T
        gq_store(s).start()

    o, (u0, u1, u2), (d0, d1) = jobs["o"][0], [jobs[0, i][0] for i in range(3)], [jobs[1, i][0] for i in range(2)]
    weights[0].wait()
    o.start()

    def steps(s, by_set):
        for at, due in by_set.items():

            @pl.when(s == at)
            def _():
                for one in due:
                    one()

    def work(s, carry):
        end(set_loads(s))
        steps(s, {
            0: [lambda: begin(weights[1:2]), lambda: begin(feed_loads(0, 0))],
            1: [lambda: begin(feed_loads(1, 0)), lambda: begin(weights[2:3]), lambda: begin(feed_loads(0, 1))],
            2: [lambda: begin(feed_loads(1, 1)), lambda: begin(set_loads(3))],
            3: [lambda: begin(feed_loads(2, 0)), lambda: begin(feed_loads(2, 1))],
        })
        pairs = width // LANES // 2

        def some_heads(half_at, carry):
            heads(s, [half_at * pairs + i for i in range(pairs)])

            @pl.when(half_at == 0)
            def _():
                steps(s, {0: [o.first], 1: [u0.first], 2: [d0.first], 3: [d1.first]})

            return carry

        lax.fori_loop(0, 2, some_heads, 0)
        steps(s, {0: [lambda: end(weights[3:])], 1: [o.second], 2: [u0.second], 3: [u1.second, d0.second]})
        joins(s)
        sums.serve_many(s * BACK_PIECES, 2)

        @pl.when(s != 2)
        def _():
            chunk = s - s // 3
            end(feed_loads(chunk, 0))
            steps(s, {0: [lambda: end(weights[1:2]), lambda: begin(set_loads(1))], 1: [lambda: begin(set_loads(2))]})
            feed_grad(0)
            scatter_job(0, chunk).start()
            sums.serve_many(s * BACK_PIECES + 2, 2)

        @pl.when(s > 0)
        def _():
            end(feed_loads(s - 1, 1))
            steps(s, {1: [lambda: end(weights[2:3])]})
            feed_grad(1)

            @pl.when(s < sets - 1)
            def _():
                scatter_job(1, s - 1).start()

        steps(s, {1: [u1.first], 2: [lambda: sums.serve_many(2 * BACK_PIECES + 2, 2)], 3: [begin_late, u2.first]})
        return carry

    late = copies(((x_any, hidden), (c_any, gdown.at[: c_any.shape[0]])), late_sems)

    def begin_late():
        begin(late)

    lax.fori_loop(0, sets, work, 0)
    d2 = jobs[1, 2][0]
    d2.start()
    places = (feed.at[0, :width, :width], feed.at[0, width : 2 * width, :width], feed.at[1, :width, :width])
    flat = lambda ref, span: ref[:, :, span].reshape(-1, span.size)
    sources = ((hidden, gq), (gdown.at[: c_any.shape[0]], gk), (gdown.at[: c_any.shape[0]], gv))
    square_stores = [pltpu.make_async_copy(places[i], squares.at[i], late_sems.at[2 + i]) for i in range(3)]

    def square_grad_part(i):
        left, right = sources[i]
        grad_columns(places[i], lambda: left[...], lambda span: flat(right, span))
        square_stores[i].start()

    served = sets * BACK_PIECES
    sums.serve_many(served, 2)
    late[0].wait()
    square_grad_part(0)
    d2.first()
    d1.second()
    sums.serve_many(served + 2, 1)
    late[1].wait()
    square_grad_part(1)
    sums.serve_many(served + 3, 1)
    square_grad_part(2)
    sums.serve_many(served + 4, 1)
    u2.second()
    sums.serve_many(served + 5, sums.slots() - served - 5)
    d2.second()
    for name in ("o", (0, 0), (1, 0)):
        across(name)
    for s in range(sets):
        for piece in range(s * BACK_PIECES, (s + 1) * BACK_PIECES):
            own[piece] = sums.total(piece, long_ref[s] > 0)
    g_store = pltpu.make_async_copy(own, g_any, g_sem.at[0])
    g_store.start()
    for name in ("o", (0, 0), (1, 0)):
        jobs[name][1].middle()
    for name in jobs:
        job, line_job, out = jobs[name]
        if line_job is not None:
            unfold(line_job.done(), out)
        else:
            out[...] = job.done().astype(bf16)
    for name in jobs:
        job, line_job, _ = jobs[name]
        job.finish()
        if line_job is not None:
            line_job.finish()
    for store in square_stores:
        store.wait()
    for s in range(sets):
        gq_store(s).wait()
    g_store.wait()
    sums.finish()


def back(set_kind, hidden, gup, act, gdown, output_part, e, go, mixed, q, kc, vc, wk, wv, x, c):
    line = lax.axis_size("seq")
    sets, rows, width = q.shape
    comp = kc.shape[1]
    tokens, units = gup.shape
    eighth = width // 8
    wide, tall = units // CHUNKS, units // 8 // CHUNKS
    count = sets * BACK_PIECES
    dma = lambda *n: pltpu.SemaphoreType.DMA(n)
    vmem, anywhere = pl.BlockSpec(memory_space=pltpu.VMEM), pl.BlockSpec(memory_space=pl.ANY)
    shape = lambda *dims, kind=bf16: jax.ShapeDtypeStruct(dims, kind)
    buffer = lambda *dims, kind=bf16: pltpu.VMEM(dims, kind)
    scratch = [buffer(tokens, width)] * 2 + [buffer(2, tokens, wide)] + [buffer(width, width)] * 2
    scratch += [buffer(2, rows, e.shape[2])] + [buffer(2, rows, width)] * 3 + [buffer(2, comp, width)] * 2
    scratch += [buffer(sets, rows, width)] + [buffer(width, comp)] * 2 + [buffer(sets, comp, width)] * 2
    scratch += [buffer(count, width // BACK_PIECES, comp)] * 3
    scratch += [buffer(2, 2, 2, eighth, wide), buffer(2, 2, 2, tall, width), buffer(2, 2, 2, eighth, width)]
    scratch += [dma(5), dma(2, 8), dma(2, 6), dma(sets), dma(1), dma(5)] + [dma(count)] * 4
    scratch += scatter_scratch(eighth, width)
    for size in ((eighth, width), (eighth, wide), (tall, width)):
        scratch += line_scratch(*size, line)
    scratch += scatter_scratch(eighth, wide, CHUNKS) + scatter_scratch(tall, width, CHUNKS)
    return pl.pallas_call(
        functools.partial(back_kernel, line),
        in_specs=[pl.BlockSpec(memory_space=pltpu.SMEM)] + [anywhere] * 15,
        out_specs=[anywhere] * 3 + [vmem] * 5,
        out_shape=[
            shape(sets, rows, width),
            shape(count, width // BACK_PIECES, comp),
            shape(3, width, width),
            shape(eighth, width // line, kind=f32),
            shape(eighth, wide // line * HERE, kind=f32), shape(tall * HERE, width // line, kind=f32),
            shape(CHUNKS - HERE, eighth, wide), shape(CHUNKS - HERE, tall, width),
        ],
        scratch_shapes=scratch,
        compiler_params=params(collective_id=1, has_side_effects=True),
        name="back",
    )(set_kind, hidden, gup, act, gdown, output_part.reshape(2, 2, 2, eighth, width), e, go, mixed, q, kc, vc, wk, wv, x, c)


def attention_back_kernel(
    e_ref, go_ref, mixed_ref, q_ref, kc_ref, vc_ref, wk_ref, wv_ref,
    gq_ref, gk_ref, gv_ref, g_ref,
    gkt, gvt,
):
    width = q_ref.shape[2]
    comp = kc_ref.shape[1]
    half = lax.broadcasted_iota(jnp.int32, (comp, LANES), 1) < DH
    minus = head_blocks(jnp.full((comp, LANES), -1.0, bf16), half)
    refs = [ref.at[0] for ref in (e_ref, go_ref, mixed_ref, q_ref, kc_ref, vc_ref, gq_ref)]
    for pair in range(width // LANES):
        pair_back(pair, *refs, gkt, gvt, half, minus)
    g_ref[0] = (dot(wk_ref[...], gkt[...]) + dot(wv_ref[...], gvt[...])).astype(bf16)
    gk_ref[0] = gkt[...].T
    gv_ref[0] = gvt[...].T


def attention_back(e, go, mixed, q, kc, vc, wk, wv):
    sets, rows, width = q.shape
    comp = kc.shape[1]
    outs = [
        ((rows, width), bf16),
        ((comp, width), bf16),
        ((comp, width), bf16),
        ((width, comp), bf16),
    ]
    tokens = per_set((rows, width))
    short = per_set((comp, width))
    return pl.pallas_call(
        attention_back_kernel,
        grid=(sets,),
        in_specs=[per_set(e.shape[1:])] + [tokens] * 3 + [short] * 2
        + [whole(w.shape) for w in (wk, wv)],
        out_specs=[per_set(shape) for shape, _ in outs],
        out_shape=[jax.ShapeDtypeStruct((sets,) + shape, kind) for shape, kind in outs],
        scratch_shapes=[pltpu.VMEM((width, comp), bf16)] * 2,
        compiler_params=params(),
        name="attention_back",
    )(e, go, mixed, q, kc, vc, wk, wv)


def feed_grads_kernel(hidden_ref, gup_ref, act_ref, gdown_ref, up_out, down_out):
    up_out[...] = dot_tn(hidden_ref[...], gup_ref[...]).astype(bf16)
    down_out[...] = dot_tn(act_ref[...], gdown_ref[...]).astype(bf16)


def feed_grads(hidden, gup, act, gdown):
    tokens, width = hidden.shape
    units = gup.shape[1]
    chunk = 512
    return pl.pallas_call(
        feed_grads_kernel,
        grid=(units // chunk,),
        in_specs=[
            whole((tokens, width)),
            pl.BlockSpec((tokens, chunk), lambda i: (0, i)),
            pl.BlockSpec((tokens, chunk), lambda i: (0, i)),
            whole((tokens, width)),
        ],
        out_specs=[
            pl.BlockSpec((width, chunk), lambda i: (0, i)),
            pl.BlockSpec((chunk, width), lambda i: (i, 0)),
        ],
        out_shape=[jax.ShapeDtypeStruct((width, units), bf16), jax.ShapeDtypeStruct((units, width), bf16)],
        compiler_params=params(),
        name="feed_grads",
    )(hidden, gup, act, gdown)


def square_grad_kernel(left_ref, right_ref, out_ref):
    out_ref[...] = dot_tn(left_ref[...], right_ref[...]).astype(bf16)


def square_grad(left, right):
    count, width = left.shape
    return pl.pallas_call(
        square_grad_kernel,
        grid=(1,),
        in_specs=[whole((count, width)), whole((count, width))],
        out_specs=whole((width, width)),
        out_shape=jax.ShapeDtypeStruct((width, width), bf16),
        compiler_params=params(),
        name="square_grad",
    )(left, right)


def last_kernel(kind_ref, offset_ref, table_any, x_any, g_any, gfirst_any, gq_any, wq_any, out_any, compress_ref,
                table, x, g, gfirst, gq, wq, out, total, load_sems, weight_sem, out_sems):
    sets, rows, _ = x.shape
    longest = compress_ref.shape[0]
    pairs = ((g_any, g), (x_any, x), (gq_any, gq), (table_any, table), (gfirst_any, gfirst))
    loads = [[pltpu.make_async_copy(src.at[s], dst.at[s], load_sems.at[s, i]) for i, (src, dst) in enumerate(pairs)] for s in range(sets)]
    stores = [pltpu.make_async_copy(out.at[s], out_any.at[s], out_sems.at[s]) for s in range(sets)]
    weight = pltpu.make_async_copy(wq_any, wq, weight_sem.at[0])
    for load in loads[0]:
        load.start()
    weight.start()
    for s in range(1, sets):
        for load in loads[s]:
            load.start()
    total[...] = jnp.zeros_like(total)
    weight.wait()

    def work(s, carry):
        for i, (src, dst) in enumerate(pairs):
            pltpu.make_async_copy(src.at[s], dst.at[s], load_sems.at[s, i]).wait()
        out[s] = gfirst[s].astype(f32) + (dot_nt(table[s], g[s]) + dot_nt(gq[s], wq[...]))
        pltpu.make_async_copy(out.at[s], out_any.at[s], out_sems.at[s]).start()
        terms = dot(x[s], g[s])
        begin, shift = aligned(own_start(kind_ref, offset_ref, s, rows, longest // 4))
        padded = jnp.concatenate([terms, jnp.zeros((TILE, terms.shape[1]), f32)], axis=0)
        total[pl.ds(begin, rows + TILE), :] += pltpu.roll(padded, shift, 0)
        return carry

    lax.fori_loop(0, sets, work, 0)
    compress_ref[...] = total[:longest, :].astype(compress_ref.dtype)
    for store in stores:
        store.wait()


def last(kinds, offsets, table, x, g, gfirst, gq, wq, longest, kind):
    sets, rows, width = x.shape
    comp = table.shape[2]
    anywhere, smem = pl.BlockSpec(memory_space=pl.ANY), pl.BlockSpec(memory_space=pltpu.SMEM)
    dma = lambda *n: pltpu.SemaphoreType.DMA(n)
    return pl.pallas_call(
        last_kernel,
        in_specs=[smem] * 2 + [anywhere] * 6,
        out_specs=[anywhere, pl.BlockSpec(memory_space=pltpu.VMEM)],
        out_shape=[
            jax.ShapeDtypeStruct((sets, rows, width), f32),
            jax.ShapeDtypeStruct((longest, comp), kind),
        ],
        scratch_shapes=[pltpu.VMEM(v.shape, v.dtype) for v in (table, x, g, gfirst, gq, wq)]
        + [pltpu.VMEM(x.shape, f32), pltpu.VMEM((longest + TILE, comp), f32), dma(sets, 5), dma(1), dma(sets)],
        compiler_params=params(),
        name="last",
    )(kinds, offsets, table, x, g, gfirst, gq, wq)


def finish_kernel(layer_any, table, norms, up_first, up_more, down_first, down_more, *refs):
    (squares, output), (layer_out, table_out, up_out, down_out), outs, (held, sems) = refs[:2], refs[2:6], refs[6:-2], refs[-2:]
    sets = range(held.shape[0])
    loads = [pltpu.make_async_copy(layer_any.at[i], held.at[i], sems.at[0, i]) for i in sets]
    stores = [pltpu.make_async_copy(held.at[i], layer_out.at[i], sems.at[1, i]) for i in sets]
    for load in loads:
        load.start()
    for load, store in zip(loads, stores):
        load.wait()
        store.start()
    table_out[...] = table[...].astype(f32).reshape(table_out.shape)
    wide, tall = up_first.shape[1], down_first.shape[0]
    up_out[:, :wide] = up_first[...]
    down_out[:, :tall] = down_first[...].T
    for i in range(up_more.shape[0]):
        up_out[:, (i + 1) * wide : (i + 2) * wide] = up_more[i]
    for i in range(down_more.shape[0]):
        down_out[:, (i + 1) * tall : (i + 2) * tall] = down_more[i].T
    for i in range(4):
        outs[i][...] = squares[i] if i < 3 else output[...]
        outs[4 + i][...] = norms[i, :]
    for store in stores:
        store.wait()


def finish(layer_out, table, norms, up_first, up_more, down_first, down_more, squares, output):
    vmem, anywhere = pl.BlockSpec(memory_space=pltpu.VMEM), pl.BlockSpec(memory_space=pl.ANY)
    width = norms.shape[1]
    out = lambda *dims: jax.ShapeDtypeStruct(dims, f32)
    return pl.pallas_call(
        finish_kernel,
        in_specs=[anywhere] + [vmem] * 8,
        out_specs=[anywhere] + [vmem] * 11,
        out_shape=[
            jax.ShapeDtypeStruct(layer_out.shape, layer_out.dtype),
            out(table.size // table.shape[-1], table.shape[-1]),
            out(up_first.shape[0], up_first.shape[1] * (1 + up_more.shape[0])),
            out(down_first.shape[1], down_first.shape[0] * (1 + down_more.shape[0])),
        ]
        + [out(*output.shape)] * 4
        + [out(width)] * 4,
        scratch_shapes=[pltpu.VMEM(layer_out.shape, layer_out.dtype), pltpu.SemaphoreType.DMA((2, layer_out.shape[0]))],
        compiler_params=params(),
        name="finish",
    )(layer_out, table, norms, up_first, up_more, down_first, down_more, squares, output)


def sequence_sum(part, is_long, row_count, shortest):
    seq_count = lax.axis_size("seq")
    total = lax.psum(part, "seq")
    span = shortest // row_count
    if span > 1:
        groups = [list(range(i, i + span)) for i in range(0, seq_count, span)]
        part = lax.psum(part, "seq", axis_index_groups=groups)
    return jnp.where(is_long[:, None, None], total, part)


def table_start(set_kind, row_offset, block_index, row_count, shortest):
    position = block_index * row_count
    member = position // shortest
    chosen = jnp.sum(jnp.where(jnp.arange(4)[None, :] == member, row_offset, 0), axis=1)
    return jnp.where(set_kind > 0, position, chosen + position % shortest)


def local(
    inputs, cotangent, set_kind, row_offset, query_w, key_w, value_w, output_w, up_w, down_w, compress,
    first_gain, first_bias, second_gain, second_bias,
):
    sets, rows, width = inputs.shape
    longest, comp = compress.shape
    shortest = longest // 4
    ranked = lax.axis_index("seq")
    tokens = sets * rows
    is_long = set_kind > 0
    norms = (first_gain, first_bias, second_gain, second_bias)
    linked = lax.axis_size("batch") == 8 and lax.axis_size("seq") == 4 and rows == shortest
    weights = (query_w, key_w, value_w, output_w, up_w, down_w)
    if linked:
        summed, line = inputs, lax.axis_size("seq")
    else:
        starts = table_start(set_kind, row_offset, ranked, rows, shortest).astype(jnp.int32)
        table, part, _ = front(starts, compress, inputs, query_w)
        summed, line = sequence_sum(part, is_long, rows, shortest), 0
    (kc, vc, summed, mixed, hidden, layer_out, gdown, gatt, go, new_table, queries, e, act, gup, output_part, norm_sums) = layer(
        set_kind, row_offset, compress, summed, inputs, cotangent, weights, norms, line
    )
    flat = lambda v: v.reshape(-1, v.shape[-1])
    if linked:
        gq, g, squares, output_grad, up_first, down_first, up_rows, down_rows = back(
            set_kind, flat(hidden), flat(gup), flat(act), flat(gdown), output_part, e, go, mixed, queries, kc, vc, key_w, value_w,
            flat(inputs), flat(summed),
        )
        g = g.reshape(sets, width, comp)
        input_grad, compress_part = last(set_kind, row_offset, new_table, inputs, g, gatt, gq, query_w, longest, bf16)
        table_sum, norm_total, up_more, down_more, squares = closing(
            compress_part, norm_sums, up_rows, down_rows, squares
        )
        layer_out, compress_grad, up_grad, down_grad, *rest = finish(
            layer_out, table_sum, norm_total, up_first, up_more, down_first, down_more, squares, output_grad
        )
        weights, norm_grads = tuple(rest[:4]) + (up_grad, down_grad.T), rest[4:]
    else:
        up_part, down_part = feed_grads(flat(hidden), flat(gup), flat(act), flat(gdown))
        gq, gk, gv, g_part = attention_back(e, go, mixed, queries, kc, vc, key_w, value_w)
        g = sequence_sum(g_part, is_long, rows, shortest)
        query_part = square_grad(flat(inputs), flat(gq))
        key_part = square_grad(flat(summed), flat(gk))
        value_part = square_grad(flat(summed), flat(gv))
        input_grad, compress_part = last(set_kind, row_offset, table, inputs, g, gatt, gq, query_w, longest, f32)

        def scattered(v):
            v = lax.psum_scatter(v, "seq", scatter_dimension=1, tiled=True)
            return lax.psum_scatter(v, "batch", scatter_dimension=0, tiled=True).astype(f32)

        parts = (query_part, key_part, value_part, output_part, up_part, down_part)
        weights = tuple(scattered(v) for v in parts)
        compress_grad, norm_grads = lax.psum((compress_part, norm_sums), ("batch", "seq"))
    return (layer_out, input_grad) + weights + (compress_grad,) + tuple(norm_grads[i] for i in range(4))


def solution(mesh):
    tokens = P("batch", "seq", None)
    in_specs = (tokens, tokens, P("batch"), P("batch", None)) + (P(),) * 11
    out_specs = (tokens, tokens) + (P("batch", "seq"),) * 6 + (P(),) * 5
    return jax.shard_map(local, mesh=mesh, in_specs=in_specs, out_specs=out_specs, check_vma=False)
```

```python
import functools

import jax
import jax.numpy as jnp
from jax import lax
from jax.experimental import pallas as pl
from jax.experimental.pallas import tpu as pltpu
from jax.sharding import PartitionSpec as P

DH = 64
LANES = 128
TILE = 8
SCALE = DH ** (-0.5)
EPS = 1e-05
MESH = pl.DeviceIdType.MESH
VMEM_LIMIT = 63 * 1024 * 1024
bf16 = jnp.bfloat16
f32 = jnp.float32


def dot(left, right):
    return lax.dot_general(left, right, (((1,), (0,)), ((), ())), preferred_element_type=f32)


def dot_nt(left, right):
    return lax.dot_general(left, right, (((1,), (1,)), ((), ())), preferred_element_type=f32)


def dot_tn(left, right):
    return lax.dot_general(left, right, (((0,), (0,)), ((), ())), preferred_element_type=f32)


def params(**more):
    return pltpu.CompilerParams(vmem_limit_bytes=VMEM_LIMIT, **more)


def whole(shape):
    return pl.BlockSpec(shape, lambda *_: (0,) * len(shape), pipeline_mode=pl.Buffered(1))


def per_set(shape):
    return pl.BlockSpec((1,) + tuple(shape), lambda s, *_: (s,) + (0,) * len(shape))


def own_start(kinds, offsets, at, row_count, shortest):
    position = lax.axis_index("seq") * row_count
    return jnp.where(kinds[at] > 0, position, offsets[at, position // shortest] + position % shortest)


def aligned(start):
    begin = start // TILE * TILE
    return pl.multiple_of(begin, TILE), start - begin


def place():
    batch = lax.axis_index("batch")
    return batch // 4, batch // 2 % 2, batch % 2, lax.axis_index("seq")


def device(y, x, core, z):
    return ((y * 2 + x) * 2 + core, z)


def greet(others):
    barrier = pltpu.get_barrier_semaphore()
    for other in others:
        pl.semaphore_signal(barrier, inc=1, device_id=other, device_id_type=MESH)
    pl.semaphore_wait(barrier, len(others))


def remote(src, dst, send_sem, recv_sem, target):
    return pltpu.make_async_remote_copy(src, dst, send_sem, recv_sem, device_id=target, device_id_type=MESH)


class LineSum:
    def __init__(self, line, lag, own, from_left, from_right, sems):
        y, x, core, self.z = place()
        self.line, self.lag, self.own = line, lag, own
        self.right = device(y, x, core, (self.z + 1) % line)
        self.left = device(y, x, core, (self.z + line - 1) % line)
        inner, outer = self.z > 0, self.z < line - 1
        self.ways = (
            (from_left, self.right, inner, outer, sems[0], sems[1]),
            (from_right, self.left, outer, inner, sems[2], sems[3]),
        )

    def greet(self):
        barrier = pltpu.get_barrier_semaphore()
        for way in self.ways:

            @pl.when(way[3])
            def _():
                pl.semaphore_signal(barrier, inc=1, device_id=way[1], device_id_type=MESH)

        both = jnp.logical_and(self.z > 0, self.z < self.line - 1).astype(jnp.int32)
        pl.semaphore_wait(barrier, 1 + both)

    def prepare(self):
        for way in self.ways:

            @pl.when(jnp.logical_not(way[2]))
            def _():
                way[0][...] = jnp.zeros_like(way[0])

    def copy(self, way, at):
        held, target, _, _, send, recv = way
        return remote(held.at[at], held.at[at], send.at[at], recv.at[at], target)

    def forward(self, way, at):
        @pl.when(way[2])
        def _():
            self.copy(way, at).wait_recv()

        way[0][at] = way[0][at] + self.own[at]

        @pl.when(way[3])
        def _():
            self.copy(way, at).start()

    def slots(self):
        return self.own.shape[0] + self.lag * (self.line - 1)

    def serve(self, slot):
        for way, hops in zip(self.ways, (self.z, self.line - 1 - self.z)):
            at = slot - self.lag * hops

            @pl.when(jnp.logical_and(at >= 0, at < self.own.shape[0]))
            def _():
                self.forward(way, at)

    def serve_many(self, begin, count):
        def slot(at, carry):
            self.serve(at)
            return carry

        lax.fori_loop(begin, begin + count, slot, 0)

    def total(self, at, joined):
        own = self.own[at].astype(f32)
        both = self.ways[0][0][at].astype(f32) + self.ways[1][0][at].astype(f32)
        return jnp.where(joined, both - own, own).astype(bf16)

    def finish(self):
        for way in self.ways:

            @pl.when(way[3])
            def _():
                def wait(at, carry):
                    self.copy(way, at).wait_send()
                    return carry

                lax.fori_loop(0, self.own.shape[0], wait, 0)


class Scatter:
    def __init__(self, x_first, part, from_core, from_first, from_second, send, recv):
        y, x, core, z = place()
        self.part, self.recvs = part, (from_core, from_first, from_second)
        along_x, along_y = device(y, 1 - x, core, z), device(1 - y, x, core, z)
        self.core, self.x, self.y, self.x_first = core, x, y, x_first
        if x_first:
            sources = (part.at[:, :, 1 - core], from_core.at[:, 1 - x], from_first.at[1 - y])
            targets = (device(y, x, 1 - core, z), along_x, along_y)
        else:
            sources = (part.at[:, :, 1 - core], from_core.at[1 - y], from_first.at[1 - x])
            targets = (device(y, x, 1 - core, z), along_y, along_x)
        self.copies = [
            remote(sources[i], self.recvs[i], send.at[i], recv.at[i], targets[i]) for i in range(3)
        ]

    def start(self):
        self.copies[0].start()

    def first(self):
        self.copies[0].wait()
        self.recvs[0][...] = self.recvs[0][...] + self.part[:, :, self.core]
        self.copies[1].start()

    def second(self):
        self.copies[1].wait_recv()
        kept = self.recvs[0][:, self.x] if self.x_first else self.recvs[0][self.y]
        self.recvs[1][...] = self.recvs[1][...] + kept
        self.copies[2].start()

    def done(self):
        self.copies[2].wait_recv()
        kept = self.recvs[1][self.y] if self.x_first else self.recvs[1][self.x]
        return self.recvs[2][...].astype(f32) + kept.astype(f32)

    def finish(self):
        for copy in self.copies[1:]:
            copy.wait_send()


class LineScatter:
    def __init__(self, blocks, near, far, send, recv):
        y, x, core, z = place()
        self.blocks, self.near, self.far = blocks, near, far
        self.high, self.low = z // 2, z % 2
        self.copies = [
            remote(blocks.at[:, 1 - self.low], near, send.at[0], recv.at[0], device(y, x, core, z + 1 - 2 * self.low)),
            remote(near.at[1 - self.high], far, send.at[1], recv.at[1], device(y, x, core, (z + 2) % 4)),
        ]

    def start(self):
        self.copies[0].start()

    def middle(self):
        self.copies[0].wait_recv()
        self.near[...] = self.near[...] + self.blocks[:, self.low]
        self.copies[1].start()

    def done(self):
        self.copies[1].wait_recv()
        return self.near[self.high].astype(f32) + self.far[...].astype(f32)

    def finish(self):
        for copy in self.copies:
            copy.wait_send()


def line_scatter_blocks(blocks, rows, line):
    step = rows.shape[1] // line
    for z in range(line):
        mine = rows[:, z * step : (z + 1) * step]
        if step % LANES:
            top = rows.shape[0] // 2
            mine = jnp.concatenate([mine[:top], mine[top:]], axis=1)
        blocks[z // 2, z % 2] = mine.astype(bf16)


def unfold(total, out):
    if total.shape[1] == out.shape[1]:
        out[...] = total
    else:
        top, step = total.shape[0], out.shape[1]
        out[:top, :] = total[:, :step]
        out[top:, :] = total[:, step:]


def block_shape(rows, width, line):
    step = width // line
    return (rows, step) if step % LANES == 0 else (rows // 2, step * 2)


def grad_columns(part, left, right):
    step = 2 * LANES

    def columns(j, carry):
        span = pl.ds(pl.multiple_of(j * step, LANES), step)
        part[:, span] = dot_tn(left(), right(span)).astype(bf16)
        return carry

    lax.fori_loop(0, part.shape[-1] // step, columns, 0)


def scatter_scratch(rows, width, *count):
    shapes = [(2, 2, rows, width), (2, rows, width), (rows, width)]
    return [pltpu.VMEM(count + shape, bf16) for shape in shapes] + [pltpu.SemaphoreType.DMA(count + (3,))] * 2


def line_scratch(rows, width, line):
    block = block_shape(rows, width, line)
    return [pltpu.VMEM(n + block, bf16) for n in ((2, 2), (2,), ())] + [pltpu.SemaphoreType.DMA((2,))] * 2


class Neighbours:
    def __init__(self, line):
        y, x, core, z = place()
        self.core = device(y, x, 1 - core, z)
        places = [((y + dy) % 2, (x + dx) % 2) for dy, dx in ((0, 1), (1, 0), (1, 1))]
        self.plane = [(py * 2 + px, device(py, px, core, z)) for py, px in places]
        self.line = [((z + d) % line, device(y, x, core, (z + d) % line)) for d in range(1, line)]

    def everyone(self):
        return [self.core] + [to for _, to in self.plane] + [to for _, to in self.line]


class Total:
    counts = lambda line: (2, 6, 2 * (line - 1), line - 1, 3, 1)

    def __init__(self, line, near, table, norms, table_out, norms_out, mine, from_core, from_plane, from_line, gathered,
                 core_norms, plane_norms, line_norms, *sems):
        y, x, core, z = place()
        plane = y * 2 + x
        pairs = [(sems[2 * i], sems[2 * i + 1]) for i in range(6)]
        self.running = []

        def start(stage, moves):
            send, recv = pairs[stage]
            self.running = [remote(src, dst, send.at[i], recv.at[i], to) for i, (src, dst, to) in enumerate(moves)]
            for copy in self.running:
                copy.start()

        def to_core():
            mine[...] = table[...]
            core_norms[0] = norms[...]
            start(0, [(mine.at[1 - core], from_core, near.core), (core_norms.at[0], core_norms.at[1], near.core)])

        def to_plane():
            from_core[...] = from_core[...] + mine[core]
            plane_norms[plane] = core_norms[0] + core_norms[1]
            kept = plane_norms.at[plane]
            start(1, [(from_core.at[p], from_plane.at[i], to) for i, (p, to) in enumerate(near.plane)]
                  + [(kept, kept, to) for _, to in near.plane])

        def to_line():
            total = from_core[plane].astype(f32)
            for i in range(3):
                total = total + from_plane[i].astype(f32)
            mine[0, 0] = total.astype(bf16)
            line_norms[z] = plane_norms[0] + plane_norms[1] + plane_norms[2] + plane_norms[3]
            kept = line_norms.at[z]
            start(2, [(mine.at[0, 0, p], from_line.at[i], to) for i, (p, to) in enumerate(near.line)]
                  + [(kept, kept, to) for _, to in near.line])

        def back_line():
            total = mine[0, 0, z].astype(f32)
            for i in range(line - 1):
                total = total + from_line[i].astype(f32)
            gathered[core, plane, z] = total.astype(bf16)
            all_norms = line_norms[0]
            for i in range(1, line):
                all_norms = all_norms + line_norms[i]
            norms_out[...] = all_norms
            block = gathered.at[core, plane, z]
            start(3, [(block, block, to) for _, to in near.line])

        def back_plane():
            block = gathered.at[core, plane]
            start(4, [(block, block, to) for _, to in near.plane])

        def back_core():
            block = gathered.at[core]
            start(5, [(block, block, near.core)])

        def close():
            table_out[...] = gathered[...]

        self.stages = [to_core, to_plane, to_line, back_line, back_plane, back_core, close]

    def advance(self):
        for copy in self.running:
            copy.wait()
        self.running = []
        self.stages.pop(0)()

    @staticmethod
    def scratch(line, shape, norms):
        vmem = pltpu.VMEM
        return [
            vmem(shape, bf16), vmem(shape[1:], bf16), vmem((3,) + shape[2:], bf16), vmem((line - 1,) + shape[3:], bf16),
            vmem(shape, bf16), vmem((2,) + norms, f32), vmem((4,) + norms, f32), vmem((line,) + norms, f32),
        ] + [pltpu.SemaphoreType.DMA((n,)) for n in Total.counts(line) for _ in range(2)]


def closing_kernel(line, table_ref, norms_ref, up_ref, down_ref, square_any,
                   table_out, norms_out, up_out, down_out, square_out, square_part, load_sems, *scratch):
    scratch = list(scratch)
    take = lambda n: [scratch.pop(0) for _ in range(n)]
    pairs = [(square_any.at[i], square_part.at[i]) for i in range(3)]
    loads = [pltpu.make_async_copy(src, dst, load_sems.at[i]) for i, (src, dst) in enumerate(pairs)]
    for load in loads:
        load.start()
    near = Neighbours(line)
    greet(near.everyone())
    total = Total(line, near, table_ref, norms_ref, table_out, norms_out, *take(8 + 12))
    total.advance()
    query, key, value = [Scatter(i != 1, square_part.at[i], *take(5)) for i in range(3)]
    square_lines = [LineScatter(*take(5)) for _ in range(3)]
    for load, job in zip(loads, (query, key, value)):
        load.wait()
        job.start()
    across = []
    for rows, out in ((up_ref, up_out), (down_ref, down_out)):
        for chunk in range(rows.shape[0]):
            job = LineScatter(*take(5))
            line_scatter_blocks(job.blocks, rows[chunk], line)
            job.start()
            across.append((job, out.at[chunk]))
    total.advance()
    query.first()
    key.first()
    value.first()
    for job, _ in across:
        job.middle()
    total.advance()
    query.second()
    key.second()
    total.advance()
    for job, out in across:
        unfold(job.done(), out)
    value.second()
    total.advance()
    jobs = [(job, square_lines[i], square_out.at[i]) for i, job in enumerate((query, key, value))]
    for job, line_job, _ in jobs:
        line_scatter_blocks(line_job.blocks, job.done(), line)
        line_job.start()
    total.advance()
    for _, line_job, _ in jobs:
        line_job.middle()
    total.advance()
    for _, line_job, out in jobs:
        unfold(line_job.done(), out)
    for job, _ in across:
        job.finish()
    for job, line_job, _ in jobs:
        job.finish()
        line_job.finish()


def closing(table, norms, up_rows, down_rows, squares):
    line = lax.axis_size("seq")
    longest, comp = table.shape
    shape = (2, 4, line, longest // (8 * line), comp)
    vmem, anywhere = pl.BlockSpec(memory_space=pltpu.VMEM), pl.BlockSpec(memory_space=pl.ANY)
    out = lambda *dims: jax.ShapeDtypeStruct(dims, f32)
    (ups, rows, wide), (downs, tall, width), count = up_rows.shape, down_rows.shape, squares.shape[0]
    squares = squares.reshape(count, 2, 2, 2, rows, width)
    scratch = [pltpu.VMEM(squares.shape, bf16), pltpu.SemaphoreType.DMA((count,))]
    scratch += Total.scratch(line, shape, norms.shape)
    scratch += scatter_scratch(rows, width) * count + line_scratch(rows, width, line) * count
    scratch += line_scratch(rows, wide, line) * ups + line_scratch(tall, width, line) * downs
    return pl.pallas_call(
        functools.partial(closing_kernel, line),
        in_specs=[vmem] * 4 + [anywhere],
        out_specs=[vmem] * 5,
        out_shape=[
            jax.ShapeDtypeStruct(shape, bf16), out(*norms.shape), out(ups, rows, wide // line),
            out(downs, tall, width // line), out(count, rows, width // line),
        ],
        scratch_shapes=scratch,
        compiler_params=params(collective_id=3, has_side_effects=True),
        name="closing",
    )(table.reshape(shape), norms, up_rows, down_rows, squares)


def front_kernel(start_ref, compress_ref, x_ref, wq_ref, table_ref, c_ref, q_ref, wide):
    step = pl.program_id(0)

    longest = compress_ref.shape[0]

    @pl.when(step == 0)
    def _():
        wide[:longest, :] = compress_ref[...].astype(f32)
        wide[longest:, :] = jnp.zeros((TILE, wide.shape[1]), f32)

    rows = x_ref.shape[1]
    begin, shift = aligned(start_ref[step])
    window = wide[pl.ds(begin, rows + TILE), :]
    table = pltpu.roll(window, lax.rem(rows + TILE - shift, rows + TILE), 0)[:rows].astype(bf16)
    table_ref[0] = table
    x = x_ref[0]
    c_ref[0] = dot_tn(table, x).astype(bf16)
    q_ref[0] = (dot(x, wq_ref[...]) * SCALE).astype(bf16)


def front(starts, compress, x, wq):
    sets, rows, width = x.shape
    longest, comp = compress.shape
    grid_spec = pltpu.PrefetchScalarGridSpec(
        num_scalar_prefetch=1,
        grid=(sets,),
        in_specs=[whole(compress.shape), per_set((rows, width)), whole(wq.shape)],
        out_specs=[per_set((rows, comp)), per_set((comp, width)), per_set((rows, width))],
        scratch_shapes=[pltpu.VMEM((longest + TILE, comp), f32)],
    )
    return pl.pallas_call(
        front_kernel,
        grid_spec=grid_spec,
        out_shape=[
            jax.ShapeDtypeStruct((sets, rows, comp), bf16),
            jax.ShapeDtypeStruct((sets, comp, width), bf16),
            jax.ShapeDtypeStruct((sets, rows, width), bf16),
        ],
        compiler_params=params(),
        name="front",
    )(starts, compress, x, wq)


def head_blocks(pair, first_half):
    zero = jnp.zeros_like(pair)
    return jnp.concatenate([jnp.where(first_half, pair, zero), jnp.where(first_half, zero, pair)], axis=0)


def norm_forward(v):
    average = jnp.mean(v, axis=-1, keepdims=True)
    centered = v - average
    variance = jnp.mean(centered * centered, axis=-1, keepdims=True)
    inverse = lax.rsqrt(variance + EPS)
    return centered * inverse, inverse


def norm_backward(dz, z, inverse):
    return (dz - jnp.mean(dz, axis=-1, keepdims=True) - z * jnp.mean(dz * z, axis=-1, keepdims=True)) * inverse


PIECES = 4
LAG = 2
HALVES = 2


def layer_kernel(
    line, long_ref, offset_ref, compress_ref, c_ref, x_any, cot_ref, gain1_ref, bias1_ref, gain2_ref, bias2_ref, wq_any, wk_any, wv_any, wo_any, up_any, down_any,
    kc_ref, vc_ref, csum_ref, mixed_ref, hidden_ref, out_ref, gdown_ref, gatt_ref, go_ref, table_any, q_any,
    e_any, act_any, gup_any, output_grad_ref, sums_ref,
    xs, qs, wq, wk, wv, wo, up, down, e_buf, act, gup, z_first, rinv_ref, held, output_grad, weight_sems, x_sems, out_sems,
    *linked,
):
    step = pl.program_id(0)
    last = pl.num_programs(0) - 1
    sets, rows, width = xs.shape
    comp = kc_ref.shape[1]
    units = up.shape[1]
    chunk = 768
    loads = [
        pltpu.make_async_copy(src, dst, weight_sems.at[i])
        for i, (src, dst) in enumerate(
            ((wq_any, wq), (wk_any, wk), (wv_any, wv), (wo_any, wo), (up_any, up), (down_any, down))
        )
    ]
    x_loads = [pltpu.make_async_copy(x_any.at[s], xs.at[s], x_sems.at[s]) for s in range(sets)]
    q_store = pltpu.make_async_copy(qs, q_any, out_sems.at[3])
    e_store = pltpu.make_async_copy(e_buf, e_any.at[step], out_sems.at[0])
    act_store = pltpu.make_async_copy(act, act_any.at[step], out_sems.at[1])
    gup_store = pltpu.make_async_copy(gup, gup_any.at[step], out_sems.at[2])

    if line:
        tables, own, from_left, from_right, table_sems, *sems = linked
        sums = LineSum(line, LAG, own, from_left, from_right, sems)
        ahead = PIECES + LAG * (line - 1)
        t_stores = [pltpu.make_async_copy(tables.at[s], table_any.at[s], table_sems.at[s]) for s in range(sets)]

    def first_use(load):
        @pl.when(step == 0)
        def _():
            load.wait()

    @pl.when(step == 0)
    def _():
        for load in x_loads:
            load.start()
        sums_ref[...] = jnp.zeros_like(sums_ref)
        output_grad[...] = jnp.zeros_like(output_grad)
        if line:
            longest = compress_ref.shape[0]
            sums.greet()
            sums.prepare()
            grid = (rows, rows)
            ahead_by = lax.broadcasted_iota(jnp.int32, grid, 1) - lax.broadcasted_iota(jnp.int32, grid, 0)

        def summarize(s, carry):
            pltpu.make_async_copy(x_any.at[s], xs.at[s], x_sems.at[s]).wait()

            @pl.when(s == 0)
            def _():
                loads[0].start()

            if line:
                table = jnp.zeros((rows, comp), f32)
                start = own_start(long_ref, offset_ref, s, rows, longest // 4)
                for at in range(0, longest, rows):
                    chosen = jnp.where(ahead_by == start - at, 1.0, 0.0).astype(bf16)
                    table = table + dot(chosen, compress_ref[at : at + rows, :])
                table = table.astype(bf16)
                tables[s] = table
                pltpu.make_async_copy(tables.at[s], table_any.at[s], table_sems.at[s]).start()
                c = dot_tn(table, xs[s]).astype(bf16)
                own[pl.ds(s * PIECES, PIECES)] = c.reshape(PIECES, comp // PIECES, width)
                sums.serve(s)
            return carry

        lax.fori_loop(0, sets, summarize, 0)
        for load in loads[1:]:
            load.start()
        loads[0].wait()

        def query(s, carry):
            qs[s] = (dot(xs[s], wq[...]) * SCALE).astype(bf16)
            if line:
                sums.serve(sets + s)
            return carry

        lax.fori_loop(0, sets, query, 0)
        q_store.start()
        if line:
            sums.serve_many(2 * sets, ahead - 2 * sets)

    def serve(part):
        if line:
            count = PIECES // 2

            @pl.when(step < last)
            def _():
                sums.serve_many(ahead + step * PIECES + part * count, count)

    if line:
        joined = long_ref[step] > 0
        for piece in range(PIECES):
            size = comp // PIECES
            csum_ref[0, piece * size : (piece + 1) * size, :] = sums.total(step * PIECES + piece, joined)
    else:
        csum_ref[0] = c_ref[0]
    first_use(loads[1])
    first_use(loads[2])
    c = csum_ref[0]
    kc_ref[0] = dot(c, wk[...]).astype(bf16)
    vc_ref[0] = dot(c, wv[...]).astype(bf16)
    half = lax.broadcasted_iota(jnp.int32, (comp, LANES), 1) < DH
    ones = head_blocks(jnp.ones((comp, LANES), bf16), half)

    @pl.when(step > 0)
    def _():
        e_store.wait()

    def attend(pair):
        lanes = pl.ds(pl.multiple_of(pair * LANES, LANES), LANES)
        keys = head_blocks(kc_ref[0, :, lanes], half)
        values = jnp.concatenate([head_blocks(vc_ref[0, :, lanes], half), ones], axis=1)
        scores = dot_nt(qs[step, :, lanes], keys)
        parts = []
        for head in range(2):
            mine = scores[:, head * comp : (head + 1) * comp]
            top = jnp.max(mine, axis=-1, keepdims=True)
            parts.append(jnp.exp(mine - top).astype(bf16))
        e = jnp.concatenate(parts, axis=1)
        e_buf[:, pl.ds(pl.multiple_of(pair * 2 * comp, LANES), 2 * comp)] = e
        total = dot(e, values)
        rinv = 1.0 / total[:, LANES:]
        rinv_ref[:, lanes] = rinv
        mixed_ref[0, :, lanes] = (total[:, :LANES] * rinv).astype(bf16)

    pairs = width // LANES // 2

    def some_heads(half_at, carry):
        for i in range(pairs):
            attend(half_at * pairs + i)
        return carry

    lax.fori_loop(0, 2, some_heads, 0)
    e_store.start()
    first_use(loads[3])
    gain1, bias1, gain2, bias2 = (ref[...].reshape(1, width) for ref in (gain1_ref, bias1_ref, gain2_ref, bias2_ref))
    size = rows // HALVES
    halves = [pl.ds(h * size, size) for h in range(HALVES)]
    inverse1 = []
    for part in halves:
        z1, inv1 = norm_forward(xs[step, part, :].astype(f32) + dot(mixed_ref[0, part, :], wo[...]))
        inverse1.append(inv1)
        z_first[part, :] = z1
        hidden = z1 * gain1 + bias1
        hidden_ref[0, part, :] = hidden.astype(bf16)
        held[part, :] = hidden
    first_use(loads[4])
    first_use(loads[5])

    @pl.when(step > 0)
    def _():
        act_store.wait()
        gup_store.wait()

    for part in halves:
        hidden_low = hidden_ref[0, part, :]
        for at in range(0, units, chunk):
            span = pl.ds(at, chunk)
            upward = dot(hidden_low, up[:, span])
            cdf = 0.5 + 0.5 * lax.erf(upward * (0.5**0.5))
            density = jnp.exp(upward * upward * -0.5) * 0.3989422804014327
            act[part, span] = (upward * cdf).astype(bf16)
            gup[part, span] = (cdf + upward * density).astype(bf16)
    act_store.start()
    serve(0)
    sums2 = []
    for part in halves:
        z2, inv2 = norm_forward(held[part, :] + dot(act[part, :], down[...]))
        out_ref[0, part, :] = (z2 * gain2 + bias2).astype(bf16)
        dy = cot_ref[0, part, :].astype(f32)
        gsecond = norm_backward(dy * gain2, z2, inv2)
        sums2.append((jnp.sum(dy * z2, axis=0, keepdims=True), jnp.sum(dy, axis=0, keepdims=True)))
        gdown_ref[0, part, :] = gsecond.astype(bf16)
        held[part, :] = gsecond
    for part in halves:
        gdown = gdown_ref[0, part, :]
        for at in range(0, units, chunk):
            span = pl.ds(at, chunk)
            gact = dot_nt(gdown, down[span, :])
            gup[part, span] = (gact * gup[part, span].astype(f32)).astype(bf16)
    gup_store.start()
    sums1 = []
    for part, inv1 in zip(halves, inverse1):
        ghidden = held[part, :] + dot_nt(gup[part, :], up[...])
        z1 = z_first[part, :]
        sums1.append((jnp.sum(ghidden * z1, axis=0, keepdims=True), jnp.sum(ghidden, axis=0, keepdims=True)))
        gatt_ref[0, part, :] = norm_backward(ghidden * gain1, z1, inv1).astype(bf16)
    for part in halves:
        go_ref[0, part, :] = (dot_nt(gatt_ref[0, part, :], wo[...]) * rinv_ref[part, :]).astype(bf16)
    output_grad[...] += dot_tn(mixed_ref[0], gatt_ref[0])
    for i, pieces in enumerate((sums1, sums2)):
        for j in range(2):
            sums_ref[2 * i + j : 2 * i + j + 1, :] += sum(piece[j] for piece in pieces)
    serve(1)

    @pl.when(step == last)
    def _():
        output_grad_ref[...] = output_grad[...].astype(bf16)
        e_store.wait()
        act_store.wait()
        gup_store.wait()
        q_store.wait()
        if line:
            for store in t_stores:
                store.wait()
            sums.finish()


def layer(set_kind, row_offset, compress, c, x, cot, weights, norms, line):
    sets, rows, width = x.shape
    longest, comp = compress.shape
    wq, wk, wv, wo, up, down = weights
    units = up.shape[1]
    tokens = per_set((rows, width))
    short = per_set((comp, width))
    anywhere = pl.BlockSpec(memory_space=pl.ANY)
    smem = pl.BlockSpec(memory_space=pltpu.SMEM)
    shape = lambda *dims, kind=bf16: jax.ShapeDtypeStruct(dims, kind)
    dma = lambda n: pltpu.SemaphoreType.DMA((n,))
    linked = []
    if line:
        count = sets * PIECES
        linked = [pltpu.VMEM((sets, rows, comp), bf16)]
        linked += [pltpu.VMEM((count, comp // PIECES, width), bf16)] * 3 + [dma(sets)] + [dma(count)] * 4
    more = dict(collective_id=0, has_side_effects=True) if line else {}
    return pl.pallas_call(
        functools.partial(layer_kernel, line),
        grid=(sets,),
        in_specs=[smem, smem, whole(compress.shape), anywhere if line else short, anywhere, tokens]
        + [whole((width,))] * 4
        + [anywhere] * 6,
        out_specs=[short] * 3 + [tokens] * 6 + [anywhere] * 5 + [whole((width, width)), whole((8, width))],
        out_shape=[shape(sets, comp, width)] * 3
        + [shape(sets, rows, width)] * 6
        + [shape(sets, rows, comp), shape(sets, rows, width)]
        + [shape(sets, rows, width // DH * comp)]
        + [shape(sets, rows, units)] * 2
        + [shape(width, width), shape(8, width, kind=f32)],
        scratch_shapes=[pltpu.VMEM(x.shape, bf16)] * 2
        + [pltpu.VMEM(w.shape, bf16) for w in weights]
        + [pltpu.VMEM((rows, width // DH * comp), bf16)]
        + [pltpu.VMEM((rows, units), bf16)] * 2
        + [pltpu.VMEM((rows, width), f32)] * 3
        + [pltpu.VMEM((width, width), f32), dma(6), dma(sets), dma(4)]
        + linked,
        compiler_params=params(**more),
        name="layer",
    )(set_kind, row_offset, compress, c, x, cot, *norms, *weights)


def pair_back(pair, e_ref, go_ref, mixed_ref, q_ref, kc_ref, vc_ref, gq_ref, gkt, gvt, half, minus):
    comp = kc_ref.shape[0]
    at = pair * LANES if isinstance(pair, int) else pl.multiple_of(pair * LANES, LANES)
    lanes = pl.ds(at, LANES)
    wide = pair * 2 * comp if isinstance(pair, int) else pl.multiple_of(pair * 2 * comp, LANES)
    e = e_ref[:, pl.ds(wide, 2 * comp)]
    keys = head_blocks(kc_ref[:, lanes], half)
    values = jnp.concatenate([head_blocks(vc_ref[:, lanes], half), minus], axis=1)
    go = go_ref[:, lanes]
    delta = (go.astype(f32) * mixed_ref[:, lanes].astype(f32)).astype(bf16)
    gp = dot_nt(jnp.concatenate([go, delta], axis=1), values)
    gs = (gp * e.astype(f32)).astype(bf16)
    gq_ref[:, lanes] = (dot(gs, keys) * SCALE).astype(bf16)
    for into, left, right in ((gkt, q_ref[:, lanes], gs), (gvt, go, e)):
        both = dot_tn(left, right)
        into[pl.ds(at, DH), :] = both[:DH, :comp].astype(bf16)
        into[pl.ds(at + DH, DH), :] = both[DH:, comp:].astype(bf16)


CHUNKS = 3
HERE = 1
BACK_PIECES = 4
BACK_LAG = 2


def back_kernel(
    line, long_ref, hidden_any, gup_any, act_any, gdown_any, output_any, e_any, go_any, mixed_any, q_any, kc_any, vc_any, wk_any, wv_any, x_any, c_any,
    gq_any, g_any, squares, output_out, up_out, down_out, up_rows, down_rows,
    hidden, gdown, feed, wk, wv, e, go, mixed, q, kc, vc, gq, gkt, gvt, gk, gv, own, from_left, from_right,
    up_part, down_part, output_part, load_sems, feed_sems, set_sems, out_sems, g_sem, late_sems, *scratch,
):
    scratch = list(scratch)
    take = lambda n: [scratch.pop(0) for _ in range(n)]
    sets, rows, width = q_any.shape
    comp = kc_any.shape[1]
    units = gup_any.shape[1]
    sums = LineSum(line, BACK_LAG, own, from_left, from_right, take(4))

    def copies(pairs, sems):
        return [pltpu.make_async_copy(src, dst, sems.at[i]) for i, (src, dst) in enumerate(pairs)]

    def feed_loads(chunk, which):
        if which == 0:
            wide, count, source = units // line, line, gup_any
        else:
            wide, count, source = units // 8, 8, act_any
        step = wide // CHUNKS
        return copies(
            [
                (source.at[:, pl.ds(pl.multiple_of(i * wide + chunk * step, LANES), step)], feed.at[which, :, pl.ds(i * step, step)])
                for i in range(count)
            ],
            feed_sems.at[which],
        )

    def set_loads(s):
        at = s % 2
        return copies(
            [(e_any.at[s], e.at[at]), (go_any.at[s], go.at[at]), (mixed_any.at[s], mixed.at[at]), (q_any.at[s], q.at[at]),
             (kc_any.at[s], kc.at[at]), (vc_any.at[s], vc.at[at])],
            set_sems.at[at],
        )

    def gq_store(s):
        return pltpu.make_async_copy(gq.at[s], gq_any.at[s], out_sems.at[s])

    def begin(some):
        for copy in some:
            copy.start()

    def end(some):
        for copy in some:
            copy.wait()

    weights = copies(((output_any, output_part), (hidden_any, hidden), (gdown_any, gdown), (wk_any, wk), (wv_any, wv)), load_sems)
    begin(weights[:1])
    begin(set_loads(0))
    begin(weights[3:])
    near = Neighbours(line)
    greet(near.everyone())
    sums.prepare()

    jobs = {"o": (Scatter(True, output_part, *take(5)), LineScatter(*take(5)), output_out)}
    lines = [LineScatter(*take(5)), LineScatter(*take(5))]
    kept = (take(5), take(5))

    def scatter_job(which, chunk):
        buffers = [ref.at[chunk] for ref in kept[which]]
        return Scatter(which == 0, (up_part, down_part)[which], *buffers)

    for chunk in range(CHUNKS):
        for which in range(2):
            if chunk < HERE:
                jobs[which, chunk] = (scatter_job(which, chunk), lines[which], (up_out, down_out)[which])
            else:
                jobs[which, chunk] = (scatter_job(which, chunk), None, (up_rows, down_rows)[which].at[chunk - HERE])

    def across(name):
        job, line_job, _ = jobs[name]
        line_scatter_blocks(line_job.blocks, job.done(), line)
        line_job.start()

    def feed_grad(which):
        if which == 0:
            up_part[...] = dot_tn(hidden[...], feed[0]).astype(bf16).reshape(up_part.shape)
        else:
            down_part[...] = dot_tn(feed[1], gdown[...]).astype(bf16).reshape(down_part.shape)

    half = lax.broadcasted_iota(jnp.int32, (comp, LANES), 1) < DH
    minus = head_blocks(jnp.full((comp, LANES), -1.0, bf16), half)

    def heads(s, pairs):
        at = s % 2
        for pair in pairs:
            pair_back(pair, e.at[at], go.at[at], mixed.at[at], q.at[at], kc.at[at], vc.at[at], gq.at[s], gkt, gvt, half, minus)

    def joins(s):
        g = dot(wk[...], gkt[...]) + dot(wv[...], gvt[...])
        own[pl.ds(s * BACK_PIECES, BACK_PIECES)] = g.astype(bf16).reshape(BACK_PIECES, width // BACK_PIECES, comp)
        gk[s] = gkt[...].T
        gv[s] = gvt[...].T
        gq_store(s).start()

    o, (u0, u1, u2), (d0, d1) = jobs["o"][0], [jobs[0, i][0] for i in range(3)], [jobs[1, i][0] for i in range(2)]
    weights[0].wait()
    o.start()

    def steps(s, by_set):
        for at, due in by_set.items():

            @pl.when(s == at)
            def _():
                for one in due:
                    one()

    def work(s, carry):
        end(set_loads(s))
        steps(s, {
            0: [lambda: begin(weights[1:2]), lambda: begin(feed_loads(0, 0))],
            1: [lambda: begin(feed_loads(1, 0)), lambda: begin(weights[2:3]), lambda: begin(feed_loads(0, 1))],
            2: [lambda: begin(feed_loads(1, 1)), lambda: begin(set_loads(3))],
            3: [lambda: begin(feed_loads(2, 0)), lambda: begin(feed_loads(2, 1))],
        })
        pairs = width // LANES // 2

        def some_heads(half_at, carry):
            heads(s, [half_at * pairs + i for i in range(pairs)])

            @pl.when(half_at == 0)
            def _():
                steps(s, {0: [o.first], 1: [u0.first], 2: [d0.first], 3: [d1.first]})

            return carry

        lax.fori_loop(0, 2, some_heads, 0)
        steps(s, {0: [lambda: end(weights[3:])], 1: [o.second], 2: [u0.second], 3: [u1.second, d0.second]})
        joins(s)
        sums.serve_many(s * BACK_PIECES, 2)

        @pl.when(s != 2)
        def _():
            chunk = s - s // 3
            end(feed_loads(chunk, 0))
            steps(s, {0: [lambda: end(weights[1:2]), lambda: begin(set_loads(1))], 1: [lambda: begin(set_loads(2))]})
            feed_grad(0)
            scatter_job(0, chunk).start()
            sums.serve_many(s * BACK_PIECES + 2, 2)

        @pl.when(s > 0)
        def _():
            end(feed_loads(s - 1, 1))
            steps(s, {1: [lambda: end(weights[2:3])]})
            feed_grad(1)

            @pl.when(s < sets - 1)
            def _():
                scatter_job(1, s - 1).start()

        steps(s, {1: [u1.first], 2: [lambda: sums.serve_many(2 * BACK_PIECES + 2, 2)], 3: [begin_late, u2.first]})
        return carry

    late = copies(((x_any, hidden), (c_any, gdown.at[: c_any.shape[0]])), late_sems)

    def begin_late():
        begin(late)

    lax.fori_loop(0, sets, work, 0)
    d2 = jobs[1, 2][0]
    d2.start()
    places = (feed.at[0, :width, :width], feed.at[0, width : 2 * width, :width], feed.at[1, :width, :width])
    flat = lambda ref, span: ref[:, :, span].reshape(-1, span.size)
    sources = ((hidden, gq), (gdown.at[: c_any.shape[0]], gk), (gdown.at[: c_any.shape[0]], gv))
    square_stores = [pltpu.make_async_copy(places[i], squares.at[i], late_sems.at[2 + i]) for i in range(3)]

    def square_grad_part(i):
        left, right = sources[i]
        grad_columns(places[i], lambda: left[...], lambda span: flat(right, span))
        square_stores[i].start()

    served = sets * BACK_PIECES
    sums.serve_many(served, 2)
    late[0].wait()
    square_grad_part(0)
    d2.first()
    d1.second()
    sums.serve_many(served + 2, 1)
    late[1].wait()
    square_grad_part(1)
    sums.serve_many(served + 3, 1)
    square_grad_part(2)
    sums.serve_many(served + 4, 1)
    u2.second()
    sums.serve_many(served + 5, sums.slots() - served - 5)
    d2.second()
    for name in ("o", (0, 0), (1, 0)):
        across(name)
    for s in range(sets):
        for piece in range(s * BACK_PIECES, (s + 1) * BACK_PIECES):
            own[piece] = sums.total(piece, long_ref[s] > 0)
    g_store = pltpu.make_async_copy(own, g_any, g_sem.at[0])
    g_store.start()
    for name in ("o", (0, 0), (1, 0)):
        jobs[name][1].middle()
    for name in jobs:
        job, line_job, out = jobs[name]
        if line_job is not None:
            unfold(line_job.done(), out)
        else:
            out[...] = job.done().astype(bf16)
    for name in jobs:
        job, line_job, _ = jobs[name]
        job.finish()
        if line_job is not None:
            line_job.finish()
    for store in square_stores:
        store.wait()
    for s in range(sets):
        gq_store(s).wait()
    g_store.wait()
    sums.finish()


def back(set_kind, hidden, gup, act, gdown, output_part, e, go, mixed, q, kc, vc, wk, wv, x, c):
    line = lax.axis_size("seq")
    sets, rows, width = q.shape
    comp = kc.shape[1]
    tokens, units = gup.shape
    eighth = width // 8
    wide, tall = units // CHUNKS, units // 8 // CHUNKS
    count = sets * BACK_PIECES
    dma = lambda *n: pltpu.SemaphoreType.DMA(n)
    vmem, anywhere = pl.BlockSpec(memory_space=pltpu.VMEM), pl.BlockSpec(memory_space=pl.ANY)
    shape = lambda *dims, kind=bf16: jax.ShapeDtypeStruct(dims, kind)
    buffer = lambda *dims, kind=bf16: pltpu.VMEM(dims, kind)
    scratch = [buffer(tokens, width)] * 2 + [buffer(2, tokens, wide)] + [buffer(width, width)] * 2
    scratch += [buffer(2, rows, e.shape[2])] + [buffer(2, rows, width)] * 3 + [buffer(2, comp, width)] * 2
    scratch += [buffer(sets, rows, width)] + [buffer(width, comp)] * 2 + [buffer(sets, comp, width)] * 2
    scratch += [buffer(count, width // BACK_PIECES, comp)] * 3
    scratch += [buffer(2, 2, 2, eighth, wide), buffer(2, 2, 2, tall, width), buffer(2, 2, 2, eighth, width)]
    scratch += [dma(5), dma(2, 8), dma(2, 6), dma(sets), dma(1), dma(5)] + [dma(count)] * 4
    scratch += scatter_scratch(eighth, width)
    for size in ((eighth, width), (eighth, wide), (tall, width)):
        scratch += line_scratch(*size, line)
    scratch += scatter_scratch(eighth, wide, CHUNKS) + scatter_scratch(tall, width, CHUNKS)
    return pl.pallas_call(
        functools.partial(back_kernel, line),
        in_specs=[pl.BlockSpec(memory_space=pltpu.SMEM)] + [anywhere] * 15,
        out_specs=[anywhere] * 3 + [vmem] * 5,
        out_shape=[
            shape(sets, rows, width),
            shape(count, width // BACK_PIECES, comp),
            shape(3, width, width),
            shape(eighth, width // line, kind=f32),
            shape(eighth, wide // line * HERE, kind=f32), shape(tall * HERE, width // line, kind=f32),
            shape(CHUNKS - HERE, eighth, wide), shape(CHUNKS - HERE, tall, width),
        ],
        scratch_shapes=scratch,
        compiler_params=params(collective_id=1, has_side_effects=True),
        name="back",
    )(set_kind, hidden, gup, act, gdown, output_part.reshape(2, 2, 2, eighth, width), e, go, mixed, q, kc, vc, wk, wv, x, c)


def attention_back_kernel(
    e_ref, go_ref, mixed_ref, q_ref, kc_ref, vc_ref, wk_ref, wv_ref,
    gq_ref, gk_ref, gv_ref, g_ref,
    gkt, gvt,
):
    width = q_ref.shape[2]
    comp = kc_ref.shape[1]
    half = lax.broadcasted_iota(jnp.int32, (comp, LANES), 1) < DH
    minus = head_blocks(jnp.full((comp, LANES), -1.0, bf16), half)
    refs = [ref.at[0] for ref in (e_ref, go_ref, mixed_ref, q_ref, kc_ref, vc_ref, gq_ref)]
    for pair in range(width // LANES):
        pair_back(pair, *refs, gkt, gvt, half, minus)
    g_ref[0] = (dot(wk_ref[...], gkt[...]) + dot(wv_ref[...], gvt[...])).astype(bf16)
    gk_ref[0] = gkt[...].T
    gv_ref[0] = gvt[...].T


def attention_back(e, go, mixed, q, kc, vc, wk, wv):
    sets, rows, width = q.shape
    comp = kc.shape[1]
    outs = [
        ((rows, width), bf16),
        ((comp, width), bf16),
        ((comp, width), bf16),
        ((width, comp), bf16),
    ]
    tokens = per_set((rows, width))
    short = per_set((comp, width))
    return pl.pallas_call(
        attention_back_kernel,
        grid=(sets,),
        in_specs=[per_set(e.shape[1:])] + [tokens] * 3 + [short] * 2
        + [whole(w.shape) for w in (wk, wv)],
        out_specs=[per_set(shape) for shape, _ in outs],
        out_shape=[jax.ShapeDtypeStruct((sets,) + shape, kind) for shape, kind in outs],
        scratch_shapes=[pltpu.VMEM((width, comp), bf16)] * 2,
        compiler_params=params(),
        name="attention_back",
    )(e, go, mixed, q, kc, vc, wk, wv)


def feed_grads_kernel(hidden_ref, gup_ref, act_ref, gdown_ref, up_out, down_out):
    up_out[...] = dot_tn(hidden_ref[...], gup_ref[...]).astype(bf16)
    down_out[...] = dot_tn(act_ref[...], gdown_ref[...]).astype(bf16)


def feed_grads(hidden, gup, act, gdown):
    tokens, width = hidden.shape
    units = gup.shape[1]
    chunk = 512
    return pl.pallas_call(
        feed_grads_kernel,
        grid=(units // chunk,),
        in_specs=[
            whole((tokens, width)),
            pl.BlockSpec((tokens, chunk), lambda i: (0, i)),
            pl.BlockSpec((tokens, chunk), lambda i: (0, i)),
            whole((tokens, width)),
        ],
        out_specs=[
            pl.BlockSpec((width, chunk), lambda i: (0, i)),
            pl.BlockSpec((chunk, width), lambda i: (i, 0)),
        ],
        out_shape=[jax.ShapeDtypeStruct((width, units), bf16), jax.ShapeDtypeStruct((units, width), bf16)],
        compiler_params=params(),
        name="feed_grads",
    )(hidden, gup, act, gdown)


def square_grad_kernel(left_ref, right_ref, out_ref):
    out_ref[...] = dot_tn(left_ref[...], right_ref[...]).astype(bf16)


def square_grad(left, right):
    count, width = left.shape
    return pl.pallas_call(
        square_grad_kernel,
        grid=(1,),
        in_specs=[whole((count, width)), whole((count, width))],
        out_specs=whole((width, width)),
        out_shape=jax.ShapeDtypeStruct((width, width), bf16),
        compiler_params=params(),
        name="square_grad",
    )(left, right)


def last_kernel(kind_ref, offset_ref, table_any, x_any, g_any, gfirst_any, gq_any, wq_any, out_any, compress_ref,
                table, x, g, gfirst, gq, wq, out, total, load_sems, weight_sem, out_sems):
    sets, rows, _ = x.shape
    longest = compress_ref.shape[0]
    pairs = ((g_any, g), (x_any, x), (gq_any, gq), (table_any, table), (gfirst_any, gfirst))
    loads = [[pltpu.make_async_copy(src.at[s], dst.at[s], load_sems.at[s, i]) for i, (src, dst) in enumerate(pairs)] for s in range(sets)]
    stores = [pltpu.make_async_copy(out.at[s], out_any.at[s], out_sems.at[s]) for s in range(sets)]
    weight = pltpu.make_async_copy(wq_any, wq, weight_sem.at[0])
    for load in loads[0]:
        load.start()
    weight.start()
    for s in range(1, sets):
        for load in loads[s]:
            load.start()
    total[...] = jnp.zeros_like(total)
    weight.wait()

    def work(s, carry):
        for i, (src, dst) in enumerate(pairs):
            pltpu.make_async_copy(src.at[s], dst.at[s], load_sems.at[s, i]).wait()
        out[s] = gfirst[s].astype(f32) + (dot_nt(table[s], g[s]) + dot_nt(gq[s], wq[...]))
        pltpu.make_async_copy(out.at[s], out_any.at[s], out_sems.at[s]).start()
        terms = dot(x[s], g[s])
        begin, shift = aligned(own_start(kind_ref, offset_ref, s, rows, longest // 4))
        padded = jnp.concatenate([terms, jnp.zeros((TILE, terms.shape[1]), f32)], axis=0)
        total[pl.ds(begin, rows + TILE), :] += pltpu.roll(padded, shift, 0)
        return carry

    lax.fori_loop(0, sets, work, 0)
    compress_ref[...] = total[:longest, :].astype(compress_ref.dtype)
    for store in stores:
        store.wait()


def last(kinds, offsets, table, x, g, gfirst, gq, wq, longest, kind):
    sets, rows, width = x.shape
    comp = table.shape[2]
    anywhere, smem = pl.BlockSpec(memory_space=pl.ANY), pl.BlockSpec(memory_space=pltpu.SMEM)
    dma = lambda *n: pltpu.SemaphoreType.DMA(n)
    return pl.pallas_call(
        last_kernel,
        in_specs=[smem] * 2 + [anywhere] * 6,
        out_specs=[anywhere, pl.BlockSpec(memory_space=pltpu.VMEM)],
        out_shape=[
            jax.ShapeDtypeStruct((sets, rows, width), f32),
            jax.ShapeDtypeStruct((longest, comp), kind),
        ],
        scratch_shapes=[pltpu.VMEM(v.shape, v.dtype) for v in (table, x, g, gfirst, gq, wq)]
        + [pltpu.VMEM(x.shape, f32), pltpu.VMEM((longest + TILE, comp), f32), dma(sets, 5), dma(1), dma(sets)],
        compiler_params=params(),
        name="last",
    )(kinds, offsets, table, x, g, gfirst, gq, wq)


def finish_kernel(layer_any, table, norms, up_first, up_more, down_first, down_more, *refs):
    (squares, output), (layer_out, table_out, up_out, down_out), outs, (held, sems) = refs[:2], refs[2:6], refs[6:-2], refs[-2:]
    sets = range(held.shape[0])
    loads = [pltpu.make_async_copy(layer_any.at[i], held.at[i], sems.at[0, i]) for i in sets]
    stores = [pltpu.make_async_copy(held.at[i], layer_out.at[i], sems.at[1, i]) for i in sets]
    for load in loads:
        load.start()
    for load, store in zip(loads, stores):
        load.wait()
        store.start()
    table_out[...] = table[...].astype(f32).reshape(table_out.shape)
    wide, tall = up_first.shape[1], down_first.shape[0]
    up_out[:, :wide] = up_first[...]
    down_out[:, :tall] = down_first[...].T
    for i in range(up_more.shape[0]):
        up_out[:, (i + 1) * wide : (i + 2) * wide] = up_more[i]
    for i in range(down_more.shape[0]):
        down_out[:, (i + 1) * tall : (i + 2) * tall] = down_more[i].T
    for i in range(4):
        outs[i][...] = squares[i] if i < 3 else output[...]
        outs[4 + i][...] = norms[i, :]
    for store in stores:
        store.wait()


def finish(layer_out, table, norms, up_first, up_more, down_first, down_more, squares, output):
    vmem, anywhere = pl.BlockSpec(memory_space=pltpu.VMEM), pl.BlockSpec(memory_space=pl.ANY)
    width = norms.shape[1]
    out = lambda *dims: jax.ShapeDtypeStruct(dims, f32)
    return pl.pallas_call(
        finish_kernel,
        in_specs=[anywhere] + [vmem] * 8,
        out_specs=[anywhere] + [vmem] * 11,
        out_shape=[
            jax.ShapeDtypeStruct(layer_out.shape, layer_out.dtype),
            out(table.size // table.shape[-1], table.shape[-1]),
            out(up_first.shape[0], up_first.shape[1] * (1 + up_more.shape[0])),
            out(down_first.shape[1], down_first.shape[0] * (1 + down_more.shape[0])),
        ]
        + [out(*output.shape)] * 4
        + [out(width)] * 4,
        scratch_shapes=[pltpu.VMEM(layer_out.shape, layer_out.dtype), pltpu.SemaphoreType.DMA((2, layer_out.shape[0]))],
        compiler_params=params(),
        name="finish",
    )(layer_out, table, norms, up_first, up_more, down_first, down_more, squares, output)


def sequence_sum(part, is_long, row_count, shortest):
    seq_count = lax.axis_size("seq")
    total = lax.psum(part, "seq")
    span = shortest // row_count
    if span > 1:
        groups = [list(range(i, i + span)) for i in range(0, seq_count, span)]
        part = lax.psum(part, "seq", axis_index_groups=groups)
    return jnp.where(is_long[:, None, None], total, part)


def table_start(set_kind, row_offset, block_index, row_count, shortest):
    position = block_index * row_count
    member = position // shortest
    chosen = jnp.sum(jnp.where(jnp.arange(4)[None, :] == member, row_offset, 0), axis=1)
    return jnp.where(set_kind > 0, position, chosen + position % shortest)


def local(
    inputs, cotangent, set_kind, row_offset, query_w, key_w, value_w, output_w, up_w, down_w, compress,
    first_gain, first_bias, second_gain, second_bias,
):
    sets, rows, width = inputs.shape
    longest, comp = compress.shape
    shortest = longest // 4
    ranked = lax.axis_index("seq")
    tokens = sets * rows
    is_long = set_kind > 0
    norms = (first_gain, first_bias, second_gain, second_bias)
    linked = lax.axis_size("batch") == 8 and lax.axis_size("seq") == 4 and rows == shortest
    weights = (query_w, key_w, value_w, output_w, up_w, down_w)
    if linked:
        summed, line = inputs, lax.axis_size("seq")
    else:
        starts = table_start(set_kind, row_offset, ranked, rows, shortest).astype(jnp.int32)
        table, part, _ = front(starts, compress, inputs, query_w)
        summed, line = sequence_sum(part, is_long, rows, shortest), 0
    (kc, vc, summed, mixed, hidden, layer_out, gdown, gatt, go, new_table, queries, e, act, gup, output_part, norm_sums) = layer(
        set_kind, row_offset, compress, summed, inputs, cotangent, weights, norms, line
    )
    flat = lambda v: v.reshape(-1, v.shape[-1])
    if linked:
        gq, g, squares, output_grad, up_first, down_first, up_rows, down_rows = back(
            set_kind, flat(hidden), flat(gup), flat(act), flat(gdown), output_part, e, go, mixed, queries, kc, vc, key_w, value_w,
            flat(inputs), flat(summed),
        )
        g = g.reshape(sets, width, comp)
        input_grad, compress_part = last(set_kind, row_offset, new_table, inputs, g, gatt, gq, query_w, longest, bf16)
        table_sum, norm_total, up_more, down_more, squares = closing(
            compress_part, norm_sums, up_rows, down_rows, squares
        )
        layer_out, compress_grad, up_grad, down_grad, *rest = finish(
            layer_out, table_sum, norm_total, up_first, up_more, down_first, down_more, squares, output_grad
        )
        weights, norm_grads = tuple(rest[:4]) + (up_grad, down_grad.T), rest[4:]
    else:
        up_part, down_part = feed_grads(flat(hidden), flat(gup), flat(act), flat(gdown))
        gq, gk, gv, g_part = attention_back(e, go, mixed, queries, kc, vc, key_w, value_w)
        g = sequence_sum(g_part, is_long, rows, shortest)
        query_part = square_grad(flat(inputs), flat(gq))
        key_part = square_grad(flat(summed), flat(gk))
        value_part = square_grad(flat(summed), flat(gv))
        input_grad, compress_part = last(set_kind, row_offset, table, inputs, g, gatt, gq, query_w, longest, f32)

        def scattered(v):
            v = lax.psum_scatter(v, "seq", scatter_dimension=1, tiled=True)
            return lax.psum_scatter(v, "batch", scatter_dimension=0, tiled=True).astype(f32)

        parts = (query_part, key_part, value_part, output_part, up_part, down_part)
        weights = tuple(scattered(v) for v in parts)
        compress_grad, norm_grads = lax.psum((compress_part, norm_sums), ("batch", "seq"))
    return (layer_out, input_grad) + weights + (compress_grad,) + tuple(norm_grads[i] for i in range(4))


def solution(mesh):
    tokens = P("batch", "seq", None)
    in_specs = (tokens, tokens, P("batch"), P("batch", None)) + (P(),) * 11
    out_specs = (tokens, tokens) + (P("batch", "seq"),) * 6 + (P(),) * 5
    return jax.shard_map(local, mesh=mesh, in_specs=in_specs, out_specs=out_specs, check_vma=False)
```
